32 devices in a mesh: dp: 4 (over y, core), fsdp: 8 (over z, x).
Axes of the slice: x: 2, y: 2, z: 4, core: 2. Of those that a mesh axis runs over, the one named last changes fastest.
Arguments:
- tokens: bfloat16 [32, 1024, 768], P(('dp', 'fsdp')), may hold values from -36 to 36
- cotangent: bfloat16 [32, 1024, 768], P(('dp', 'fsdp')), may hold values from -6 to 6
- document_ids: int32 [32, 1024], P(('dp', 'fsdp')), may hold values from 0 to 3, never falling along the last dimension, each value on 1 to 512 neighbouring positions
- source_layer: int32 [], replicated, may hold values from 0 to 11
- attngain: bfloat16 [12, 768], P(None, ('dp', 'fsdp')), may hold values from 0.5 to 1.5
- attnshift: bfloat16 [12, 768], P(None, ('dp', 'fsdp')), may hold values from -3 to 3
- qkvmatrix: bfloat16 [12, 768, 2304], P(None, ('dp', 'fsdp')), may hold values from -0.21875 to 0.21875
- qvoffset: bfloat16 [12, 1536], P(None, ('dp', 'fsdp')), may hold values from -3 to 3
- outmatrix: bfloat16 [12, 768, 768], P(None, ('dp', 'fsdp')), may hold values from -0.875 to 0.875
- outoffset: bfloat16 [12, 768], P(None, ('dp', 'fsdp')), may hold values from -3 to 3
- mlpgain: bfloat16 [12, 768], P(None, ('dp', 'fsdp')), may hold values from 0.5 to 1.5
- mlpshift: bfloat16 [12, 768], P(None, ('dp', 'fsdp')), may hold values from -3 to 3
- upmatrix: bfloat16 [12, 768, 3072], P(None, ('dp', 'fsdp')), may hold values from -0.21875 to 0.21875
- upoffset: bfloat16 [12, 3072], P(None, ('dp', 'fsdp')), may hold values from -3 to 3
- downmatrix: bfloat16 [12, 3072, 768], P(None, ('dp', 'fsdp')), may hold values from -0.109375 to 0.109375
- downoffset: bfloat16 [12, 768], P(None, ('dp', 'fsdp')), may hold values from -3 to 3
Outputs:
- layer_output: float32 [32, 1024, 768], P(('dp', 'fsdp'))
- input_grad: float32 [32, 1024, 768], P(('dp', 'fsdp'))
- attngain_grad: float32 [768], P(('dp', 'fsdp'))
- attnshift_grad: float32 [768], P(('dp', 'fsdp'))
- qkvmatrix_grad: float32 [768, 2304], P(('dp', 'fsdp'))
- qvoffset_grad: float32 [1536], P(('dp', 'fsdp'))
- outmatrix_grad: float32 [768, 768], P(('dp', 'fsdp'))
- outoffset_grad: float32 [768], P(('dp', 'fsdp'))
- mlpgain_grad: float32 [768], P(('dp', 'fsdp'))
- mlpshift_grad: float32 [768], P(('dp', 'fsdp'))
- upmatrix_grad: float32 [768, 3072], P(('dp', 'fsdp'))
- upoffset_grad: float32 [3072], P(('dp', 'fsdp'))
- downmatrix_grad: float32 [3072, 768], P(('dp', 'fsdp'))
- downoffset_grad: float32 [768], P(('dp', 'fsdp'))
The draws below stay inside these ranges and needn't reach their ends.
Inputs may be any that keep to these rules, and one draw needn't show every extreme that they name: `document_ids`: in each packed row the document numbers start at 0 and never fall; a document holds at most 512 tokens, and one of each row holds exactly that many.
All inputs are finite; a program needn't handle non-finite values.
Results may differ from the reference program's by a relative error of at most 0.0095.
Values may be sent and summed in bfloat16 or wider, within the bound.
A program may use at most 256 MiB of HBM per device.

```python
import math
from functools import partial
import jax
import jax.numpy as jnp
import numpy as np
from jax import lax

D = 768
HEADS = 12
HEAD_DIM = 64
FF = 3072
LAYERS = 12
LEN = 1024
DOCS = 4
ROWS = 32


def draw_tokens(key, part):
    key = jax.random.fold_in(key, 11)
    row_key, col_key, base_key = jax.random.split(key, 3)
    row_scale = jnp.exp(jax.random.uniform(row_key, (ROWS, LEN, 1), jnp.float32, math.log(0.3), math.log(3.0)))
    col_scale = jnp.exp(jax.random.uniform(col_key, (1, 1, D), jnp.float32, math.log(0.3), math.log(3.0)))
    base = jax.random.truncated_normal(base_key, -4.0, 4.0, (ROWS, LEN, D), jnp.float32)
    values = base * row_scale * col_scale
    return values.astype(jnp.bfloat16)


def block_scale(stream_key, dims, pieces, low, largest):
    loudness, own = 1.0, jax.random.fold_in(stream_key, 6)
    for dim, parts in pieces:
        draws = jnp.exp(jax.random.uniform(jax.random.fold_in(own, dim), (parts,), jnp.float32, low / len(pieces), largest / len(pieces)))
        loudness = loudness * jnp.repeat(draws, dims[dim] // parts).reshape([-1 if axis == dim else 1 for axis in range(len(dims))])
    return loudness


def length_profile(amount, total, reach, slope):
    weights = [(1 << 20) // math.isqrt(grade ** slope) + 1 for grade in range(2, amount + 1)]
    spare, given = total - reach - (amount - 1), [1] * (amount - 1)
    while spare > 0:
        movable = [i for i in range(amount - 1) if given[i] < reach]
        mass, budget = sum([weights[i] for i in movable]), spare
        for i in movable:
            extra = min(reach - given[i], max(1, budget * weights[i] // mass), spare)
            given[i] = given[i] + extra
            spare = spare - extra
    return np.array([reach] + given)


def ragged_sizes(stream_key, number_of, total, most, skew):
    if number_of == 2:
        one = jax.random.randint(stream_key, (), max(1, total - most), min(most, total - 1) + 1)
        return jnp.stack([one, total - one])
    sizes = jnp.asarray(length_profile(number_of, total, most, skew), jnp.int32)
    couples = (number_of - 1) // 2
    source_of, taker = sizes[1:1 + 2 * couples:2], sizes[2:2 + 2 * couples:2]
    room = jnp.minimum(source_of - 1, most - taker)
    passed = jax.random.randint(jax.random.fold_in(stream_key, 1), (couples,), 0, 1 << 20) % (room + 1)
    sizes = sizes.at[1:1 + 2 * couples:2].set(source_of - passed).at[2:2 + 2 * couples:2].set(taker + passed)
    return sizes[jax.random.permutation(jax.random.fold_in(stream_key, 2), number_of)]


def bell_draw(stream_key, dims, scale, limit, cuts=(), held_as=jnp.bfloat16):
    array = scale * jax.random.normal(stream_key, dims, jnp.float32)
    if cuts:
        array = array * block_scale(stream_key, dims, cuts, -0.22, 0.18)
    return jnp.clip(array, -limit, limit).astype(held_as)


def setup_inputs(seed: int = 0) -> dict:
    seeds = jax.random.split(jax.random.key(seed), 17)
    tokens = draw_tokens(jax.random.fold_in(seeds[16], 71), 0)
    cotangent = bell_draw(seeds[1], (ROWS, LEN, D), 1.0, 6.0, ((0, 32),))
    document_ids = jax.vmap(lambda own: jnp.searchsorted(jnp.cumsum(ragged_sizes(own, DOCS, LEN, LEN // 2, 0)), jnp.arange(LEN), side="right"))(jax.random.split(seeds[2], ROWS)).reshape((ROWS, LEN)).astype(jnp.int32)
    source_layer = jax.random.randint(seeds[3], (), 0, LAYERS).astype(jnp.int32)
    attngain = jnp.clip(1.0 + 0.1 * jax.random.normal(seeds[4], (LAYERS, D), jnp.float32), 0.5, 1.5).astype(jnp.bfloat16)
    attnshift = bell_draw(seeds[5], (LAYERS, D), 0.5, 3.0, ((1, 32),))
    qkvmatrix = bell_draw(seeds[6], (LAYERS, D, 3 * D), D ** -0.5, 0.21875, ((1, 32),))
    qvoffset = bell_draw(seeds[7], (LAYERS, 2 * D), 0.5, 3.0, ((1, 32),))
    outmatrix = bell_draw(seeds[8], (LAYERS, D, D), (D // 16) ** -0.5, 0.875, ((1, 32),))
    outoffset = bell_draw(seeds[9], (LAYERS, D), 0.5, 3.0, ((1, 32),))
    mlpgain = jnp.clip(1.0 + 0.1 * jax.random.normal(seeds[10], (LAYERS, D), jnp.float32), 0.5, 1.5).astype(jnp.bfloat16)
    mlpshift = bell_draw(seeds[11], (LAYERS, D), 0.5, 3.0, ((1, 32),))
    upmatrix = bell_draw(seeds[12], (LAYERS, D, FF), D ** -0.5, 0.21875, ((1, 32),))
    upoffset = bell_draw(seeds[13], (LAYERS, FF), 0.5, 3.0, ((1, 32),))
    downmatrix = bell_draw(seeds[14], (LAYERS, FF, D), FF ** -0.5, 0.109375, ((1, 32),))
    downoffset = bell_draw(seeds[15], (LAYERS, D), 0.5, 3.0, ((1, 32),))
    return dict(tokens=tokens, cotangent=cotangent, document_ids=document_ids, source_layer=source_layer, attngain=attngain, attnshift=attnshift, qkvmatrix=qkvmatrix, qvoffset=qvoffset, outmatrix=outmatrix, outoffset=outoffset, mlpgain=mlpgain, mlpshift=mlpshift, upmatrix=upmatrix, upoffset=upoffset, downmatrix=downmatrix, downoffset=downoffset)


EPSILON = 1e-05
NEG_LARGE = -1000000000.0
GELU_COEF = 0.7978845608028654

@jax.custom_vjp
def low(v):
    return lax.optimization_barrier(v.astype(jnp.bfloat16)).astype(jnp.float32)

@jax.custom_vjp
def low_back(v):
    return v

def low_keep(v):
    return (low(v), None)

def low_pass(kept, grad):
    return (grad,)

def back_keep(v):
    return (v, None)

def back_low(kept, grad):
    return (low(grad),)
low.defvjp(low_keep, low_pass)
low_back.defvjp(back_keep, back_low)

def layer_norm(values, scaling, offset):
    centre = lax.optimization_barrier(jnp.mean(values, axis=-1, keepdims=True))
    spread = lax.optimization_barrier(jnp.mean(jnp.square(values - centre), axis=-1, keepdims=True))
    return (values - centre) * lax.rsqrt(spread + EPSILON) * scaling + offset

def gelu_tanh(values):
    cubic = values + 0.044715 * values * values * values
    return 0.5 * values * (1.0 + jnp.tanh(GELU_COEF * cubic))

def matmul(left, right):
    return jnp.dot(left, right, preferred_element_type=jnp.float32, precision=lax.Precision.HIGHEST)

def block_forward(documents, params, inputs):
    gain_one, shift_one, qkv_w, qv_b, out_w, out_b, gain_two, shift_two, up_w, up_b, down_w, down_b = params
    group_rows, length_rows, model_width = inputs.shape
    flat = inputs.reshape(-1, model_width)
    normed_one = low(layer_norm(flat, gain_one, shift_one))
    projected = matmul(normed_one, qkv_w)
    queries = low(low_back(projected[:, :model_width] + qv_b[:model_width]))
    key_rows = low(low_back(projected[:, model_width:2 * model_width]))
    value_rows = low(low_back(projected[:, 2 * model_width:] + qv_b[model_width:]))
    head_shape = (group_rows, length_rows, HEADS, HEAD_DIM)
    queries = queries.reshape(head_shape)
    key_rows = key_rows.reshape(head_shape)
    value_rows = value_rows.reshape(head_shape)
    scores = jnp.einsum('gqhd,gkhd->ghqk', queries, key_rows, precision=lax.Precision.HIGHEST) * HEAD_DIM ** (-0.5)
    scores = low_back(scores)
    positions = jnp.arange(length_rows)
    causal = positions[None, :] <= positions[:, None]
    same_doc = documents[:, None, :] == documents[:, :, None]
    allowed = causal[None] & same_doc
    masked = jnp.where(allowed[:, None], scores, NEG_LARGE)
    soft_rows = low(jax.nn.softmax(masked, axis=-1))
    mixed = jnp.einsum('ghqk,gkhd->gqhd', soft_rows, value_rows, precision=lax.Precision.HIGHEST)
    mixed = low(low_back(mixed.reshape(-1, model_width)))
    attended = low_back(matmul(mixed, out_w) + out_b)
    residual = flat + attended
    normed_two = low(layer_norm(residual, gain_two, shift_two))
    expanded = low_back(matmul(normed_two, up_w) + up_b)
    activated = low(gelu_tanh(expanded))
    result = residual + low_back(matmul(activated, down_w) + down_b)
    return result.reshape(inputs.shape)

def reference(tokens, cotangent, document_ids, source_layer, attngain, attnshift, qkvmatrix, qvoffset, outmatrix, outoffset, mlpgain, mlpshift, upmatrix, upoffset, downmatrix, downoffset):
    stacks = (attngain, attnshift, qkvmatrix, qvoffset, outmatrix, outoffset, mlpgain, mlpshift, upmatrix, upoffset, downmatrix, downoffset)
    params = tuple((lax.dynamic_index_in_dim(stack, source_layer, 0, keepdims=False).astype(jnp.float32) for stack in stacks))
    groups = ROWS // 4
    tok_groups = tokens.astype(jnp.float32).reshape(groups, 4, LEN, D)
    cot_groups = cotangent.astype(jnp.float32).reshape(groups, 4, LEN, D)
    doc_groups = document_ids.reshape(groups, 4, LEN)

    def step(totals, operands):
        tok_group, cot_group, doc_group = operands
        output, pullback = jax.vjp(partial(block_forward, doc_group), params, tok_group)
        param_grads, input_part = pullback(cot_group)
        totals = jax.tree.map(jnp.add, totals, param_grads)
        return (totals, (output, input_part))
    zeros = jax.tree.map(jnp.zeros_like, params)
    totals, stacked = lax.scan(step, zeros, (tok_groups, cot_groups, doc_groups))
    outputs, input_grads = stacked
    return (outputs.reshape(ROWS, LEN, D), input_grads.reshape(ROWS, LEN, D), totals[0], totals[1], totals[2], totals[3], totals[4], totals[5], totals[6], totals[7], totals[8], totals[9], totals[10], totals[11])
```

```python
import functools

import jax
import jax.numpy as jnp
from jax import lax
from jax.experimental import pallas as pl
from jax.experimental.pallas import tpu as pltpu
from jax.sharding import PartitionSpec as P

MESH = pl.DeviceIdType.MESH
F32 = jnp.float32
BF = jnp.bfloat16
EPSILON = 1e-05
NEG_LARGE = -1000000000.0
GELU_COEF = 0.7978845608028654
GELU_CUBIC = 0.044715
WIDTH = 768
HALF = 384
HEAD = 64
QB = 256
VEC_ROWS = 8
VMEM_BYTES = 63 * 2**20
VEC_SIZES = (1, 1, 2, 1, 1, 1, 4, 1)
QKV, OUT, UP, DOWN = 0, 3, 4, 8
UNITS = 12


def dg(left, right, left_dim, right_dim):
    return lax.dot_general(
        left, right, (((left_dim,), (right_dim,)), ((), ())), preferred_element_type=F32
    )


def mm(left, right):
    return jnp.dot(left, right, preferred_element_type=F32)


def pack_kernel(layer_ref, *refs):
    vec_in, (qkv, out, up, down), units, vec_out = refs[:8], refs[8:12], refs[12], refs[13]
    layer = layer_ref[0]
    for t in range(3):
        for part in range(3):
            units[t, :, 256 * part : 256 * part + 256] = qkv[
                0, :, WIDTH * part + 256 * t : WIDTH * part + 256 * t + 256
            ]
    units[OUT] = out[0]
    for j in range(4):
        units[UP + j] = up[0, :, WIDTH * j : WIDTH * j + WIDTH]
    rows = units.shape[1]
    wide = down[0].astype(F32)
    for j in range(4):
        units[DOWN + j] = wide[rows * j : rows * j + rows].astype(BF)
    vec_out[...] = jnp.zeros_like(vec_out)
    for r, ref in enumerate(vec_in):
        stack = ref[...].astype(F32)
        index = lax.broadcasted_iota(jnp.int32, stack.shape, 0)
        row = jnp.sum(jnp.where(index == layer, stack, 0.0), axis=0, keepdims=True)
        vec_out[r : r + 1, 0 : stack.shape[1]] = row


def pack_layer(layer, vectors, matrices):
    rows = matrices[0].shape[1]
    whole = [pl.BlockSpec(v.shape, lambda i, s: (0, 0)) for v in vectors]
    picked = [
        pl.BlockSpec((1,) + m.shape[1:], lambda i, s: (s[0], 0, 0)) for m in matrices
    ]
    return pl.pallas_call(
        pack_kernel,
        grid_spec=pltpu.PrefetchScalarGridSpec(
            num_scalar_prefetch=1,
            grid=(1,),
            in_specs=whole + picked,
            out_specs=[
                pl.BlockSpec((UNITS, rows, WIDTH), lambda i, s: (0, 0, 0)),
                pl.BlockSpec((VEC_ROWS, 128), lambda i, s: (0, 0)),
            ],
        ),
        out_shape=[
            jax.ShapeDtypeStruct((UNITS, rows, WIDTH), BF),
            jax.ShapeDtypeStruct((VEC_ROWS, 128), F32),
        ],
        name="pick_layer",
    )(layer.reshape(1), *vectors, *matrices)


def page_maps(shards, width):
    total = shards * width
    col = lax.broadcasted_iota(jnp.int32, (128, total), 1).astype(F32)
    place = lax.broadcasted_iota(jnp.int32, (128, total), 0).astype(F32)
    one_hot = (col - jnp.floor((col + 0.5) / width) * width) == place
    col_s = lax.broadcasted_iota(jnp.int32, (shards, total), 1).astype(F32)
    page = lax.broadcasted_iota(jnp.int32, (shards, total), 0).astype(F32)
    mine = jnp.floor((col_s + 0.5) / width) == page
    return one_hot, mine


def pages_to_rows(pages, fvec, shards):
    base = WIDTH // shards
    for size in sorted(set(VEC_SIZES)):
        width = base * size
        one_hot, mine = page_maps(shards, width)
        one_hot = one_hot.astype(BF)
        for r, s in enumerate(VEC_SIZES):
            if s == size:
                spread = mm(pages[:, r, :].astype(BF), one_hot)
                fvec[r : r + 1, 0 : WIDTH * size] = jnp.sum(
                    jnp.where(mine, spread, 0.0), axis=0, keepdims=True
                )


def rows_to_pages(svec, pages, shards):
    base = WIDTH // shards
    for size in sorted(set(VEC_SIZES)):
        width = base * size
        one_hot, mine = page_maps(shards, width)
        one_hot = one_hot.astype(F32)
        for r, s in enumerate(VEC_SIZES):
            if s == size:
                spread = jnp.where(mine, svec[r : r + 1, 0 : WIDTH * size], 0.0)
                pages[:, r, :] = lax.dot_general(
                    spread,
                    one_hot,
                    (((1,), (1,)), ((), ())),
                    preferred_element_type=F32,
                    precision=lax.Precision.HIGHEST,
                )


def norm_stats(values):
    mean = jnp.mean(values, axis=-1, keepdims=True)
    centred = values - mean
    spread = jnp.mean(centred * centred, axis=-1, keepdims=True)
    scale = lax.rsqrt(spread + EPSILON)
    return centred * scale, scale


def norm_back(grad, gain, normed, scale):
    scaled = grad * gain
    mean_one = jnp.mean(scaled, axis=-1, keepdims=True)
    mean_two = jnp.mean(scaled * normed, axis=-1, keepdims=True)
    return scale * (scaled - mean_one - normed * mean_two)


def key_ranges(length):
    reach = length // 2
    return [(max(0, i * QB - reach), (i + 1) * QB) for i in range(length // QB)]


def mask_blocks(length):
    blocks = {}
    for i, (lo, hi) in enumerate(key_ranges(length)):
        for key in range(lo, hi, QB):
            blocks[i, key // QB] = len(blocks)
    return blocks


def build_masks(doc_ref, masks, transposed):
    length = doc_ref.shape[1]
    row = doc_ref[...].astype(F32)
    for (i, b), at in mask_blocks(length).items():
        queries = row[:, i * QB : (i + 1) * QB]
        keys = row[:, b * QB : (b + 1) * QB]
        along, down = (queries, keys) if transposed else (keys, queries)
        down = jnp.transpose(jnp.broadcast_to(down, (128, QB)))
        down = jnp.concatenate([down, down], 1)
        q_dim = 1 if transposed else 0
        q_pos = lax.broadcasted_iota(jnp.int32, (QB, QB), q_dim) + i * QB
        k_pos = lax.broadcasted_iota(jnp.int32, (QB, QB), 1 - q_dim) + b * QB
        masks[at] = jnp.where((k_pos <= q_pos) & (down == along), 0.0, NEG_LARGE)


def head_lanes(values, head, other=0.0):
    lane = lax.broadcasted_iota(jnp.int32, values.shape, 1)
    keep = lane >= HEAD if head else lane < HEAD
    return jnp.where(keep, values, jnp.full(values.shape, other, values.dtype))


def pair_lanes(unit, half):
    start = [unit * WIDTH + 256 * part for part in range(3)]
    return [pl.ds(pl.multiple_of(s + 128 * half, 128), 128) for s in start]


def forward_pair(unit, half, qkv, mixed, lse, masks):
    length = qkv.shape[0]
    lanes_q, lanes_k, lanes_v = pair_lanes(unit, half)
    ranges, blocks = key_ranges(length), mask_blocks(length)
    pair = 2 * unit + half
    lanes_o = pl.ds(pl.multiple_of(pair * 128, 128), 128)
    steps = [(i, h) for i in range(len(ranges)) for h in range(2)]

    def scores(step):
        i, h = step
        lo, hi = ranges[i]
        rows = slice(i * QB, (i + 1) * QB)
        raw = dg(head_lanes(qkv[rows, lanes_q], h), qkv[lo:hi, lanes_k], 1, 1)
        mask = [masks[blocks[i, b]] for b in range(lo // QB, hi // QB)]
        return raw + jnp.concatenate(mask, 1)

    def finish(step, score):
        i, h = step
        lo, hi = ranges[i]
        top = jnp.max(score, axis=1, keepdims=True)
        soft = jnp.exp(score - top).astype(BF)
        return mm(soft, head_lanes(qkv[lo:hi, lanes_v], h, 1.0)), top

    current, done = scores(steps[0]), {}
    for n, step in enumerate(steps):
        following = scores(steps[n + 1]) if n + 1 < len(steps) else None
        done[step] = finish(step, current)
        current = following
        i, h = step
        if h == 1:
            (acc0, top0), (acc1, top1) = done.pop((i, 0)), done.pop((i, 1))
            rows = slice(i * QB, (i + 1) * QB)
            first = lax.broadcasted_iota(jnp.int32, acc0.shape, 1) < HEAD
            total = pltpu.roll(jnp.where(first, acc1, acc0), HEAD, 1)
            mixed[rows, lanes_o] = (jnp.where(first, acc0, acc1) / total).astype(BF)
            logs = jnp.transpose(jnp.where(first, top0, top1) + jnp.log(total))
            lse[pair, 0:1, rows] = logs[0:1]
            lse[pair, 1:2, rows] = logs[HEAD : HEAD + 1]


def backward_pair(unit, half, qkv, mixed, mixed_grad, lse, masks, key_acc, value_acc):
    length = qkv.shape[0]
    lanes_q, lanes_k, lanes_v = pair_lanes(unit, half)
    ranges, blocks = key_ranges(length), mask_blocks(length)
    pair = 2 * unit + half
    lanes_o = pl.ds(pl.multiple_of(pair * 128, 128), 128)
    keys_t = jnp.transpose(qkv[:, lanes_k])
    steps = [(i, h) for i in range(len(ranges)) for h in range(2)]
    products = {}

    def start(step):
        i, h = step
        lo, hi = ranges[i]
        rows = slice(i * QB, (i + 1) * QB)
        query = head_lanes(qkv[rows, lanes_q], h)
        grad = head_lanes(mixed_grad[rows, lanes_o], h)
        mask = [masks[blocks[i, b]] for b in range(lo // QB, hi // QB)]
        score = dg(qkv[lo:hi, lanes_k], query, 1, 1) + jnp.concatenate(mask, 0)
        return score, dg(qkv[lo:hi, lanes_v], grad, 1, 1), query, grad

    def finish(step, started):
        i, h = step
        lo, hi = ranges[i]
        rows = slice(i * QB, (i + 1) * QB)
        score, soft_grad, query, grad = started
        if h == 0:
            products[i] = jnp.transpose(
                mixed_grad[rows, lanes_o].astype(F32) * mixed[rows, lanes_o].astype(F32)
            )
        soft = jnp.exp(score - lse[pair, h : h + 1, rows])
        centre = jnp.sum(products[i][HEAD * h : HEAD * h + HEAD], axis=0, keepdims=True)
        score_grad = (soft * (soft_grad - centre)).astype(BF)
        soft = soft.astype(BF)
        return (
            mm(keys_t[HEAD * h : HEAD * h + HEAD, lo:hi], score_grad),
            mm(score_grad, query),
            mm(soft, grad),
        )

    current, done = start(steps[0]), {}
    for n, step in enumerate(steps):
        following = start(steps[n + 1]) if n + 1 < len(steps) else None
        done[step] = finish(step, current)
        current = following
        i, h = step
        if h == 1:
            (q0, k0, v0), (q1, k1, v1) = done.pop((i, 0)), done.pop((i, 1))
            rows = slice(i * QB, (i + 1) * QB)
            lo, hi = ranges[i]
            query_grad = jnp.transpose(jnp.concatenate([q0, q1], 0))
            qkv[rows, lanes_q] = (query_grad * HEAD**-0.5).astype(BF)
            keys, values, old = k0 + k1, v0 + v1, hi - QB - lo
            if old:
                key_acc[lo : lo + old] += keys[:old]
                value_acc[lo : lo + old] += values[:old]
            key_acc[hi - QB : hi] = keys[old:]
            value_acc[hi - QB : hi] = values[old:]
    qkv[:, lanes_k] = key_acc[...].astype(BF)
    qkv[:, lanes_v] = value_acc[...].astype(BF)


class Exchange:
    def __init__(self, mesh_shape, weights, down, shards, refs):
        self.depth = mesh_shape["fsdp"] // 2
        self.weights, self.down, self.shards = weights, down, shards
        self.__dict__.update(refs)
        dp, fsdp = lax.axis_index("dp"), lax.axis_index("fsdp")
        self.y, self.c = dp // 2, dp % 2
        self.z, self.x = fsdp // 2, fsdp % 2
        self.waits, self.started = {}, []

    def device(self, y=None, c=None, z=None, x=None):
        y, c = self.y if y is None else y, self.c if c is None else c
        z, x = self.z if z is None else z, self.x if x is None else x
        return (y * 2 + c, z * 2 + x)

    def peers(self):
        far = [self.device(z=lax.rem(self.z + d, self.depth)) for d in range(1, self.depth)]
        return far + [
            self.device(x=1 - self.x),
            self.device(y=1 - self.y),
            self.device(c=1 - self.c),
        ]

    def barrier(self):
        barrier = pltpu.get_barrier_semaphore()
        peers = self.peers()
        for peer in peers:
            pl.semaphore_signal(barrier, inc=1, device_id=peer, device_id_type=MESH)
        pl.semaphore_wait(barrier, len(peers))

    def at(self, unit, y, c, z, x, lanes=slice(None)):
        if unit >= DOWN:
            return self.down.at[y, c, z, x, unit - DOWN, :, lanes]
        return self.weights.at[unit, y, c, z, x, :, lanes]

    def send(self, key, src, dst, sems, slot, device):
        copy = pltpu.make_async_remote_copy(
            src_ref=src,
            dst_ref=dst,
            send_sem=sems[0].at[slot],
            recv_sem=sems[1].at[slot],
            device_id=device,
            device_id_type=MESH,
        )
        copy.start()
        self.waits.setdefault(key, []).append(copy)

    def received(self, key):
        for copy in self.waits[key]:
            copy.wait_recv()

    def sent(self, *keys):
        for key in keys:
            for copy in self.waits.pop(key):
                copy.wait_send()

    def gather_start(self, unit):
        for d in range(1, self.depth):
            there = self.device(z=lax.rem(self.z + d, self.depth))
            place = self.at(unit, self.y, self.c, self.z, self.x)
            self.send(("g1", unit), self.shards.at[unit], place, self.gather_sems, 10 * unit + d, there)
        place = self.at(unit, self.y, self.c, self.z, self.x)
        local = pltpu.make_async_copy(self.shards.at[unit], place, self.local_sems.at[unit])
        local.start()
        self.waits["local", unit] = local

    def gather_step(self, unit, step):
        y, c, z, x = self.y, self.c, self.z, self.x
        low, high, every = slice(0, HALF), slice(HALF, WIDTH), slice(None)
        sems, base = self.gather_sems, 10 * unit
        to_x, to_y, to_c = self.device(x=1 - x), self.device(y=1 - y), self.device(c=1 - c)
        if step == 2:
            self.waits["local", unit].wait()
            self.received(("g1", unit))
            column = lambda lanes: self.at(unit, y, c, every, x, lanes)
            self.send(("g2", unit), column(low), column(low), sems, base + 4, to_x)
            self.send(("g2", unit), column(high), column(high), sems, base + 5, to_y)
        elif step == 3:
            self.received(("g2", unit))
            one = self.at(unit, y, c, every, every, low)
            two = self.at(unit, every, c, every, x, high)
            self.send(("g3", unit), one, one, sems, base + 6, to_y)
            self.send(("g3", unit), two, two, sems, base + 7, to_x)
        elif step == 4:
            self.received(("g3", unit))
            core = self.at(unit, every, c, every, every)
            self.send(("g4", unit), core, core, sems, base + 8, to_c)

    def gathered(self, unit):
        self.received(("g4", unit))

    def gather_sent(self, unit):
        self.sent(*[(g, unit) for g in ("g1", "g2", "g3", "g4")])

    def gather_vectors(self, step):
        y, c, z, x = self.y, self.c, self.z, self.x
        pages, every, sems = self.vec_pages, slice(None), self.vec_sems
        if step == 1:
            for d in range(1, self.depth):
                there = self.device(z=lax.rem(z + d, self.depth))
                self.send("v1", self.vec_shard, pages.at[y, c, z, x], sems, d, there)
            local = pltpu.make_async_copy(self.vec_shard, pages.at[y, c, z, x], self.local_sems.at[UNITS])
            local.start()
            self.waits["vlocal"] = local
        elif step == 2:
            self.waits["vlocal"].wait()
            self.received("v1")
            part = pages.at[y, c, :, x]
            self.send("v2", part, part, sems, 4, self.device(x=1 - x))
        elif step == 3:
            self.received("v2")
            part = pages.at[y, c]
            self.send("v3", part, part, sems, 5, self.device(y=1 - y))
        elif step == 4:
            self.received("v3")
            part = pages.at[:, c]
            self.send("v4", part, part, sems, 6, self.device(c=1 - c))
        else:
            self.received("v4")
            self.sent("v1", "v2", "v3", "v4")

    def add(self, place, other):
        place[...] = (place[...].astype(F32) + other[...].astype(F32)).astype(BF)

    def sum_down_start(self, half):
        core = self.down.at[half, 1 - self.c]
        self.send(("s1d", half), core, self.from_core_down.at[half], self.sum_sems, 10 * UNITS + half, self.device(c=1 - self.c))

    def sum_start(self, unit):
        core = self.at(unit, slice(None), 1 - self.c, slice(None), slice(None))
        self.send(("s1", unit), core, self.from_core.at[unit], self.sum_sems, 10 * unit, self.device(c=1 - self.c))

    def sum_step(self, unit, step):
        y, c, z, x = self.y, self.c, self.z, self.x
        low, high, every = slice(0, HALF), slice(HALF, WIDTH), slice(None)
        sems, base = self.sum_sems, 10 * unit
        to_x, to_y = self.device(x=1 - x), self.device(y=1 - y)
        if step == 2:
            if unit >= DOWN:
                if unit == DOWN:
                    self.received(("s1d", 0))
                    self.received(("s1d", 1))
                for half in range(2):
                    for k in range(self.depth):
                        self.add(
                            self.down.at[half, c, k, :, unit - DOWN],
                            self.from_core_down.at[half, k, :, unit - DOWN],
                        )
            else:
                self.received(("s1", unit))
                for half in range(2):
                    self.add(self.weights.at[unit, half, c], self.from_core.at[unit, half])
            self.send(("s2", unit), self.at(unit, 1 - y, c, every, every, low), self.from_two.at[unit, 0], sems, base + 1, to_y)
            for half in range(2):
                self.send(("s2", unit), self.at(unit, half, c, every, 1 - x, high), self.from_two.at[unit, 1, :, half], sems, base + 2 + half, to_x)
        elif step == 3:
            self.received(("s2", unit))
            for k in range(self.depth):
                for xx in range(2):
                    self.add(self.at(unit, y, c, k, xx, low), self.from_two.at[unit, 0, k, xx])
                for half in range(2):
                    self.add(self.at(unit, half, c, k, x, high), self.from_two.at[unit, 1, k, half])
            self.send(("s3", unit), self.at(unit, y, c, every, 1 - x, low), self.from_three.at[unit, 0], sems, base + 4, to_x)
            self.send(("s3", unit), self.at(unit, 1 - y, c, every, x, high), self.from_three.at[unit, 1], sems, base + 5, to_y)
        elif step == 4:
            self.received(("s3", unit))
            for k in range(self.depth):
                self.add(self.at(unit, y, c, k, x, low), self.from_three.at[unit, 0, k])
                self.add(self.at(unit, y, c, k, x, high), self.from_three.at[unit, 1, k])
            for d in range(1, self.depth):
                zz = lax.rem(z + d, self.depth)
                self.send(("s4", unit), self.at(unit, y, c, zz, x), self.from_four.at[unit, d - 1], sems, base + 5 + d, self.device(z=zz))
        elif step == 5:
            self.received(("s4", unit))
            total = self.at(unit, y, c, z, x)[...].astype(F32)
            for d in range(self.depth - 1):
                total += self.from_four[unit, d].astype(F32)
            rows = total.shape[0]
            if unit < OUT:
                for part in range(3):
                    start = WIDTH * part + 256 * unit
                    self.qkv_sum[:, start : start + 256] = total[:, 256 * part : 256 * part + 256]
            elif unit == OUT:
                self.out_sum[...] = total
            elif unit < DOWN:
                start = WIDTH * (unit - UP)
                self.up_sum[:, start : start + WIDTH] = total
            else:
                start = rows * (unit - DOWN)
                self.down_sum[start : start + rows] = total

    def sum_vectors(self, step):
        y, c, z, x = self.y, self.c, self.z, self.x
        pages, sems, every = self.vec_pages, self.vec_sems, slice(None)
        landing = self.vec_landing
        if step == 1:
            self.send("w1", pages.at[:, 1 - c], landing.at[0:2], sems, 7, self.device(c=1 - c))
        elif step == 2:
            self.received("w1")
            pages[:, c] = pages[:, c] + landing[0:2]
            self.send("w2", pages.at[1 - y, c], landing.at[2], sems, 8, self.device(y=1 - y))
        elif step == 3:
            self.received("w2")
            pages[y, c] = pages[y, c] + landing[2]
            self.send("w3", pages.at[y, c, :, 1 - x], landing.at[3, :, 0], sems, 9, self.device(x=1 - x))
        elif step == 4:
            self.received("w3")
            for k in range(self.depth):
                pages[y, c, k, x] = pages[y, c, k, x] + landing[3, k, 0]
            for d in range(1, self.depth):
                zz = lax.rem(z + d, self.depth)
                self.send("w4", pages.at[y, c, zz, x], landing.at[3, d, 1], sems, 9 + d, self.device(z=zz))
        else:
            self.received("w4")
            total = pages[y, c, z, x]
            for d in range(1, self.depth):
                total = total + landing[3, d, 1]
            self.vec_sum[...] = total
            self.sent("w1", "w2", "w3", "w4")


def block_kernel(mesh_shape, exchanged, *refs):
    refs = list(refs)
    take = lambda n: [refs.pop(0) for _ in range(n)]
    tokens, cotangent, documents = take(3)
    if exchanged:
        shards, vec_shard = take(2)
    else:
        weights_in, down_in, vectors_in = take(3)
    result, input_grad = take(2)
    if exchanged:
        qkv_sum, out_sum, up_sum, down_sum, vec_sum = take(5)
    else:
        weights_out, down_out, vectors_out = take(3)
    (weights, down, cot, normed_one, qkv, mixed, lse, masks, residual, normed_two) = take(10)
    (acc_one, acc_two, low_one, low_two, key_acc, value_acc, fvec, svec, io_sems) = take(9)
    x_in = low_two
    length = x_in.shape[0]
    tiles = length // QB

    ex = None
    if exchanged:
        names = ("vec_pages", "vec_landing", "from_core", "from_core_down", "from_two", "from_three", "from_four")
        extra = dict(zip(names, take(len(names))))
        gs, gr, ss, sr, vs, vr, local = take(7)
        extra.update(gather_sems=(gs, gr), sum_sems=(ss, sr), vec_sems=(vs, vr), local_sems=local)
        extra.update(vec_shard=vec_shard, qkv_sum=qkv_sum, out_sum=out_sum, up_sum=up_sum, down_sum=down_sum, vec_sum=vec_sum)
        ex = Exchange(mesh_shape, weights, down, shards, extra)

    def matrix(unit, start=0, width=WIDTH):
        if exchanged:
            return weights[unit, :, :, :, :, :, start : start + width].reshape(WIDTH, width)
        return weights[unit, :, start : start + width]

    def matrix_store(unit, half, values):
        if exchanged:
            weights[unit, half] = values.astype(BF).reshape(weights.shape[2:])
        else:
            weights[unit, HALF * half : HALF * half + HALF] = values.astype(BF)

    def down_rows(chunk, half):
        if exchanged:
            depth = mesh_shape["fsdp"] // 4
            part = down[chunk // 2, chunk % 2, depth * half : depth * half + depth]
            return part.reshape(HALF, WIDTH)
        start = WIDTH * chunk + HALF * half
        return down[start : start + HALF]

    def down_store(chunk, half, values):
        if exchanged:
            depth = mesh_shape["fsdp"] // 4
            part = down.at[chunk // 2, chunk % 2, depth * half : depth * half + depth]
            part[...] = values.astype(BF).reshape(part.shape)
        else:
            start = WIDTH * chunk + HALF * half
            down[start : start + HALF] = values.astype(BF)

    def down_chunk(chunk):
        return jnp.concatenate([down_rows(chunk, 0), down_rows(chunk, 1)], 0)

    def tile_loop(body, size=QB):
        def step(i, carry):
            body(pl.ds(pl.multiple_of(i * size, size), size), i)
            return carry

        lax.fori_loop(0, length // size, step, 0)

    def fv(row, size=1):
        return fvec[row : row + 1, 0 : WIDTH * size]

    copies = {}

    def start_copy(slot, src, dst):
        copies[slot] = pltpu.make_async_copy(src, dst, io_sems.at[slot])
        copies[slot].start()

    start_copy(0, tokens, x_in)
    start_copy(1, cotangent, cot)
    if exchanged:
        ex.barrier()
        ex.gather_vectors(1)
        for unit in range(3):
            ex.gather_start(unit)
        ex.gather_start(OUT)
        for unit in range(DOWN, UNITS):
            ex.gather_start(unit)
        for unit in range(UP, DOWN):
            ex.gather_start(unit)
    else:
        start_copy(2, weights_in, weights)
        start_copy(3, down_in, down)

    order = [0, 1, 2, OUT, *range(DOWN, UNITS), *range(UP, DOWN)]

    def tick(k):
        if not exchanged:
            return
        for back, step in ((2, 4), (1, 3), (0, 2)):
            if 0 <= k - back < len(order):
                ex.gather_step(order[k - back], step)

    def arrived(unit):
        if exchanged:
            ex.gathered(unit)

    if exchanged:
        ex.gather_vectors(2)
        tick(0)
        ex.gather_vectors(3)
        build_masks(documents, masks, False)
        ex.gather_vectors(4)
        tick(1)
        ex.gather_vectors(5)
        pages_to_rows(ex.vec_pages.reshape(32, VEC_ROWS, 128), fvec, 32)
        tick(2)
    else:
        build_masks(documents, masks, False)
        fvec[...] = vectors_in[...]
    copies[0].wait()

    def norm_one(rows, i):
        normed, _ = norm_stats(x_in[rows].astype(F32))
        normed_one[rows] = (normed * fv(0) + fv(1)).astype(BF)

    tile_loop(norm_one)
    if not exchanged:
        copies[2].wait()
        copies[3].wait()

    for unit in range(3):
        arrived(unit)

        def project(rows, i, unit=unit):
            full = mm(normed_one[rows], matrix(unit))
            lanes = slice(256 * unit, 256 * unit + 256)
            bias = fvec[2:3, 256 * unit : 256 * unit + 256]
            query = (full[:, 0:256] + bias).astype(BF).astype(F32) * HEAD**-0.5
            base = WIDTH * unit
            qkv[rows, base : base + 256] = query.astype(BF)
            qkv[rows, base + 256 : base + 512] = full[:, 256:512].astype(BF)
            bias = fvec[2:3, WIDTH + 256 * unit : WIDTH + 256 * unit + 256]
            qkv[rows, base + 512 : base + WIDTH] = (full[:, 512:] + bias).astype(BF)

        tile_loop(project, 2 * QB)
        tick(3 + unit)

        def pair_step(half, carry, unit=unit):
            forward_pair(unit, half, qkv, mixed, lse, masks)
            return carry

        lax.fori_loop(0, 2, pair_step, 0)

    tick(6)
    arrived(OUT)
    copies[1].wait()

    def attend(rows, i):
        total = x_in[rows].astype(F32) + (mm(mixed[rows], matrix(OUT)) + fv(3))
        residual[rows] = total
        normed, _ = norm_stats(total)
        normed_two[rows] = (normed * fv(4) + fv(5)).astype(BF)
        acc_one[rows] = total + fv(7)

    tile_loop(attend)
    build_masks(documents, masks, True)
    tick(7)
    tick(8)
    tick(9)
    for unit in range(DOWN, UNITS):
        arrived(unit)

    def tokens_sum(values):
        return jnp.sum(values.astype(F32), axis=0, keepdims=True)

    for chunk in range(4):
        if chunk < 2:
            tick(10 + 2 * chunk)
            tick(11 + 2 * chunk)
        arrived(UP + chunk)
        svec[6:7, WIDTH * chunk : WIDTH * chunk + WIDTH] = jnp.zeros((1, WIDTH), F32)
        for half in range(2):
            lanes = slice(HALF * half, HALF * half + HALF)
            wide = slice(WIDTH * chunk + HALF * half, WIDTH * chunk + HALF * half + HALF)

            def hidden(start, chunk=chunk, half=half, wide=wide):
                rows = slice(start, start + QB)
                pre = mm(normed_two[rows], matrix(UP + chunk, HALF * half, HALF)) + fvec[6:7, wide]
                return pre, dg(cot[rows], down_rows(chunk, half), 1, 1)

            def activate(start, pair, lanes=lanes, wide=wide):
                pre, grad = pair
                square = pre * pre
                bent = jnp.tanh(pre * (GELU_COEF + (GELU_COEF * GELU_CUBIC) * square))
                upper = 0.5 + 0.5 * bent
                slope = upper + (0.5 * pre) * (1.0 - bent * bent) * (
                    GELU_COEF + (3.0 * GELU_COEF * GELU_CUBIC) * square
                )
                rows = slice(start, start + QB)
                low_one[rows, lanes] = (pre * upper).astype(BF)
                back = (grad * slope).astype(BF)
                low_two[rows, lanes] = back
                svec[6:7, wide] += tokens_sum(back)

            current = hidden(0)
            for i in range(tiles):
                following = hidden((i + 1) * QB) if i + 1 < tiles else None
                activate(i * QB, current)
                current = following

        def outward(rows, i, chunk=chunk):
            acc_one[rows] += mm(low_one[rows], down_chunk(chunk))
            back = dg(low_two[rows], matrix(UP + chunk), 1, 1)
            if chunk == 0:
                acc_two[rows] = back
            else:
                acc_two[rows] += back

        tile_loop(outward, 2 * QB)
        if exchanged:
            if chunk == 0:
                for unit in range(DOWN, UNITS):
                    ex.gather_sent(unit)
            ex.gather_sent(UP + chunk)
        for half in range(2):
            lanes = slice(HALF * half, HALF * half + HALF)
            down_store(chunk, half, dg(low_one[:, lanes], cot[...], 0, 0))
        for half in range(2):
            lanes = slice(HALF * half, HALF * half + HALF)
            matrix_store(UP + chunk, half, dg(normed_two[:, lanes], low_two[...], 0, 0))
        if exchanged:
            ex.sum_start(UP + chunk)
            if chunk % 2:
                ex.sum_down_start(chunk // 2)

    start_copy(4, acc_one, result)

    for row in (0, 1, 3, 4, 5, 7):
        svec[row : row + 1, 0:WIDTH] = jnp.zeros((1, WIDTH), F32)

    def back_two(rows, i):
        normed, scale = norm_stats(residual[rows])
        grad = acc_two[rows]
        grads = cot[rows].astype(F32)
        total = grads + norm_back(grad, fv(4), normed, scale)
        acc_two[rows] = total
        low = total.astype(BF)
        low_two[rows] = low
        for row, part in ((4, grad * normed), (5, grad), (7, grads), (3, low)):
            svec[row : row + 1, 0:WIDTH] += tokens_sum(part)

    tile_loop(back_two)

    def back_out(rows, i):
        low_one[rows] = dg(low_two[rows], matrix(OUT), 1, 1).astype(BF)

    tile_loop(back_out, 2 * QB)
    if exchanged:
        ex.gather_sent(OUT)
    for half in range(2):
        lanes = slice(HALF * half, HALF * half + HALF)
        matrix_store(OUT, half, dg(mixed[:, lanes], low_two[...], 0, 0))
    copies[4].wait()
    start_copy(0, tokens, x_in)

    flows = [UP, UP + 1, UP + 2, UP + 3, DOWN, DOWN + 1, DOWN + 2, DOWN + 3, OUT, 0, 1, 2]
    progress = {}

    def advance(limit):
        if not exchanged:
            return
        moved = 0
        for unit in flows:
            if unit in progress and progress[unit] <= 5 and moved < limit:
                ex.sum_step(unit, progress[unit])
                progress[unit] += 1
                moved += 1

    if exchanged:
        ex.sum_start(OUT)
        progress.update({unit: 2 for unit in flows[:9]})

    for unit in range(3):

        def pair_back(half, carry, unit=unit):
            backward_pair(unit, half, qkv, mixed, low_one, lse, masks, key_acc, value_acc)
            return carry

        advance(3)
        lax.fori_loop(0, 2, pair_back, 0)
        advance(3)
        base = WIDTH * unit

        def back_qkv(rows, i, unit=unit, base=base):
            back = dg(qkv[rows, base : base + WIDTH], matrix(unit), 1, 1)
            if unit == 0:
                acc_one[rows] = back
            else:
                acc_one[rows] += back

        tile_loop(back_qkv, 2 * QB)
        for part, row in ((0, 0), (2, WIDTH)):
            grads = tokens_sum(qkv[:, base + 256 * part : base + 256 * part + 256])
            svec[2:3, row + 256 * unit : row + 256 * unit + 256] = grads
        if exchanged:
            ex.gather_sent(unit)
        for half in range(2):
            lanes = slice(HALF * half, HALF * half + HALF)
            matrix_store(unit, half, dg(normed_one[:, lanes], qkv[:, base : base + WIDTH], 0, 0))
        if exchanged:
            ex.sum_start(unit)
            progress[unit] = 2

    copies[0].wait()

    def back_one(rows, i):
        normed, scale = norm_stats(x_in[rows].astype(F32))
        grad = acc_one[rows]
        acc_two[rows] += norm_back(grad, fv(0), normed, scale)
        for row, part in ((0, grad * normed), (1, grad)):
            svec[row : row + 1, 0:WIDTH] += tokens_sum(part)

    tile_loop(back_one)
    start_copy(5, acc_two, input_grad)
    if exchanged:
        rows_to_pages(svec, ex.vec_pages.reshape(32, VEC_ROWS, 128), 32)
        for step in range(1, 6):
            ex.sum_vectors(step)
        while any(step <= 5 for step in progress.values()):
            advance(3)
        for key in list(ex.waits):
            if key[0] in ("s1", "s1d", "s2", "s3", "s4"):
                ex.sent(key)
    else:
        vectors_out[...] = svec[...]
        start_copy(6, weights, weights_out)
        start_copy(7, down, down_out)
        copies[6].wait()
        copies[7].wait()
    copies[5].wait()


def run_block(mesh_shape, exchanged, tokens, cotangent, documents, *weights):
    length, width = tokens.shape
    depth = mesh_shape["fsdp"] // 2
    vmem = pltpu.VMEM
    whole = pl.BlockSpec(memory_space=pltpu.VMEM)
    far = pl.BlockSpec(memory_space=pl.ANY)
    blocks = len(mask_blocks(length))
    rows = [jax.ShapeDtypeStruct((length, WIDTH), F32)] * 2
    if exchanged:
        shard = weights[0].shape[1]
        in_specs = [far, far, whole, far, far]
        out_shape = rows + [
            jax.ShapeDtypeStruct((shard, 3 * WIDTH), F32),
            jax.ShapeDtypeStruct((shard, WIDTH), F32),
            jax.ShapeDtypeStruct((shard, 4 * WIDTH), F32),
            jax.ShapeDtypeStruct((4 * shard, WIDTH), F32),
            jax.ShapeDtypeStruct((VEC_ROWS, 128), F32),
        ]
        out_specs = [far, far] + [whole] * 5
        places = (2, 2, depth, 2)
        held = [vmem((DOWN, *places, shard, WIDTH), BF), vmem((*places, 4, shard, WIDTH), BF)]
    else:
        in_specs = [far, far, whole, far, far, whole]
        out_shape = rows + [
            jax.ShapeDtypeStruct((DOWN, WIDTH, WIDTH), BF),
            jax.ShapeDtypeStruct((4 * WIDTH, WIDTH), BF),
            jax.ShapeDtypeStruct((VEC_ROWS, 4 * WIDTH), F32),
        ]
        out_specs = [far, far, far, far, whole]
        held = [vmem((DOWN, WIDTH, WIDTH), BF), vmem((4 * WIDTH, WIDTH), BF)]
    low, full = vmem((length, WIDTH), BF), vmem((length, WIDTH), F32)
    scratch = held + [
        low,
        low,
        vmem((length, 3 * WIDTH), BF),
        low,
        vmem((6, 8, length), F32),
        vmem((blocks, QB, QB), F32),
        full,
        low,
        full,
        full,
        low,
        low,
        vmem((length, 128), F32),
        vmem((length, 128), F32),
        vmem((VEC_ROWS, 4 * WIDTH), F32),
        vmem((VEC_ROWS, 4 * WIDTH), F32),
        pltpu.SemaphoreType.DMA((8,)),
    ]
    if exchanged:
        dma = pltpu.SemaphoreType.DMA
        scratch += [
            vmem((2, 2, depth, 2, VEC_ROWS, 128), F32),
            vmem((4, depth, 2, VEC_ROWS, 128), F32),
            vmem((DOWN, 2, depth, 2, shard, WIDTH), BF),
            vmem((2, depth, 2, 4, shard, WIDTH), BF),
            vmem((UNITS, 2, depth, 2, shard, HALF), BF),
            vmem((UNITS, 2, depth, shard, HALF), BF),
            vmem((UNITS, depth - 1, shard, WIDTH), BF),
            dma((10 * UNITS,)),
            dma((10 * UNITS,)),
            dma((10 * UNITS + 2,)),
            dma((10 * UNITS + 2,)),
            dma((16,)),
            dma((16,)),
            dma((UNITS + 1,)),
        ]
    params = dict(vmem_limit_bytes=VMEM_BYTES)
    if exchanged:
        params.update(collective_id=0, has_side_effects=True)
    return pl.pallas_call(
        functools.partial(block_kernel, mesh_shape, exchanged),
        out_shape=out_shape,
        in_specs=in_specs,
        out_specs=out_specs,
        scratch_shapes=scratch,
        compiler_params=pltpu.CompilerParams(**params),
        name="block",
    )(tokens, cotangent, documents, *weights)


def local(mesh_shape, tokens, cotangent, document_ids, source_layer, *stacks):
    (attngain, attnshift, qkvmatrix, qvoffset, outmatrix, outoffset) = stacks[:6]
    (mlpgain, mlpshift, upmatrix, upoffset, downmatrix, downoffset) = stacks[6:]
    vectors = (attngain, attnshift, qvoffset, outoffset, mlpgain, mlpshift, upoffset, downoffset)
    matrices = (qkvmatrix, outmatrix, upmatrix, downmatrix)
    rows_seq, length, width = tokens.shape
    shard = qkvmatrix.shape[1]
    shards = WIDTH // shard
    x_rows, c_rows = tokens.reshape(length, width), cotangent.reshape(length, width)
    axes = ("dp", "fsdp")
    exchanged = mesh_shape["dp"] == 4 and mesh_shape["fsdp"] == 8 and shard % 8 == 0
    if exchanged:
        units, page = pack_layer(source_layer, vectors, matrices)
        result, input_grad, qkv, out, up, down, page = run_block(
            mesh_shape, True, x_rows, c_rows, document_ids, units, page
        )
        pieces = [page[r, 0 : shard * s] for r, s in enumerate(VEC_SIZES)]
    else:
        pick = lambda stack: lax.dynamic_index_in_dim(stack, source_layer, 0, keepdims=False)
        gather = lambda part: lax.all_gather(part, axes, axis=0, tiled=True)
        scatter = lambda part: lax.psum_scatter(part, axes, scatter_dimension=0, tiled=True)
        qkv, out, up, down = [gather(pick(m)) for m in matrices]
        thirds = qkv.reshape(WIDTH, 3, 3, 256).transpose(2, 0, 1, 3).reshape(3, WIDTH, WIDTH)
        quarters = up.reshape(WIDTH, 4, WIDTH).transpose(1, 0, 2)
        weights = jnp.concatenate([thirds, out[None], quarters], 0)
        rows = [gather(pick(v)).astype(F32) for v in vectors]
        table = jnp.stack([jnp.pad(r, (0, 4 * WIDTH - r.shape[0])) for r in rows])
        result, input_grad, weights, down, table = run_block(
            mesh_shape, False, x_rows, c_rows, document_ids, weights, down, table
        )
        weights = weights.astype(F32)
        qkv = weights[0:3].reshape(3, WIDTH, 3, 256).transpose(1, 2, 0, 3).reshape(WIDTH, -1)
        up = weights[UP:DOWN].transpose(1, 0, 2).reshape(WIDTH, -1)
        qkv, out, up, down = [scatter(m) for m in (qkv, weights[OUT], up, down.astype(F32))]
        pieces = [scatter(table[r, 0 : WIDTH * s]) for r, s in enumerate(VEC_SIZES)]
    gain, shift, qv, outb, mid_gain, mid_shift, upb, downb = pieces
    shape = tokens.shape
    return (
        result.reshape(shape),
        input_grad.reshape(shape),
        gain,
        shift,
        qkv,
        qv,
        out,
        outb,
        mid_gain,
        mid_shift,
        up,
        upb,
        down,
        downb,
    )


def solution(mesh):
    axes = ("dp", "fsdp")
    rows, vector, matrix = P(axes, None, None), P(None, axes), P(None, axes, None)
    return jax.shard_map(
        functools.partial(local, dict(mesh.shape)),
        mesh=mesh,
        in_specs=(
            rows,
            rows,
            P(axes, None),
            P(),
            vector,
            vector,
            matrix,
            vector,
            matrix,
            vector,
            vector,
            vector,
            matrix,
            vector,
            matrix,
            vector,
        ),
        out_specs=(
            rows,
            rows,
            P(axes),
            P(axes),
            P(axes, None),
            P(axes),
            P(axes, None),
            P(axes),
            P(axes),
            P(axes),
            P(axes, None),
            P(axes),
            P(axes, None),
            P(axes),
        ),
        check_vma=False,
    )
```

```python
import functools

import jax
import jax.numpy as jnp
from jax import lax
from jax.experimental import pallas as pl
from jax.experimental.pallas import tpu as pltpu
from jax.sharding import PartitionSpec as P

MESH = pl.DeviceIdType.MESH
F32 = jnp.float32
BF = jnp.bfloat16
EPSILON = 1e-05
NEG_LARGE = -1000000000.0
GELU_COEF = 0.7978845608028654
GELU_CUBIC = 0.044715
WIDTH = 768
HALF = 384
HEAD = 64
QB = 256
VEC_ROWS = 8
VMEM_BYTES = 63 * 2**20
VEC_SIZES = (1, 1, 2, 1, 1, 1, 4, 1)
QKV, OUT, UP, DOWN = 0, 3, 4, 8
UNITS = 12
GATHER_LAGS = ((2, 0), (3, 1), (4, 2))
SUM_LAGS = ((2, 0), (3, 1), (4, 2), (5, 4))


def dg(left, right, left_dim, right_dim):
    return lax.dot_general(
        left, right, (((left_dim,), (right_dim,)), ((), ())), preferred_element_type=F32
    )


def mm(left, right):
    return jnp.dot(left, right, preferred_element_type=F32)


def regroup(rows, back):
    to = lax.broadcasted_iota(jnp.int32, (HALF, HALF), 1).astype(F32)
    source = lax.broadcasted_iota(jnp.int32, (HALF, HALF), 0).astype(F32)
    if back:
        to, source = source, to
    high = jnp.floor((to + 0.5) * (1 / (4 * rows)))
    rest = to - 4 * rows * high
    middle = jnp.floor((rest + 0.5) * (1 / rows))
    return source == 4 * rows * middle + rows * high + (rest - rows * middle)


def pack_kernel(layer_ref, *refs):
    vec_in, (qkv, out, up, down), units, vec_out = refs[:8], refs[8:12], refs[12], refs[13]
    layer = layer_ref[0]
    for t in range(3):
        for part in range(3):
            units[t, :, 256 * part : 256 * part + 256] = qkv[
                0, :, WIDTH * part + 256 * t : WIDTH * part + 256 * t + 256
            ]
    units[OUT] = out[0]
    rows = units.shape[1]
    shards = WIDTH // rows
    wide = up[0].astype(F32)
    groups = [wide[:, HALF * g : HALF * g + HALF] for g in range(shards // 4)]
    moved = mm(jnp.concatenate(groups, 0).astype(BF), regroup(rows, False).astype(BF))
    for j in range(4):
        lanes = slice(4 * rows * j, 4 * rows * j + 4 * rows)
        pieces = [moved[rows * g : rows * g + rows, lanes] for g in range(shards // 4)]
        units[UP + j] = jnp.concatenate(pieces, 1).astype(BF)
    wide = down[0].astype(F32)
    for j in range(4):
        units[DOWN + j] = wide[rows * j : rows * j + rows].astype(BF)
    vec_out[...] = jnp.zeros_like(vec_out)
    for r, ref in enumerate(vec_in):
        stack = ref[...].astype(F32)
        index = lax.broadcasted_iota(jnp.int32, stack.shape, 0)
        row = jnp.sum(jnp.where(index == layer, stack, 0.0), axis=0, keepdims=True)
        vec_out[r : r + 1, 0 : stack.shape[1]] = row


def pack_layer(layer, vectors, matrices):
    rows = matrices[0].shape[1]
    whole = [pl.BlockSpec(v.shape, lambda i, s: (0, 0)) for v in vectors]
    picked = [
        pl.BlockSpec((1,) + m.shape[1:], lambda i, s: (s[0], 0, 0)) for m in matrices
    ]
    return pl.pallas_call(
        pack_kernel,
        grid_spec=pltpu.PrefetchScalarGridSpec(
            num_scalar_prefetch=1,
            grid=(1,),
            in_specs=whole + picked,
            out_specs=[
                pl.BlockSpec((UNITS, rows, WIDTH), lambda i, s: (0, 0, 0)),
                pl.BlockSpec((VEC_ROWS, 128), lambda i, s: (0, 0)),
            ],
        ),
        out_shape=[
            jax.ShapeDtypeStruct((UNITS, rows, WIDTH), BF),
            jax.ShapeDtypeStruct((VEC_ROWS, 128), F32),
        ],
        name="pick_layer",
    )(layer.reshape(1), *vectors, *matrices)


def vector_parts(shards):
    base = WIDTH // shards
    parts = {}
    for r, size in enumerate(VEC_SIZES):
        for j in range(4 if size == 4 else 1):
            width = base * (1 if size == 4 else size)
            parts.setdefault(width, []).append((r, base * j, WIDTH * j))
    return parts


def page_maps(shards, width):
    total = shards * width
    col = lax.broadcasted_iota(jnp.int32, (128, total), 1).astype(F32)
    place = lax.broadcasted_iota(jnp.int32, (128, total), 0).astype(F32)
    one_hot = (col - jnp.floor((col + 0.5) * (1 / width)) * width) == place
    col_s = lax.broadcasted_iota(jnp.int32, (shards, total), 1)
    first = lax.broadcasted_iota(jnp.int32, (shards, total), 0) * width
    return one_hot, (col_s >= first) & (col_s < first + width)


def pages_to_rows(pages, fvec, shards):
    for width, parts in vector_parts(shards).items():
        one_hot, mine = page_maps(shards, width)
        one_hot = one_hot.astype(BF)
        for r, lane, start in parts:
            page = pages[:, r, :]
            if lane:
                page = pltpu.roll(page, 128 - lane, 1)
            spread = mm(page.astype(BF), one_hot)
            fvec[r : r + 1, start : start + shards * width] = jnp.sum(
                jnp.where(mine, spread, 0.0), axis=0, keepdims=True
            )


def rows_to_pages(svec, pages, shards):
    for width, parts in vector_parts(shards).items():
        one_hot, mine = page_maps(shards, width)
        one_hot = one_hot.astype(BF)
        for r, lane, start in parts:
            spread = jnp.where(mine, svec[r : r + 1, start : start + shards * width], 0.0)
            high = spread.astype(BF)
            low = (spread - high.astype(F32)).astype(BF)
            page = dg(high, one_hot, 1, 1) + dg(low, one_hot, 1, 1)
            if lane:
                pages[:, r, :] = pages[:, r, :] + pltpu.roll(page, lane, 1)
            else:
                pages[:, r, :] = page


def norm_stats(values):
    mean = jnp.mean(values, axis=-1, keepdims=True)
    centred = values - mean
    spread = jnp.mean(centred * centred, axis=-1, keepdims=True)
    scale = lax.rsqrt(spread + EPSILON)
    return centred * scale, scale


def norm_back(grad, gain, normed, scale):
    scaled = grad * gain
    mean_one = jnp.mean(scaled, axis=-1, keepdims=True)
    mean_two = jnp.mean(scaled * normed, axis=-1, keepdims=True)
    return scale * (scaled - mean_one - normed * mean_two)


def key_ranges(length):
    reach = length // 2
    return [(max(0, i * QB - reach), (i + 1) * QB) for i in range(length // QB)]


def mask_blocks(length):
    blocks = {}
    for i, (lo, hi) in enumerate(key_ranges(length)):
        for key in range(lo, hi, QB):
            blocks[i, key // QB] = len(blocks)
    return blocks


def build_masks(doc_ref, masks, transposed):
    length = doc_ref.shape[1]
    row = doc_ref[...].astype(F32)
    for (i, b), at in mask_blocks(length).items():
        queries = row[:, i * QB : (i + 1) * QB]
        keys = row[:, b * QB : (b + 1) * QB]
        along, down = (queries, keys) if transposed else (keys, queries)
        down = jnp.transpose(jnp.broadcast_to(down, (128, QB)))
        down = jnp.concatenate([down, down], 1)
        q_dim = 1 if transposed else 0
        q_pos = lax.broadcasted_iota(jnp.int32, (QB, QB), q_dim) + i * QB
        k_pos = lax.broadcasted_iota(jnp.int32, (QB, QB), 1 - q_dim) + b * QB
        masks[at] = jnp.where((k_pos <= q_pos) & (down == along), 0.0, NEG_LARGE)


def head_lanes(values, head, other=0.0):
    lane = lax.broadcasted_iota(jnp.int32, values.shape, 1)
    keep = lane >= HEAD if head else lane < HEAD
    return jnp.where(keep, values, jnp.full(values.shape, other, values.dtype))


def pair_lanes(unit, half):
    start = [unit * WIDTH + 256 * part for part in range(3)]
    return [pl.ds(pl.multiple_of(s + 128 * half, 128), 128) for s in start]


def forward_pair(unit, half, qkv, mixed, lse, masks):
    length = qkv.shape[0]
    lanes_q, lanes_k, lanes_v = pair_lanes(unit, half)
    ranges, blocks = key_ranges(length), mask_blocks(length)
    pair = 2 * unit + half
    lanes_o = pl.ds(pl.multiple_of(pair * 128, 128), 128)
    steps = [(i, h) for i in range(len(ranges)) for h in range(2)]

    def scores(step):
        i, h = step
        lo, hi = ranges[i]
        rows = slice(i * QB, (i + 1) * QB)
        raw = dg(head_lanes(qkv[rows, lanes_q], h), qkv[lo:hi, lanes_k], 1, 1)
        mask = [masks[blocks[i, b]] for b in range(lo // QB, hi // QB)]
        return raw + jnp.concatenate(mask, 1)

    def finish(step, score):
        i, h = step
        lo, hi = ranges[i]
        top = jnp.max(score, axis=1, keepdims=True)
        soft = jnp.exp(score - top).astype(BF)
        return mm(soft, head_lanes(qkv[lo:hi, lanes_v], h, 1.0)), top

    current, done = scores(steps[0]), {}
    for n, step in enumerate(steps):
        following = scores(steps[n + 1]) if n + 1 < len(steps) else None
        done[step] = finish(step, current)
        current = following
        i, h = step
        if h == 1:
            (acc0, top0), (acc1, top1) = done.pop((i, 0)), done.pop((i, 1))
            rows = slice(i * QB, (i + 1) * QB)
            first = lax.broadcasted_iota(jnp.int32, acc0.shape, 1) < HEAD
            total = pltpu.roll(jnp.where(first, acc1, acc0), HEAD, 1)
            mixed[rows, lanes_o] = (jnp.where(first, acc0, acc1) / total).astype(BF)
            logs = jnp.transpose(jnp.where(first, top0, top1) + jnp.log(total))
            lse[pair, 0:1, rows] = logs[0:1]
            lse[pair, 1:2, rows] = logs[HEAD : HEAD + 1]


def backward_pair(unit, half, qkv, mixed, mixed_grad, lse, masks, key_acc, value_acc):
    length = qkv.shape[0]
    lanes_q, lanes_k, lanes_v = pair_lanes(unit, half)
    ranges, blocks = key_ranges(length), mask_blocks(length)
    pair = 2 * unit + half
    lanes_o = pl.ds(pl.multiple_of(pair * 128, 128), 128)
    keys_t = jnp.transpose(qkv[:, lanes_k])
    steps = [(i, h) for i in range(len(ranges)) for h in range(2)]
    products = {}

    def start(step):
        i, h = step
        lo, hi = ranges[i]
        rows = slice(i * QB, (i + 1) * QB)
        query = head_lanes(qkv[rows, lanes_q], h)
        grad = head_lanes(mixed_grad[rows, lanes_o], h)
        mask = [masks[blocks[i, b]] for b in range(lo // QB, hi // QB)]
        score = dg(qkv[lo:hi, lanes_k], query, 1, 1) + jnp.concatenate(mask, 0)
        return score, dg(qkv[lo:hi, lanes_v], grad, 1, 1), query, grad

    def finish(step, started):
        i, h = step
        lo, hi = ranges[i]
        rows = slice(i * QB, (i + 1) * QB)
        score, soft_grad, query, grad = started
        if h == 0:
            products[i] = jnp.transpose(
                mixed_grad[rows, lanes_o].astype(F32) * mixed[rows, lanes_o].astype(F32)
            )
        soft = jnp.exp(score - lse[pair, h : h + 1, rows])
        centre = jnp.sum(products[i][HEAD * h : HEAD * h + HEAD], axis=0, keepdims=True)
        score_grad = (soft * (soft_grad - centre)).astype(BF)
        soft = soft.astype(BF)
        return (
            mm(keys_t[HEAD * h : HEAD * h + HEAD, lo:hi], score_grad),
            mm(score_grad, query),
            mm(soft, grad),
        )

    current, done = start(steps[0]), {}
    for n, step in enumerate(steps):
        following = start(steps[n + 1]) if n + 1 < len(steps) else None
        done[step] = finish(step, current)
        current = following
        i, h = step
        if h == 1:
            (q0, k0, v0), (q1, k1, v1) = done.pop((i, 0)), done.pop((i, 1))
            rows = slice(i * QB, (i + 1) * QB)
            lo, hi = ranges[i]
            query_grad = jnp.transpose(jnp.concatenate([q0, q1], 0))
            qkv[rows, lanes_q] = (query_grad * HEAD**-0.5).astype(BF)
            keys, values, old = k0 + k1, v0 + v1, hi - QB - lo
            if old:
                key_acc[lo : lo + old] += keys[:old]
                value_acc[lo : lo + old] += values[:old]
            key_acc[hi - QB : hi] = keys[old:]
            value_acc[hi - QB : hi] = values[old:]
    qkv[:, lanes_k] = key_acc[...].astype(BF)
    qkv[:, lanes_v] = value_acc[...].astype(BF)


def staggered(units, lags):
    last = max(lag for _, lag in lags)
    return [
        (units[k - lag], step)
        for k in range(len(units) + last)
        for step, lag in lags
        if 0 <= k - lag < len(units)
    ]


class Exchange:
    def __init__(self, mesh_shape, weights, shards, refs):
        self.depth = mesh_shape["fsdp"] // 2
        self.weights, self.shards = weights, shards
        self.__dict__.update(refs)
        dp, fsdp = lax.axis_index("dp"), lax.axis_index("fsdp")
        self.y, self.c = dp // 2, dp % 2
        self.z, self.x = fsdp // 2, fsdp % 2
        self.waits = {}
        self.flips = [(b // 4, b // 2 % 2, b % 2) for b in range(1, 8)]

    def device(self, y=None, c=None, z=None, x=None):
        y, c = self.y if y is None else y, self.c if c is None else c
        z, x = self.z if z is None else z, self.x if x is None else x
        return (y * 2 + c, z * 2 + x)

    def flipped(self, flip):
        own = (self.y, self.c, self.x)
        return [1 - a if f else a for a, f in zip(own, flip, strict=True)]

    def peers(self):
        far = [self.device(z=lax.rem(self.z + d, self.depth)) for d in range(1, self.depth)]
        near = [self.flipped(flip) for flip in self.flips]
        return far + [self.device(y=y, c=c, x=x) for y, c, x in near]

    def barrier(self):
        barrier = pltpu.get_barrier_semaphore()
        peers = self.peers()
        for peer in peers:
            pl.semaphore_signal(barrier, inc=1, device_id=peer, device_id_type=MESH)
        pl.semaphore_wait(barrier, len(peers))

    def at(self, unit, y, c, z, x, lanes=slice(None)):
        return self.weights.at[unit, y, c, z, x, :, lanes]

    def send(self, key, src, dst, sems, slot, device):
        copy = pltpu.make_async_remote_copy(
            src_ref=src,
            dst_ref=dst,
            send_sem=sems[0].at[slot],
            recv_sem=sems[1].at[slot],
            device_id=device,
            device_id_type=MESH,
        )
        copy.start()
        self.waits.setdefault(key, []).append(copy)

    def received(self, key):
        for copy in self.waits[key]:
            copy.wait_recv()

    def sent(self, *keys):
        for key in keys:
            for copy in self.waits.pop(key):
                copy.wait_send()

    def gather_start(self, unit):
        for d in range(1, self.depth):
            there = self.device(z=lax.rem(self.z + d, self.depth))
            place = self.at(unit, self.y, self.c, self.z, self.x)
            self.send(("g1", unit), self.shards.at[unit], place, self.gather_sems, 10 * unit + d, there)
        place = self.at(unit, self.y, self.c, self.z, self.x)
        local = pltpu.make_async_copy(self.shards.at[unit], place, self.local_sems.at[unit])
        local.start()
        self.waits["local", unit] = local

    def gather_step(self, unit, step):
        y, c, z, x = self.y, self.c, self.z, self.x
        low, high, every = slice(0, HALF), slice(HALF, WIDTH), slice(None)
        sems, base = self.gather_sems, 10 * unit
        to_x, to_y, to_c = self.device(x=1 - x), self.device(y=1 - y), self.device(c=1 - c)
        if step == 2:
            self.waits["local", unit].wait()
            self.received(("g1", unit))
            column = lambda lanes: self.at(unit, y, c, every, x, lanes)
            self.send(("g2", unit), column(low), column(low), sems, base + 4, to_x)
            self.send(("g2", unit), column(high), column(high), sems, base + 5, to_y)
        elif step == 3:
            self.received(("g2", unit))
            one = self.at(unit, y, c, every, every, low)
            two = self.at(unit, every, c, every, x, high)
            self.send(("g3", unit), one, one, sems, base + 6, to_y)
            self.send(("g3", unit), two, two, sems, base + 7, to_x)
        elif step == 4:
            self.received(("g3", unit))
            core = self.at(unit, every, c, every, every)
            self.send(("g4", unit), core, core, sems, base + 8, to_c)

    def gathered(self, unit):
        self.received(("g4", unit))

    def gather_sent(self, unit):
        self.sent(*[(g, unit) for g in ("g1", "g2", "g3", "g4")])

    def gather_vectors(self, step):
        y, c, z, x = self.y, self.c, self.z, self.x
        pages, sems = self.vec_pages, self.vec_sems
        if step == 1:
            for d in range(1, self.depth):
                there = self.device(z=lax.rem(z + d, self.depth))
                self.send("v1", self.vec_shard, pages.at[y, c, z, x], sems, d, there)
            local = pltpu.make_async_copy(self.vec_shard, pages.at[y, c, z, x], self.local_sems.at[UNITS])
            local.start()
            self.waits["vlocal"] = local
        elif step == 2:
            self.waits["vlocal"].wait()
            self.received("v1")
            part = pages.at[y, c, :, x]
            for k, flip in enumerate(self.flips):
                yy, cc, xx = self.flipped(flip)
                self.send("v2", part, part, sems, 10 + k, self.device(y=yy, c=cc, x=xx))
        else:
            self.received("v2")
            self.sent("v1", "v2")

    def sum_sent(self, unit):
        self.sent(*[(s, unit) for s in ("s1", "s2", "s3", "s4")])

    def add(self, place, other):
        place[...] = (place[...].astype(F32) + other[...].astype(F32)).astype(BF)

    def slot(self, unit):
        return UP + unit if unit < OUT else unit

    def sum_start(self, unit):
        place, unit = unit, self.slot(unit)
        core = self.at(unit, slice(None), 1 - self.c, slice(None), slice(None))
        self.send(("s1", place), core, self.from_core.at[place], self.sum_sems, 10 * place, self.device(c=1 - self.c))

    def sum_step(self, unit, step):
        y, c, z, x = self.y, self.c, self.z, self.x
        low, high, every = slice(0, HALF), slice(HALF, WIDTH), slice(None)
        sems, base = self.sum_sems, 10 * unit
        to_x, to_y = self.device(x=1 - x), self.device(y=1 - y)
        place, unit = unit, self.slot(unit)
        if step == 2:
            self.received(("s1", place))
            for half in range(2):
                self.add(self.weights.at[unit, half, c], self.from_core.at[place, half])
            self.send(("s2", place), self.at(unit, 1 - y, c, every, every, low), self.from_two.at[place, 0], sems, base + 1, to_y)
            for half in range(2):
                self.send(("s2", place), self.at(unit, half, c, every, 1 - x, high), self.from_two.at[place, 1, :, half], sems, base + 2 + half, to_x)
        elif step == 3:
            self.received(("s2", place))
            for k in range(self.depth):
                for xx in range(2):
                    self.add(self.at(unit, y, c, k, xx, low), self.from_two.at[place, 0, k, xx])
                for half in range(2):
                    self.add(self.at(unit, half, c, k, x, high), self.from_two.at[place, 1, k, half])
            self.send(("s3", place), self.at(unit, y, c, every, 1 - x, low), self.from_three.at[place, 0], sems, base + 4, to_x)
            self.send(("s3", place), self.at(unit, 1 - y, c, every, x, high), self.from_three.at[place, 1], sems, base + 5, to_y)
        elif step == 4:
            self.received(("s3", place))
            for k in range(self.depth):
                self.add(self.at(unit, y, c, k, x, low), self.from_three.at[place, 0, k])
                self.add(self.at(unit, y, c, k, x, high), self.from_three.at[place, 1, k])
            for d in range(1, self.depth):
                zz = lax.rem(z + d, self.depth)
                self.send(("s4", place), self.at(unit, y, c, zz, x), self.from_four.at[place, d - 1], sems, base + 5 + d, self.device(z=zz))
        elif step == 5:
            self.received(("s4", place))
            total = self.at(unit, y, c, z, x)[...].astype(F32)
            for d in range(self.depth - 1):
                total += self.from_four[place, d].astype(F32)
            rows = total.shape[0]
            if place < OUT:
                for part in range(3):
                    start = WIDTH * part + 256 * place
                    self.qkv_sum[:, start : start + 256] = total[:, 256 * part : 256 * part + 256]
            elif place == OUT:
                self.out_sum[...] = total
            elif place < DOWN:
                self.up_sum[place - UP] = total
            else:
                start = rows * (place - DOWN)
                self.down_sum[start : start + rows] = total

    def sum_vectors(self, step):
        y, c, z, x = self.y, self.c, self.z, self.x
        pages, sems, landing = self.vec_pages, self.vec_sems, self.vec_landing
        if step == 1:
            for k, flip in enumerate(self.flips):
                yy, cc, xx = self.flipped(flip)
                self.send("w1", pages.at[yy, cc, :, xx], landing.at[k], sems, 20 + k, self.device(y=yy, c=cc, x=xx))
        elif step == 2:
            self.received("w1")
            for k in range(self.depth):
                total = pages[y, c, k, x]
                for j in range(7):
                    total = total + landing[j, k]
                pages[y, c, k, x] = total
            for d in range(1, self.depth):
                zz = lax.rem(z + d, self.depth)
                self.send("w2", pages.at[y, c, zz, x], landing.at[7, d], sems, 30 + d, self.device(z=zz))
        else:
            self.received("w2")
            total = pages[y, c, z, x]
            for d in range(1, self.depth):
                total = total + landing[7, d]
            self.vec_sum[...] = total
            self.sent("w1", "w2")


def block_kernel(mesh_shape, exchanged, *refs):
    refs = list(refs)
    take = lambda n: [refs.pop(0) for _ in range(n)]
    tokens, cotangent, documents = take(3)
    if exchanged:
        shards, vec_shard = take(2)
    else:
        weights_in, vectors_in = take(2)
    result, input_grad = take(2)
    if exchanged:
        qkv_sum, out_sum, up_sum, down_sum, vec_sum = take(5)
    else:
        weights_out, vectors_out = take(2)
    (weights, cot, normed_one, qkv, mixed, lse, masks, residual, normed_two) = take(9)
    (acc_one, acc_two, low_one, low_two, fvec, svec, io_sems) = take(7)
    x_in = low_two
    key_acc, value_acc = residual.at[:, 0:128], residual.at[:, 128:256]
    length = x_in.shape[0]
    tiles = length // QB

    ex = None
    if exchanged:
        names = ("vec_pages", "vec_landing", "from_core", "from_two", "from_three", "from_four")
        extra = dict(zip(names, take(len(names))))
        gs, gr, ss, sr, vs, vr, local = take(7)
        extra.update(gather_sems=(gs, gr), sum_sems=(ss, sr), vec_sems=(vs, vr), local_sems=local)
        extra.update(vec_shard=vec_shard, qkv_sum=qkv_sum, out_sum=out_sum, up_sum=up_sum, down_sum=down_sum, vec_sum=vec_sum)
        ex = Exchange(mesh_shape, weights, shards, extra)

    def matrix_rows(unit, half):
        if exchanged:
            return weights[unit, half].reshape(HALF, WIDTH)
        return weights[unit, HALF * half : HALF * half + HALF]

    def matrix(unit, start=0, width=WIDTH):
        if exchanged:
            return weights[unit, :, :, :, :, :, start : start + width].reshape(WIDTH, width)
        return weights[unit, :, start : start + width]

    def keep_matrix(unit):
        normed_two[0:WIDTH] = weights[unit]

    def kept(unit):
        return matrix(unit) if exchanged else normed_two[0:WIDTH]

    def matrix_store(unit, half, values):
        if exchanged:
            weights[unit, half] = values.astype(BF).reshape(weights.shape[2:])
        else:
            weights[unit, HALF * half : HALF * half + HALF] = values.astype(BF)

    def tile_loop(body, size=QB):
        def step(i, carry):
            body(pl.ds(pl.multiple_of(i * size, size), size), i)
            return carry

        lax.fori_loop(0, length // size, step, 0)

    def fv(row, size=1):
        return fvec[row : row + 1, 0 : WIDTH * size]

    copies = {}

    def start_copy(slot, src, dst):
        copies[slot] = pltpu.make_async_copy(src, dst, io_sems.at[slot])
        copies[slot].start()

    start_copy(0, tokens, x_in)
    start_copy(1, cotangent, cot)
    order = [0, 1, 2, OUT, *(unit + j for j in range(4) for unit in (UP, DOWN))]
    if exchanged:
        ex.barrier()
        ex.gather_vectors(1)
        for unit in order:
            ex.gather_start(unit)
    else:
        start_copy(2, weights_in, weights)

    gather_queue = staggered(order, GATHER_LAGS)

    def pump(count=1):
        for _ in range(count if exchanged else 0):
            if gather_queue:
                ex.gather_step(*gather_queue.pop(0))

    def arrived(unit):
        if exchanged:
            while (unit, 4) in gather_queue:
                pump()
            ex.gathered(unit)

    if exchanged:
        build_masks(documents, masks, False)
        ex.gather_vectors(2)
        pump(2)
        ex.gather_vectors(3)
        pages_to_rows(ex.vec_pages.reshape(32, VEC_ROWS, 128), fvec, 32)
    else:
        build_masks(documents, masks, False)
        fvec[...] = vectors_in[...]
    copies[0].wait()

    def norm_one(rows, i):
        normed, _ = norm_stats(x_in[rows].astype(F32))
        normed_one[rows] = (normed * fv(0) + fv(1)).astype(BF)

    tile_loop(norm_one)
    if not exchanged:
        copies[2].wait()

    for unit in range(3):
        arrived(unit)

        def project(rows, i, unit=unit):
            full = mm(normed_one[rows], matrix(unit))
            lanes = slice(256 * unit, 256 * unit + 256)
            bias = fvec[2:3, 256 * unit : 256 * unit + 256]
            query = (full[:, 0:256] + bias).astype(BF).astype(F32) * HEAD**-0.5
            base = WIDTH * unit
            qkv[rows, base : base + 256] = query.astype(BF)
            qkv[rows, base + 256 : base + 512] = full[:, 256:512].astype(BF)
            bias = fvec[2:3, WIDTH + 256 * unit : WIDTH + 256 * unit + 256]
            qkv[rows, base + 512 : base + WIDTH] = (full[:, 512:] + bias).astype(BF)

        tile_loop(project, 2 * QB)
        pump(2)
        for half in range(2):
            forward_pair(unit, half, qkv, mixed, lse, masks)
            pump(2)

    arrived(OUT)
    copies[1].wait()

    def attend(rows, i):
        total = x_in[rows].astype(F32) + (mm(mixed[rows], matrix(OUT)) + fv(3))
        residual[rows] = total
        normed, _ = norm_stats(total)
        normed_two[rows] = (normed * fv(4) + fv(5)).astype(BF)
        acc_one[rows] = total + fv(7)

    tile_loop(attend)
    pump(1)
    build_masks(documents, masks, True)

    def tokens_sum(values):
        return jnp.sum(values.astype(F32), axis=0, keepdims=True)

    flows = [*(unit + j for j in range(4) for unit in (DOWN, UP)), OUT, 0, 1, 2]
    sum_queue = staggered(flows, SUM_LAGS)
    begun = set()

    def advance(count):
        for _ in range(count if exchanged else 0):
            ready = [item for item in sum_queue if item[0] in begun]
            if ready:
                sum_queue.remove(ready[0])
                ex.sum_step(*ready[0])

    def begin(unit):
        if exchanged:
            ex.sum_start(unit)
        begun.add(unit)

    for chunk in range(4):
        arrived(UP + chunk)
        arrived(DOWN + chunk)
        svec[6:7, WIDTH * chunk : WIDTH * chunk + WIDTH] = jnp.zeros((1, WIDTH), F32)
        for half in range(2):
            lanes = slice(HALF * half, HALF * half + HALF)
            wide = slice(WIDTH * chunk + HALF * half, WIDTH * chunk + HALF * half + HALF)

            def hidden(start, chunk=chunk, half=half, wide=wide):
                rows = slice(start, start + QB)
                pre = mm(normed_two[rows], matrix(UP + chunk, HALF * half, HALF)) + fvec[6:7, wide]
                return pre, dg(cot[rows], matrix_rows(DOWN + chunk, half), 1, 1)

            def activate(start, pair, lanes=lanes, wide=wide):
                pre, grad = pair
                square = pre * pre
                bent = jnp.tanh(pre * (GELU_COEF + (GELU_COEF * GELU_CUBIC) * square))
                upper = 0.5 + 0.5 * bent
                slope = upper + (0.5 * pre) * (1.0 - bent * bent) * (
                    GELU_COEF + (3.0 * GELU_COEF * GELU_CUBIC) * square
                )
                rows = slice(start, start + QB)
                low_one[rows, lanes] = (pre * upper).astype(BF)
                back = (grad * slope).astype(BF)
                low_two[rows, lanes] = back
                svec[6:7, wide] += tokens_sum(back)

            current = hidden(0)
            for i in range(tiles):
                following = hidden((i + 1) * QB) if i + 1 < tiles else None
                activate(i * QB, current)
                current = following
            pump(2)
            advance(1)

        def outward(rows, i, chunk=chunk):
            acc_one[rows] += mm(low_one[rows], matrix(DOWN + chunk))
            back = dg(low_two[rows], matrix(UP + chunk), 1, 1)
            if chunk == 0:
                acc_two[rows] = back
            else:
                acc_two[rows] += back

        tile_loop(outward, 2 * QB)
        pump(2)
        advance(1)
        if exchanged:
            ex.gather_sent(UP + chunk)
            ex.gather_sent(DOWN + chunk)
        for half in range(2):
            lanes = slice(HALF * half, HALF * half + HALF)
            matrix_store(DOWN + chunk, half, dg(low_one[:, lanes], cot[...], 0, 0))
        begin(DOWN + chunk)
        pump(2)
        advance(1)
        for half in range(2):
            lanes = slice(HALF * half, HALF * half + HALF)
            matrix_store(UP + chunk, half, dg(normed_two[:, lanes], low_two[...], 0, 0))
        begin(UP + chunk)
        pump(1)

    start_copy(4, acc_one, result)

    for row in (0, 1, 3, 4, 5, 7):
        svec[row : row + 1, 0:WIDTH] = jnp.zeros((1, WIDTH), F32)

    def back_two(rows, i):
        normed, scale = norm_stats(residual[rows])
        grad = acc_two[rows]
        grads = cot[rows].astype(F32)
        total = grads + norm_back(grad, fv(4), normed, scale)
        acc_two[rows] = total
        low = total.astype(BF)
        low_two[rows] = low
        for row, part in ((4, grad * normed), (5, grad), (7, grads), (3, low)):
            svec[row : row + 1, 0:WIDTH] += tokens_sum(part)

    advance(1)
    tile_loop(back_two)
    advance(1)

    def back_out(rows, i):
        low_one[rows] = dg(low_two[rows], matrix(OUT), 1, 1).astype(BF)

    tile_loop(back_out, 2 * QB)
    advance(1)
    if exchanged:
        ex.gather_sent(OUT)
    for half in range(2):
        lanes = slice(HALF * half, HALF * half + HALF)
        matrix_store(OUT, half, dg(mixed[:, lanes], low_two[...], 0, 0))
    copies[4].wait()
    start_copy(0, tokens, x_in)

    begin(OUT)

    for unit in range(3):
        for half in range(2):
            advance(2)
            backward_pair(unit, half, qkv, mixed, low_one, lse, masks, key_acc, value_acc)
        base = WIDTH * unit
        if exchanged:
            while (UP + unit, 5) in sum_queue:
                advance(1)
            ex.sum_sent(UP + unit)
            ex.gather_sent(unit)
        else:
            advance(2)
            keep_matrix(unit)
        for half in range(2):
            lanes = slice(HALF * half, HALF * half + HALF)
            place = ex.slot(unit) if exchanged else unit
            matrix_store(place, half, dg(normed_one[:, lanes], qkv[:, base : base + WIDTH], 0, 0))
        begin(unit)
        advance(2)

        def back_qkv(rows, i, unit=unit, base=base):
            back = dg(qkv[rows, base : base + WIDTH], kept(unit), 1, 1)
            if unit == 0:
                acc_one[rows] = back
            else:
                acc_one[rows] += back

        tile_loop(back_qkv, 2 * QB)
        for part, row in ((0, 0), (2, WIDTH)):
            grads = tokens_sum(qkv[:, base + 256 * part : base + 256 * part + 256])
            svec[2:3, row + 256 * unit : row + 256 * unit + 256] = grads

    copies[0].wait()

    def back_one(rows, i):
        normed, scale = norm_stats(x_in[rows].astype(F32))
        grad = acc_one[rows]
        acc_two[rows] += norm_back(grad, fv(0), normed, scale)
        for row, part in ((0, grad * normed), (1, grad)):
            svec[row : row + 1, 0:WIDTH] += tokens_sum(part)

    advance(1)
    tile_loop(back_one)
    start_copy(5, acc_two, input_grad)
    if exchanged:
        rows_to_pages(svec, ex.vec_pages.reshape(32, VEC_ROWS, 128), 32)
        ex.sum_vectors(1)
        advance(1)
        ex.sum_vectors(2)
        advance(2)
        ex.sum_vectors(3)
        advance(len(sum_queue))
        for unit in (*range(OUT + 1), UP + 3, *range(DOWN, UNITS)):
            ex.sum_sent(unit)
    else:
        vectors_out[...] = svec[...]
        start_copy(6, weights, weights_out)
        copies[6].wait()
    copies[5].wait()


def finish_kernel(*refs):
    page, outs = refs[6], refs[7:]
    outs[0][...] = refs[0][...]
    outs[1][...] = refs[1][...]

    @pl.when(pl.program_id(0) == 0)
    def _():
        for k in (2, 3, 5):
            outs[k][...] = refs[k][...]
        up, rows = refs[4], refs[4].shape[1]
        shards = WIDTH // rows
        groups = [
            jnp.concatenate([up[j, :, 4 * rows * g : 4 * rows * g + 4 * rows] for j in range(4)], 1)
            for g in range(shards // 4)
        ]
        moved = lax.dot_general(
            jnp.concatenate(groups, 0),
            regroup(rows, True).astype(F32),
            (((1,), (0,)), ((), ())),
            preferred_element_type=F32,
            precision=lax.Precision.HIGHEST,
        )
        for g in range(shards // 4):
            outs[4][:, HALF * g : HALF * g + HALF] = moved[rows * g : rows * g + rows]
        for r, dst in enumerate(outs[6:]):
            dst[...] = page[r, 0 : dst.shape[0]]


def finish(rows, sums, page, sizes):
    block = pl.BlockSpec((rows[0].shape[0] // 2, WIDTH), lambda i: (i, 0))
    whole = lambda shape: pl.BlockSpec(shape, lambda i: (0,) * len(shape))
    ins = [block, block] + [whole(a.shape) for a in (*sums, page)]
    qkv, out, up, down = [a.shape for a in sums]
    shapes = [qkv, out, (up[1], 4 * WIDTH), down] + [(n,) for n in sizes]
    outs = [block, block] + [whole(shape) for shape in shapes]
    shapes = [a.shape for a in rows] + shapes
    return pl.pallas_call(
        finish_kernel,
        grid=(2,),
        in_specs=ins,
        out_specs=outs,
        out_shape=[jax.ShapeDtypeStruct(shape, F32) for shape in shapes],
        name="finish",
    )(*rows, *sums, page)


def run_block(mesh_shape, exchanged, tokens, cotangent, documents, *weights):
    length, width = tokens.shape
    depth = mesh_shape["fsdp"] // 2
    vmem = pltpu.VMEM
    whole = pl.BlockSpec(memory_space=pltpu.VMEM)
    far = pl.BlockSpec(memory_space=pl.ANY)
    blocks = len(mask_blocks(length))
    rows = [jax.ShapeDtypeStruct((length, WIDTH), F32)] * 2
    if exchanged:
        shard = weights[0].shape[1]
        in_specs = [far, far, whole, far, far]
        out_shape = rows + [
            jax.ShapeDtypeStruct((shard, 3 * WIDTH), F32),
            jax.ShapeDtypeStruct((shard, WIDTH), F32),
            jax.ShapeDtypeStruct((4, shard, WIDTH), F32),
            jax.ShapeDtypeStruct((4 * shard, WIDTH), F32),
            jax.ShapeDtypeStruct((VEC_ROWS, 128), F32),
        ]
        out_specs = [far, far] + [whole] * 5
        places = (2, 2, depth, 2)
        held = [vmem((UNITS, *places, shard, WIDTH), BF)]
    else:
        in_specs = [far, far, whole, far, whole]
        out_shape = rows + [
            jax.ShapeDtypeStruct((UNITS, WIDTH, WIDTH), BF),
            jax.ShapeDtypeStruct((VEC_ROWS, 4 * WIDTH), F32),
        ]
        out_specs = [far, far, far, whole]
        held = [vmem((UNITS, WIDTH, WIDTH), BF)]
    low, full = vmem((length, WIDTH), BF), vmem((length, WIDTH), F32)
    scratch = held + [
        low,
        low,
        vmem((length, 3 * WIDTH), BF),
        low,
        vmem((6, 8, length), F32),
        vmem((blocks, QB, QB), F32),
        full,
        low,
        full,
        full,
        low,
        low,
        vmem((VEC_ROWS, 4 * WIDTH), F32),
        vmem((VEC_ROWS, 4 * WIDTH), F32),
        pltpu.SemaphoreType.DMA((8,)),
    ]
    if exchanged:
        dma = pltpu.SemaphoreType.DMA
        scratch += [
            vmem((2, 2, depth, 2, VEC_ROWS, 128), F32),
            vmem((8, depth, VEC_ROWS, 128), F32),
            vmem((UNITS, 2, depth, 2, shard, WIDTH), BF),
            vmem((UNITS, 2, depth, 2, shard, HALF), BF),
            vmem((UNITS, 2, depth, shard, HALF), BF),
            vmem((UNITS, depth - 1, shard, WIDTH), BF),
            dma((10 * UNITS,)),
            dma((10 * UNITS,)),
            dma((10 * UNITS,)),
            dma((10 * UNITS,)),
            dma((40,)),
            dma((40,)),
            dma((UNITS + 1,)),
        ]
    params = dict(vmem_limit_bytes=VMEM_BYTES)
    if exchanged:
        params.update(collective_id=0, has_side_effects=True)
    return pl.pallas_call(
        functools.partial(block_kernel, mesh_shape, exchanged),
        out_shape=out_shape,
        in_specs=in_specs,
        out_specs=out_specs,
        scratch_shapes=scratch,
        compiler_params=pltpu.CompilerParams(**params),
        name="block",
    )(tokens, cotangent, documents, *weights)


def local(mesh_shape, tokens, cotangent, document_ids, source_layer, *stacks):
    (attngain, attnshift, qkvmatrix, qvoffset, outmatrix, outoffset) = stacks[:6]
    (mlpgain, mlpshift, upmatrix, upoffset, downmatrix, downoffset) = stacks[6:]
    vectors = (attngain, attnshift, qvoffset, outoffset, mlpgain, mlpshift, upoffset, downoffset)
    matrices = (qkvmatrix, outmatrix, upmatrix, downmatrix)
    rows_seq, length, width = tokens.shape
    shard = qkvmatrix.shape[1]
    shards = WIDTH // shard
    x_rows, c_rows = tokens.reshape(length, width), cotangent.reshape(length, width)
    axes = ("dp", "fsdp")
    exchanged = mesh_shape["dp"] == 4 and mesh_shape["fsdp"] == 8 and shard % 8 == 0
    if exchanged:
        units, page = pack_layer(source_layer, vectors, matrices)
        result, input_grad, qkv, out, up, down, page = run_block(
            mesh_shape, True, x_rows, c_rows, document_ids, units, page
        )
        result, input_grad, qkv, out, up, down, *pieces = finish(
            (result, input_grad), (qkv, out, up, down), page, [shard * s for s in VEC_SIZES]
        )
    else:
        pick = lambda stack: lax.dynamic_index_in_dim(stack, source_layer, 0, keepdims=False)
        gather = lambda part: lax.all_gather(part, axes, axis=0, tiled=True)
        scatter = lambda part: lax.psum_scatter(part, axes, scatter_dimension=0, tiled=True)
        qkv, out, up, down = [gather(pick(m)) for m in matrices]
        thirds = qkv.reshape(WIDTH, 3, 3, 256).transpose(2, 0, 1, 3).reshape(3, WIDTH, WIDTH)
        quarters = up.reshape(WIDTH, 4, WIDTH).transpose(1, 0, 2)
        weights = jnp.concatenate([thirds, out[None], quarters, down.reshape(4, WIDTH, WIDTH)], 0)
        rows = [gather(pick(v)).astype(F32) for v in vectors]
        table = jnp.stack([jnp.pad(r, (0, 4 * WIDTH - r.shape[0])) for r in rows])
        result, input_grad, weights, table = run_block(
            mesh_shape, False, x_rows, c_rows, document_ids, weights, table
        )
        weights = weights.astype(F32)
        qkv = weights[0:3].reshape(3, WIDTH, 3, 256).transpose(1, 2, 0, 3).reshape(WIDTH, -1)
        up = weights[UP:DOWN].transpose(1, 0, 2).reshape(WIDTH, -1)
        down = weights[DOWN:].reshape(4 * WIDTH, WIDTH)
        qkv, out, up, down = [scatter(m) for m in (qkv, weights[OUT], up, down)]
        pieces = [scatter(table[r, 0 : WIDTH * s]) for r, s in enumerate(VEC_SIZES)]
    gain, shift, qv, outb, mid_gain, mid_shift, upb, downb = pieces
    shape = tokens.shape
    return (
        result.reshape(shape),
        input_grad.reshape(shape),
        gain,
        shift,
        qkv,
        qv,
        out,
        outb,
        mid_gain,
        mid_shift,
        up,
        upb,
        down,
        downb,
    )


def solution(mesh):
    axes = ("dp", "fsdp")
    rows, vector, matrix = P(axes, None, None), P(None, axes), P(None, axes, None)
    return jax.shard_map(
        functools.partial(local, dict(mesh.shape)),
        mesh=mesh,
        in_specs=(
            rows,
            rows,
            P(axes, None),
            P(),
            vector,
            vector,
            matrix,
            vector,
            matrix,
            vector,
            vector,
            vector,
            matrix,
            vector,
            matrix,
            vector,
        ),
        out_specs=(
            rows,
            rows,
            P(axes),
            P(axes),
            P(axes, None),
            P(axes),
            P(axes, None),
            P(axes),
            P(axes),
            P(axes),
            P(axes, None),
            P(axes),
            P(axes, None),
            P(axes),
        ),
        check_vma=False,
    )
```

```python
import functools

import jax
import jax.numpy as jnp
from jax import lax
from jax.experimental import pallas as pl
from jax.experimental.pallas import tpu as pltpu
from jax.sharding import PartitionSpec as P

MESH = pl.DeviceIdType.MESH
F32 = jnp.float32
BF = jnp.bfloat16
EPSILON = 1e-05
NEG_LARGE = -1000000000.0
GELU_COEF = 0.7978845608028654
GELU_CUBIC = 0.044715
WIDTH = 768
HALF = 384
HEAD = 64
QB = 256
VEC_ROWS = 8
VMEM_BYTES = 63 * 2**20
VEC_SIZES = (1, 1, 2, 1, 1, 1, 4, 1)
OUT, UNITS = 3, 12


def up(quarter):
    return OUT + 1 + 2 * quarter


def down(quarter):
    return OUT + 2 + 2 * quarter


SCHEDULE = {
    "rows": {
        0: ((0, 0, 2),),
    },
    "att0": {
        0: ((0, 1, 2), (0, 0, 3), (0, 2, 2), (0, 1, 3), (0, 3, 2), (0, 0, 4), (0, 2, 3),),
    },
    "att2": {
        0: ((0, 4, 2),),
        1: ((0, 1, 4), (0, 3, 3), (0, 5, 2),),
        2: ((0, 4, 3),),
        3: ((0, 7, 2),),
        4: ((0, 5, 3), (0, 6, 3), (0, 8, 2),),
        5: ((0, 9, 2),),
    },
    "att1": {
        1: ((0, 2, 4), (0, 6, 2),),
        2: ((0, 3, 4),),
    },
    "attended": {
        0: ((0, 4, 4), (0, 10, 2),),
    },
    "masksT": {
        0: ((0, 7, 3),),
    },
    "ff0": {
        0: ((0, 11, 2), (0, 5, 4),),
        1: ((0, 7, 4), (1, 5, 2), (0, 11, 3), (1, 4, 2),),
    },
    "ff1": {
        1: ((0, 6, 4),),
        3: ((0, 8, 4),),
        4: ((1, 7, 2), (1, 5, 3),),
        5: ((1, 6, 2),),
        6: ((1, 7, 3), (1, 5, 4), (1, 9, 2),),
        7: ((1, 8, 2),),
    },
    "ff3": {
        0: ((0, 8, 3), (0, 9, 3),),
        1: ((0, 9, 4),),
        2: ((0, 11, 4),),
        3: ((1, 4, 4), (1, 6, 3),),
    },
    "ff4": {
        0: ((0, 10, 3),),
        2: ((1, 4, 3),),
        3: ((1, 7, 4), (1, 5, 5),),
    },
    "ff5": {
        1: ((0, 10, 4),),
        3: ((1, 9, 3),),
    },
    "back_two": {
        0: ((1, 11, 2), (1, 8, 3), (1, 10, 2), (1, 4, 5),),
    },
    "back_out": {
        0: ((1, 6, 4), (1, 7, 5),),
    },
    "dWo": {
        0: ((1, 9, 4),),
    },
    "ab0": {
        0: ((1, 11, 3), (1, 3, 2), (1, 8, 4),),
        1: ((1, 10, 3), (1, 6, 5), (1, 9, 5),),
        2: ((1, 3, 3), (1, 0, 2), (1, 8, 5),),
        3: ((1, 10, 4), (1, 11, 5),),
        4: ((1, 0, 3), (1, 1, 2),),
        5: ((1, 10, 5),),
    },
    "ab2": {
        0: ((1, 11, 4),),
        1: ((1, 3, 4),),
        2: ((1, 0, 4), (1, 3, 5),),
    },
    "da1": {
        0: ((1, 1, 3),),
        1: ((1, 2, 2),),
    },
    "back_one": {
        0: ((1, 1, 4), (1, 0, 5),),
    },
    "drain": {
        0: ((1, 2, 3), (1, 1, 5), (1, 2, 4), (1, 2, 5),),
    },
}


def dg(left, right, left_dim, right_dim):
    return lax.dot_general(
        left, right, (((left_dim,), (right_dim,)), ((), ())), preferred_element_type=F32
    )


def mm(left, right):
    return jnp.dot(left, right, preferred_element_type=F32)


def regroup(rows, back):
    to = lax.broadcasted_iota(jnp.int32, (HALF, HALF), 1).astype(F32)
    source = lax.broadcasted_iota(jnp.int32, (HALF, HALF), 0).astype(F32)
    if back:
        to, source = source, to
    high = jnp.floor((to + 0.5) * (1 / (4 * rows)))
    rest = to - 4 * rows * high
    middle = jnp.floor((rest + 0.5) * (1 / rows))
    return source == 4 * rows * middle + rows * high + (rest - rows * middle)


def pack_kernel(layer_ref, *refs):
    vec_in, (qkv, out, up_in, down_in), units, vec_out = refs[:8], refs[8:12], refs[12], refs[13]
    layer = layer_ref[0]
    for t in range(3):
        for part in range(3):
            units[t, :, 256 * part : 256 * part + 256] = qkv[
                0, :, WIDTH * part + 256 * t : WIDTH * part + 256 * t + 256
            ]
    units[OUT] = out[0]
    rows = units.shape[1]
    shards = WIDTH // rows
    wide = up_in[0].astype(F32)
    groups = [wide[:, HALF * g : HALF * g + HALF] for g in range(shards // 4)]
    moved = mm(jnp.concatenate(groups, 0).astype(BF), regroup(rows, False).astype(BF))
    for j in range(4):
        lanes = slice(4 * rows * j, 4 * rows * j + 4 * rows)
        pieces = [moved[rows * g : rows * g + rows, lanes] for g in range(shards // 4)]
        units[up(j)] = jnp.concatenate(pieces, 1).astype(BF)
    wide = down_in[0].astype(F32)
    for j in range(4):
        units[down(j)] = wide[rows * j : rows * j + rows].astype(BF)
    vec_out[...] = jnp.zeros_like(vec_out)
    for r, ref in enumerate(vec_in):
        stack = ref[...].astype(F32)
        index = lax.broadcasted_iota(jnp.int32, stack.shape, 0)
        row = jnp.sum(jnp.where(index == layer, stack, 0.0), axis=0, keepdims=True)
        vec_out[r : r + 1, 0 : stack.shape[1]] = row


def pack_layer(layer, vectors, matrices):
    rows = matrices[0].shape[1]
    whole = [pl.BlockSpec(v.shape, lambda i, s: (0, 0)) for v in vectors]
    picked = [
        pl.BlockSpec((1,) + m.shape[1:], lambda i, s: (s[0], 0, 0)) for m in matrices
    ]
    return pl.pallas_call(
        pack_kernel,
        grid_spec=pltpu.PrefetchScalarGridSpec(
            num_scalar_prefetch=1,
            grid=(1,),
            in_specs=whole + picked,
            out_specs=[
                pl.BlockSpec((UNITS, rows, WIDTH), lambda i, s: (0, 0, 0)),
                pl.BlockSpec((VEC_ROWS, 128), lambda i, s: (0, 0)),
            ],
        ),
        out_shape=[
            jax.ShapeDtypeStruct((UNITS, rows, WIDTH), BF),
            jax.ShapeDtypeStruct((VEC_ROWS, 128), F32),
        ],
        name="pick_layer",
    )(layer.reshape(1), *vectors, *matrices)


def vector_parts(shards):
    base = WIDTH // shards
    parts = {}
    for r, size in enumerate(VEC_SIZES):
        for j in range(4 if size == 4 else 1):
            width = base * (1 if size == 4 else size)
            parts.setdefault(width, []).append((r, base * j, WIDTH * j))
    return parts


def page_maps(shards, width):
    total = shards * width
    col = lax.broadcasted_iota(jnp.int32, (128, total), 1).astype(F32)
    place = lax.broadcasted_iota(jnp.int32, (128, total), 0).astype(F32)
    one_hot = (col - jnp.floor((col + 0.5) * (1 / width)) * width) == place
    col_s = lax.broadcasted_iota(jnp.int32, (shards, total), 1)
    first = lax.broadcasted_iota(jnp.int32, (shards, total), 0) * width
    return one_hot, (col_s >= first) & (col_s < first + width)


def pages_to_rows(pages, fvec, shards):
    for width, parts in vector_parts(shards).items():
        one_hot, mine = page_maps(shards, width)
        one_hot = one_hot.astype(BF)
        for r, lane, start in parts:
            page = pages[:, r, :]
            if lane:
                page = pltpu.roll(page, 128 - lane, 1)
            spread = mm(page.astype(BF), one_hot)
            fvec[r : r + 1, start : start + shards * width] = jnp.sum(
                jnp.where(mine, spread, 0.0), axis=0, keepdims=True
            )


def rows_to_pages(svec, pages, shards):
    for width, parts in vector_parts(shards).items():
        one_hot, mine = page_maps(shards, width)
        one_hot = one_hot.astype(BF)
        for r, lane, start in parts:
            spread = jnp.where(mine, svec[r : r + 1, start : start + shards * width], 0.0)
            high = spread.astype(BF)
            low = (spread - high.astype(F32)).astype(BF)
            page = dg(high, one_hot, 1, 1) + dg(low, one_hot, 1, 1)
            if lane:
                pages[:, r, :] = pages[:, r, :] + pltpu.roll(page, lane, 1)
            else:
                pages[:, r, :] = page


def norm_stats(values):
    mean = jnp.mean(values, axis=-1, keepdims=True)
    centred = values - mean
    spread = jnp.mean(centred * centred, axis=-1, keepdims=True)
    scale = lax.rsqrt(spread + EPSILON)
    return centred * scale, scale


def norm_back(grad, gain, normed, scale):
    scaled = grad * gain
    mean_one = jnp.mean(scaled, axis=-1, keepdims=True)
    mean_two = jnp.mean(scaled * normed, axis=-1, keepdims=True)
    return scale * (scaled - mean_one - normed * mean_two)


def key_ranges(length):
    reach = length // 2
    return [(max(0, i * QB - reach), (i + 1) * QB) for i in range(length // QB)]


def mask_blocks(length):
    blocks = {}
    for i, (lo, hi) in enumerate(key_ranges(length)):
        for key in range(lo, hi, QB):
            blocks[i, key // QB] = len(blocks)
    return blocks


def build_masks(doc_ref, masks, transposed):
    length = doc_ref.shape[1]
    row = doc_ref[...].astype(F32)
    for (i, b), at in mask_blocks(length).items():
        queries = row[:, i * QB : (i + 1) * QB]
        keys = row[:, b * QB : (b + 1) * QB]
        along, down = (queries, keys) if transposed else (keys, queries)
        down = jnp.transpose(jnp.broadcast_to(down, (128, QB)))
        down = jnp.concatenate([down, down], 1)
        q_dim = 1 if transposed else 0
        q_pos = lax.broadcasted_iota(jnp.int32, (QB, QB), q_dim) + i * QB
        k_pos = lax.broadcasted_iota(jnp.int32, (QB, QB), 1 - q_dim) + b * QB
        masks[at] = jnp.where((k_pos <= q_pos) & (down == along), 0.0, NEG_LARGE)


def head_lanes(values, head, other=0.0):
    lane = lax.broadcasted_iota(jnp.int32, values.shape, 1)
    keep = lane >= HEAD if head else lane < HEAD
    return jnp.where(keep, values, jnp.full(values.shape, other, values.dtype))


def pair_lanes(unit, half):
    start = [unit * WIDTH + 256 * part + 128 * half for part in range(3)]
    return [pl.ds(pl.multiple_of(s, 128), 128) for s in start]


def forward_pair(unit, half, qkv, mixed, lse, masks):
    length = qkv.shape[0]
    lanes_q, lanes_k, lanes_v = pair_lanes(unit, half)
    ranges, blocks = key_ranges(length), mask_blocks(length)
    pair = 2 * unit + half
    lanes_o = pl.ds(pl.multiple_of(pair * 128, 128), 128)
    steps = [(i, h) for i in range(len(ranges)) for h in range(2)]

    def scores(step):
        i, h = step
        lo, hi = ranges[i]
        rows = slice(i * QB, (i + 1) * QB)
        raw = dg(head_lanes(qkv[rows, lanes_q], h), qkv[lo:hi, lanes_k], 1, 1)
        mask = [masks[blocks[i, b]] for b in range(lo // QB, hi // QB)]
        return raw + jnp.concatenate(mask, 1)

    def finish(step, score):
        i, h = step
        lo, hi = ranges[i]
        top = jnp.max(score, axis=1, keepdims=True)
        soft = jnp.exp(score - top).astype(BF)
        return mm(soft, head_lanes(qkv[lo:hi, lanes_v], h, 1.0)), top

    current, done = scores(steps[0]), {}
    for n, step in enumerate(steps):
        following = scores(steps[n + 1]) if n + 1 < len(steps) else None
        done[step] = finish(step, current)
        current = following
        i, h = step
        if h == 1:
            (acc0, top0), (acc1, top1) = done.pop((i, 0)), done.pop((i, 1))
            rows = slice(i * QB, (i + 1) * QB)
            first = lax.broadcasted_iota(jnp.int32, acc0.shape, 1) < HEAD
            total = pltpu.roll(jnp.where(first, acc1, acc0), HEAD, 1)
            mixed[rows, lanes_o] = (jnp.where(first, acc0, acc1) / total).astype(BF)
            logs = jnp.transpose(jnp.where(first, top0, top1) + jnp.log(total))
            lse[pair, 0:1, rows] = logs[0:1]
            lse[pair, 1:2, rows] = logs[HEAD : HEAD + 1]


def backward_pair(unit, half, qkv, mixed, mixed_grad, lse, masks, key_acc, value_acc):
    length = qkv.shape[0]
    lanes_q, lanes_k, lanes_v = pair_lanes(unit, half)
    ranges, blocks = key_ranges(length), mask_blocks(length)
    pair = 2 * unit + half
    lanes_o = pl.ds(pl.multiple_of(pair * 128, 128), 128)
    keys_t = jnp.transpose(qkv[:, lanes_k])
    steps = [(i, h) for i in range(len(ranges)) for h in range(2)]
    products = {}

    def start(step):
        i, h = step
        lo, hi = ranges[i]
        rows = slice(i * QB, (i + 1) * QB)
        query = head_lanes(qkv[rows, lanes_q], h)
        grad = head_lanes(mixed_grad[rows, lanes_o], h)
        mask = [masks[blocks[i, b]] for b in range(lo // QB, hi // QB)]
        score = dg(qkv[lo:hi, lanes_k], query, 1, 1) + jnp.concatenate(mask, 0)
        return score, dg(qkv[lo:hi, lanes_v], grad, 1, 1), query, grad

    def finish(step, started):
        i, h = step
        lo, hi = ranges[i]
        rows = slice(i * QB, (i + 1) * QB)
        score, soft_grad, query, grad = started
        if h == 0:
            products[i] = jnp.transpose(
                mixed_grad[rows, lanes_o].astype(F32) * mixed[rows, lanes_o].astype(F32)
            )
        soft = jnp.exp(score - lse[pair, h : h + 1, rows])
        centre = jnp.sum(products[i][HEAD * h : HEAD * h + HEAD], axis=0, keepdims=True)
        score_grad = (soft * (soft_grad - centre)).astype(BF)
        soft = soft.astype(BF)
        return (
            mm(keys_t[HEAD * h : HEAD * h + HEAD, lo:hi], score_grad),
            mm(score_grad, query),
            mm(soft, grad),
        )

    current, done = start(steps[0]), {}
    for n, step in enumerate(steps):
        following = start(steps[n + 1]) if n + 1 < len(steps) else None
        done[step] = finish(step, current)
        current = following
        i, h = step
        if h == 1:
            (q0, k0, v0), (q1, k1, v1) = done.pop((i, 0)), done.pop((i, 1))
            rows = slice(i * QB, (i + 1) * QB)
            lo, hi = ranges[i]
            query_grad = jnp.transpose(jnp.concatenate([q0, q1], 0))
            qkv[rows, lanes_q] = (query_grad * HEAD**-0.5).astype(BF)
            keys, values, old = k0 + k1, v0 + v1, hi - QB - lo
            if old:
                key_acc[lo : lo + old] += keys[:old]
                value_acc[lo : lo + old] += values[:old]
            key_acc[hi - QB : hi] = keys[old:]
            value_acc[hi - QB : hi] = values[old:]
    qkv[:, lanes_k] = key_acc[...].astype(BF)
    qkv[:, lanes_v] = value_acc[...].astype(BF)


class Exchange:
    def __init__(self, mesh_shape, weights, shards, refs):
        self.depth = mesh_shape["fsdp"] // 2
        self.weights, self.shards = weights, shards
        self.__dict__.update(refs)
        dp, fsdp = lax.axis_index("dp"), lax.axis_index("fsdp")
        self.y, self.c = dp // 2, dp % 2
        self.z, self.x = fsdp // 2, fsdp % 2
        self.flips = [(b // 4, b // 2 % 2, b % 2) for b in range(1, 8)]

    def device(self, y=None, c=None, z=None, x=None):
        y, c = self.y if y is None else y, self.c if c is None else c
        z, x = self.z if z is None else z, self.x if x is None else x
        return (y * 2 + c, z * 2 + x)

    def far(self, d):
        return lax.rem(self.z + d, self.depth)

    def flipped(self, flip):
        own = (self.y, self.c, self.x)
        return [1 - a if f else a for a, f in zip(own, flip, strict=True)]

    def barrier(self):
        barrier = pltpu.get_barrier_semaphore()
        peers = [self.device(z=self.far(d)) for d in range(1, self.depth)]
        for flip in self.flips:
            y, c, x = self.flipped(flip)
            peers.append(self.device(y=y, c=c, x=x))
        for peer in peers:
            pl.semaphore_signal(barrier, inc=1, device_id=peer, device_id_type=MESH)
        pl.semaphore_wait(barrier, len(peers))

    def at(self, unit, y, c, z, x, lanes=slice(None)):
        return self.weights.at[unit, y, c, z, x, :, lanes]

    def remote(self, src, dst, sems, slot, device):
        return pltpu.make_async_remote_copy(
            src_ref=src,
            dst_ref=dst,
            send_sem=sems[0].at[slot],
            recv_sem=sems[1].at[slot],
            device_id=device,
            device_id_type=MESH,
        )

    def gather_copies(self, unit, step):
        y, c, z, x = self.y, self.c, self.z, self.x
        low, high, every = slice(0, HALF), slice(HALF, WIDTH), slice(None)
        to_x, to_y, to_c = self.device(x=1 - x), self.device(y=1 - y), self.device(c=1 - c)
        if step == 1:
            place = self.at(unit, y, c, z, x)
            moves = [(self.shards.at[unit], place, self.device(z=self.far(d))) for d in range(1, self.depth)]
        elif step == 2:
            one, two = [self.at(unit, y, c, every, x, lanes) for lanes in (low, high)]
            moves = [(one, one, to_x), (two, two, to_y)]
        elif step == 3:
            one = self.at(unit, y, c, every, every, low)
            two = self.at(unit, every, c, every, x, high)
            moves = [(one, one, to_y), (two, two, to_x)]
        else:
            core = self.at(unit, every, c, every, every)
            moves = [(core, core, to_c)]
        return [self.remote(src, dst, self.gather_sems, 4 * unit + step - 1, to) for src, dst, to in moves]

    def gather_all(self, unit, step):
        y, c, x, every = self.y, self.c, self.x, slice(None)
        part = (
            self.at(unit, y, c, slice(0, self.depth - 1), x),
            self.at(unit, y, c, every, x),
            self.at(unit, y, c, every, every),
            self.at(unit, every, c, every, every),
        )[step - 1]
        return self.remote(part, part, self.gather_sems, 4 * unit + step - 1, self.device(c=1 - c))

    def own_page(self, unit):
        place = self.at(unit, self.y, self.c, self.z, self.x)
        return pltpu.make_async_copy(self.shards.at[unit], place, self.local_sems.at[unit])

    def gather_step(self, unit, step):
        if step == 1:
            self.own_page(unit).start()
        if step == 2:
            self.own_page(unit).wait()
        if step > 1:
            self.gather_received(unit, step - 1)
        for copy in self.gather_copies(unit, step):
            copy.start()

    def gather_received(self, unit, step):
        self.gather_all(unit, step).wait_recv()

    def gather_sent(self, unit):
        for step in range(1, 5):
            self.gather_all(unit, step).wait_send()

    def vector_copies(self, step):
        y, c, z, x = self.y, self.c, self.z, self.x
        pages, landing = self.vec_pages, self.vec_landing
        moves = []
        if step == 1:
            place = pages.at[y, c, z, x]
            moves = [(self.vec_shard, place, self.device(z=self.far(d))) for d in range(1, self.depth)]
        elif step in (2, 3):
            for k, flip in enumerate(self.flips):
                yy, cc, xx = self.flipped(flip)
                own = pages.at[y, c, :, x]
                pair = (own, own) if step == 2 else (pages.at[yy, cc, :, xx], landing.at[k])
                moves.append((*pair, self.device(y=yy, c=cc, x=xx)))
        else:
            for d in range(1, self.depth):
                zz = self.far(d)
                moves.append((pages.at[y, c, zz, x], landing.at[7, d], self.device(z=zz)))
        return [self.remote(src, dst, self.vec_sems, step, to) for src, dst, to in moves]

    def vector_all(self, step):
        if step in (1, 4):
            part = self.vec_landing.at[7, 0 : self.depth - 1]
        else:
            part = self.vec_landing.at[0:7]
        return self.remote(part, part, self.vec_sems, step, self.device(c=1 - self.c))

    def vector_step(self, step):
        y, c, z, x = self.y, self.c, self.z, self.x
        pages, landing = self.vec_pages, self.vec_landing
        own = pltpu.make_async_copy(self.vec_shard, pages.at[y, c, z, x], self.local_sems.at[UNITS])
        if step == 1:
            own.start()
        elif step == 2:
            own.wait()
        if step in (2, 4, 5):
            self.vector_all(step - 1).wait_recv()
        if step == 4:
            for k in range(self.depth):
                total = pages[y, c, k, x]
                for j in range(7):
                    total = total + landing[j, k]
                pages[y, c, k, x] = total
        if step == 5:
            total = pages[y, c, z, x]
            for d in range(1, self.depth):
                total = total + landing[7, d]
            self.vec_sum[...] = total
            return
        for copy in self.vector_copies(step):
            copy.start()

    def vectors_sent(self, *steps):
        for step in steps:
            self.vector_all(step).wait_send()

    def add(self, place, other):
        place[...] = (place[...].astype(F32) + other[...].astype(F32)).astype(BF)

    def sum_copies(self, unit, slot, step):
        y, c, z, x = self.y, self.c, self.z, self.x
        low, high, every = slice(0, HALF), slice(HALF, WIDTH), slice(None)
        to_x, to_y, to_c = self.device(x=1 - x), self.device(y=1 - y), self.device(c=1 - c)
        if step == 1:
            moves = [(self.at(slot, every, 1 - c, every, every), self.from_core.at[unit], to_c)]
        elif step == 2:
            two = self.from_two
            moves = [(self.at(slot, 1 - y, c, every, every, low), two.at[unit, 0], to_y)]
            for k in range(2):
                moves.append((self.at(slot, k, c, every, 1 - x, high), two.at[unit, 1, :, k], to_x))
        elif step == 3:
            three = self.from_three
            moves = [
                (self.at(slot, y, c, every, 1 - x, low), three.at[unit, 0], to_x),
                (self.at(slot, 1 - y, c, every, x, high), three.at[unit, 1], to_y),
            ]
        else:
            moves = []
            for d in range(1, self.depth):
                zz = self.far(d)
                moves.append((self.at(slot, y, c, zz, x), self.from_four.at[unit, d - 1], self.device(z=zz)))
        return [self.remote(src, dst, self.sum_sems, 4 * unit + step - 1, to) for src, dst, to in moves]

    def sum_all(self, unit, slot, step):
        y, c, x, every = self.y, self.c, self.x, slice(None)
        src, dst = (
            (self.at(slot, every, c, every, every), self.from_core.at[unit]),
            (self.at(slot, y, c, every, every), self.from_two.at[unit]),
            (self.at(slot, y, c, every, x), self.from_three.at[unit]),
            (self.at(slot, y, c, slice(0, self.depth - 1), x), self.from_four.at[unit]),
        )[step - 1]
        return self.remote(src, dst, self.sum_sems, 4 * unit + step - 1, self.device(c=1 - c))

    def sum_sent(self, unit, slot):
        for step in range(1, 5):
            self.sum_all(unit, slot, step).wait_send()

    def sum_step(self, unit, slot, step):
        y, c, z, x = self.y, self.c, self.z, self.x
        low, high = slice(0, HALF), slice(HALF, WIDTH)
        if step > 1:
            self.sum_all(unit, slot, step - 1).wait_recv()
        def add_one(k, carry):
            if step == 2:
                for j in range(2):
                    for i in range(2):
                        self.add(self.at(slot, j, c, k, i), self.from_core.at[unit, j, k, i])
            elif step == 3:
                for j in range(2):
                    self.add(self.at(slot, y, c, k, j, low), self.from_two.at[unit, 0, k, j])
                    self.add(self.at(slot, j, c, k, x, high), self.from_two.at[unit, 1, k, j])
            else:
                self.add(self.at(slot, y, c, k, x, low), self.from_three.at[unit, 0, k])
                self.add(self.at(slot, y, c, k, x, high), self.from_three.at[unit, 1, k])
            return carry

        if step > 1:
            lax.fori_loop(0, self.depth, add_one, 0)
        for copy in self.sum_copies(unit, slot, step):
            copy.start()

    def summed(self, unit, slot):
        self.sum_all(unit, slot, 4).wait_recv()
        total = self.at(slot, self.y, self.c, self.z, self.x)[...].astype(F32)
        for d in range(self.depth - 1):
            total += self.from_four[unit, d].astype(F32)
        return total


def block_kernel(mesh_shape, exchanged, *refs):
    refs = list(refs)
    take = lambda n: [refs.pop(0) for _ in range(n)]
    tokens, cotangent, documents = take(3)
    if exchanged:
        shards, vec_shard = take(2)
    else:
        weights_in, vectors_in = take(2)
    result, input_grad = take(2)
    if exchanged:
        qkv_sum, out_sum, up_sum, down_sum, vec_sum = take(5)
    else:
        weights_out, vectors_out = take(2)
    (weights, cot, normed_one, qkv, mixed, lse, masks, residual, normed_two) = take(9)
    (acc_one, acc_two, low_one, low_two, fvec, svec, io_sems) = take(7)
    x_in = low_two
    key_acc, value_acc = residual.at[:, 0:128], residual.at[:, 128:256]
    length = x_in.shape[0]
    tiles = length // QB

    ex = None
    if exchanged:
        names = ("vec_pages", "vec_landing", "from_core", "from_two", "from_three", "from_four")
        extra = dict(zip(names, take(len(names))))
        gs, gr, ss, sr, vs, vr, local = take(7)
        extra.update(gather_sems=(gs, gr), sum_sems=(ss, sr), vec_sems=(vs, vr), local_sems=local)
        extra.update(vec_shard=vec_shard, vec_sum=vec_sum)
        ex = Exchange(mesh_shape, weights, shards, extra)

    def matrix(unit, start=0, width=WIDTH):
        lanes = pl.ds(start, width)
        if exchanged:
            return weights[unit, :, :, :, :, :, lanes].reshape(WIDTH, width)
        return weights[unit, :, lanes]

    def matrix_rows(unit, half):
        if exchanged:
            return weights[unit, half].reshape(HALF, WIDTH)
        return weights[unit, pl.ds(pl.multiple_of(HALF * half, HALF), HALF)]

    def gradient(unit, left, right):
        def step(half, carry):
            lanes = pl.ds(pl.multiple_of(HALF * half, 128), HALF)
            values = dg(left[:, lanes], right(), 0, 0).astype(BF)
            if exchanged:
                weights[unit, half] = values.reshape(weights.shape[2:])
            else:
                weights[unit, lanes] = values
            return carry

        lax.fori_loop(0, 2, step, 0)

    def tile_loop(body, size=QB):
        def step(i, carry):
            body(pl.ds(pl.multiple_of(i * size, size), size))
            return carry

        lax.fori_loop(0, length // size, step, 0)

    def fv(row, size=1):
        return fvec[row : row + 1, 0 : WIDTH * size]

    def tokens_sum(values):
        return jnp.sum(values.astype(F32), axis=0, keepdims=True)

    def copy(slot):
        src, dst = ((tokens, x_in), (cotangent, cot), (acc_one, result), (acc_two, input_grad))[slot]
        return pltpu.make_async_copy(src, dst, io_sems.at[slot])

    def place(name, turn=0):
        for index, steps in SCHEDULE.get(name, {}).items() if exchanged else ():

            def run(steps=steps):
                for of_sum, unit, step in steps:
                    if of_sum:
                        add_up(unit, step)
                    else:
                        ex.gather_step(unit, step)

            if isinstance(turn, int):
                if turn == index:
                    run()
            else:
                pl.when(turn == index)(run)

    def begin(unit, slot=None):
        if exchanged:
            ex.sum_step(unit, unit if slot is None else slot, 1)

    def arrived(unit):
        if exchanged:
            ex.gather_received(unit, 4)

    def add_up(unit, step):
        slot = up(unit) if unit < OUT else unit
        if step < 5:
            ex.sum_step(unit, slot, step)
            return
        total = ex.summed(unit, slot)
        rows = total.shape[0]
        chunk, kind = (unit - up(0)) // 2, (unit - up(0)) % 2
        if unit < OUT:
            for part in range(3):
                start = WIDTH * part + 256 * unit
                qkv_sum[:, start : start + 256] = total[:, 256 * part : 256 * part + 256]
        elif unit == OUT:
            out_sum[...] = total
        elif kind == 0:
            up_sum[chunk] = total
        else:
            down_sum[rows * chunk : rows * chunk + rows] = total

    copy(0).start()
    copy(1).start()
    svec[...] = jnp.zeros(svec.shape, F32)
    if exchanged:
        ex.barrier()
        ex.vector_step(1)
        for unit in range(UNITS):
            ex.gather_step(unit, 1)
        build_masks(documents, masks, False)
        place("masks")
        ex.vector_step(2)
        place("vec")
        ex.vector_all(2).wait_recv()
        ex.vectors_sent(1, 2)
        pages_to_rows(ex.vec_pages.reshape(32, VEC_ROWS, 128), fvec, 32)
        place("rows")
    else:
        weights_copy = pltpu.make_async_copy(weights_in, weights, io_sems.at[4])
        weights_copy.start()
        build_masks(documents, masks, False)
        fvec[...] = vectors_in[...]
    copy(0).wait()

    def norm_one(rows):
        normed, _ = norm_stats(x_in[rows].astype(F32))
        normed_one[rows] = (normed * fv(0) + fv(1)).astype(BF)

    tile_loop(norm_one)
    place("norm")
    if not exchanged:
        weights_copy.wait()

    def attention(unit, carry):
        place("att0", unit)
        arrived(unit)
        bias_lanes = [pl.ds(pl.multiple_of(WIDTH * k + 256 * unit, 256), 256) for k in range(2)]
        lanes = [pl.ds(pl.multiple_of(WIDTH * unit + 256 * k, 256), 256) for k in range(3)]

        def project(rows):
            full = mm(normed_one[rows], matrix(unit))
            query = (full[:, 0:256] + fvec[2:3, bias_lanes[0]]).astype(BF).astype(F32)
            qkv[rows, lanes[0]] = (query * HEAD**-0.5).astype(BF)
            qkv[rows, lanes[1]] = full[:, 256:512].astype(BF)
            qkv[rows, lanes[2]] = (full[:, 512:] + fvec[2:3, bias_lanes[1]]).astype(BF)

        tile_loop(project, 2 * QB)
        place("att1", unit)

        def pair(half, carry):
            forward_pair(unit, half, qkv, mixed, lse, masks)
            place("att2", 2 * unit + half)
            return carry

        return lax.fori_loop(0, 2, pair, carry)

    lax.fori_loop(0, 3, attention, 0)

    place("attend")
    arrived(OUT)
    copy(1).wait()

    def attend(rows):
        total = x_in[rows].astype(F32) + (mm(mixed[rows], matrix(OUT)) + fv(3))
        residual[rows] = total
        normed, _ = norm_stats(total)
        normed_two[rows] = (normed * fv(4) + fv(5)).astype(BF)
        acc_one[rows] = total + fv(7)
        acc_two[rows] = jnp.zeros_like(total)

    tile_loop(attend)
    place("attended")
    build_masks(documents, masks, True)
    place("masksT")

    def feed_forward(chunk, carry):
        up_unit, down_unit = up(chunk), down(chunk)
        place("ff0", chunk)
        arrived(up_unit)
        arrived(down_unit)

        def half_hidden(half, carry):
            lanes = pl.ds(pl.multiple_of(HALF * half, 128), HALF)
            wide = pl.ds(pl.multiple_of(WIDTH * chunk + HALF * half, 128), HALF)

            def hidden(start):
                rows = slice(start, start + QB)
                pre = mm(normed_two[rows], matrix(up_unit, lanes.start, HALF)) + fvec[6:7, wide]
                return pre, dg(cot[rows], matrix_rows(down_unit, half), 1, 1)

            def activate(start, pair):
                pre, grad = pair
                square = pre * pre
                bent = jnp.tanh(pre * (GELU_COEF + (GELU_COEF * GELU_CUBIC) * square))
                upper = 0.5 + 0.5 * bent
                slope = upper + (0.5 * pre) * (1.0 - bent * bent) * (
                    GELU_COEF + (3.0 * GELU_COEF * GELU_CUBIC) * square
                )
                rows = slice(start, start + QB)
                low_one[rows, lanes] = (pre * upper).astype(BF)
                back = (grad * slope).astype(BF)
                low_two[rows, lanes] = back
                svec[6:7, wide] += tokens_sum(back)

            current = hidden(0)
            for i in range(tiles):
                following = hidden((i + 1) * QB) if i + 1 < tiles else None
                activate(i * QB, current)
                current = following
            place("ff1", 2 * chunk + half)
            return carry

        lax.fori_loop(0, 2, half_hidden, 0)

        def outward(rows):
            acc_one[rows] += mm(low_one[rows], matrix(down_unit))
            acc_two[rows] += dg(low_two[rows], matrix(up_unit), 1, 1)

        tile_loop(outward, 2 * QB)
        place("ff3", chunk)
        if exchanged:
            ex.gather_sent(down_unit)
        gradient(down_unit, low_one, lambda: cot[...])
        begin(down_unit)
        place("ff4", chunk)
        if exchanged:
            ex.gather_sent(up_unit)
        gradient(up_unit, normed_two, lambda: low_two[...])
        begin(up_unit)
        place("ff5", chunk)
        return carry

    lax.fori_loop(0, 4, feed_forward, 0)
    copy(2).start()

    def back_two(rows):
        normed, scale = norm_stats(residual[rows])
        grad = acc_two[rows]
        grads = cot[rows].astype(F32)
        total = grads + norm_back(grad, fv(4), normed, scale)
        acc_two[rows] = total
        low = total.astype(BF)
        low_two[rows] = low
        for row, part in ((4, grad * normed), (5, grad), (7, grads), (3, low)):
            svec[row : row + 1, 0:WIDTH] += tokens_sum(part)

    def back_out(rows):
        low_one[rows] = dg(low_two[rows], matrix(OUT), 1, 1).astype(BF)

    tile_loop(back_two)
    place("back_two")
    tile_loop(back_out, 2 * QB)
    place("back_out")
    if exchanged:
        ex.gather_sent(OUT)
    gradient(OUT, mixed, lambda: low_two[...])
    begin(OUT)
    place("dWo")
    copy(2).wait()
    copy(0).start()

    def attention_back(unit, carry):
        slot = up(unit)

        def pair(half, carry):
            backward_pair(unit, half, qkv, mixed, low_one, lse, masks, key_acc, value_acc)

            place("ab0", 2 * unit + half)
            return carry

        lax.fori_loop(0, 2, pair, 0)
        all_three = pl.ds(pl.multiple_of(WIDTH * unit, WIDTH), WIDTH)
        if exchanged:
            ex.sum_sent(slot, slot)
        else:
            done = pltpu.make_async_copy(weights.at[slot], weights_out.at[slot], io_sems.at[4])
            done.start()
            done.wait()
        gradient(slot, normed_one, lambda: qkv[:, all_three])
        begin(unit, slot)
        place("ab2", unit)
        for part, row in ((0, 0), (2, WIDTH)):
            lanes = pl.ds(pl.multiple_of(WIDTH * unit + 256 * part, 256), 256)
            bias = pl.ds(pl.multiple_of(row + 256 * unit, 256), 256)
            svec[2:3, bias] = tokens_sum(qkv[:, lanes])

        return carry

    def back_qkv(rows):
        total = dg(qkv[rows, 0:WIDTH], matrix(0), 1, 1)
        for unit in (1, 2):
            total += dg(qkv[rows, WIDTH * unit : WIDTH * unit + WIDTH], matrix(unit), 1, 1)
        acc_one[rows] = total
        place("da1", rows.start // (2 * QB))

    lax.fori_loop(0, 3, attention_back, 0)
    tile_loop(back_qkv, 2 * QB)
    copy(0).wait()

    def back_one(rows):
        normed, scale = norm_stats(x_in[rows].astype(F32))
        grad = acc_one[rows]
        acc_two[rows] += norm_back(grad, fv(0), normed, scale)
        for row, part in ((0, grad * normed), (1, grad)):
            svec[row : row + 1, 0:WIDTH] += tokens_sum(part)

    tile_loop(back_one)
    copy(3).start()
    if exchanged:
        place("back_one")
        rows_to_pages(svec, ex.vec_pages.reshape(32, VEC_ROWS, 128), 32)
        ex.vector_step(3)
        place("r2p")
        ex.vector_step(4)
        place("drain")
        ex.vector_step(5)
        ex.vectors_sent(3, 4)
        for unit in range(3):
            ex.gather_sent(unit)
            ex.sum_sent(unit, up(unit))
        for unit in (OUT, up(3), *map(down, range(4))):
            ex.sum_sent(unit, unit)
    else:
        vectors_out[...] = svec[...]
        own = [(k, k) for k in (OUT, up(3), *map(down, range(4)))]
        for src, dst in [(up(k), k) for k in range(3)] + own:
            done = pltpu.make_async_copy(weights.at[src], weights_out.at[dst], io_sems.at[4])
            done.start()
            done.wait()
    copy(3).wait()


def finish_kernel(*refs):
    page, outs = refs[6], refs[7:]
    outs[0][...] = refs[0][...]
    outs[1][...] = refs[1][...]

    @pl.when(pl.program_id(0) == 0)
    def _():
        for k in (2, 3, 5):
            outs[k][...] = refs[k][...]
        up, rows = refs[4], refs[4].shape[1]
        shards = WIDTH // rows
        groups = [
            jnp.concatenate([up[j, :, 4 * rows * g : 4 * rows * g + 4 * rows] for j in range(4)], 1)
            for g in range(shards // 4)
        ]
        moved = lax.dot_general(
            jnp.concatenate(groups, 0),
            regroup(rows, True).astype(F32),
            (((1,), (0,)), ((), ())),
            preferred_element_type=F32,
            precision=lax.Precision.HIGHEST,
        )
        for g in range(shards // 4):
            outs[4][:, HALF * g : HALF * g + HALF] = moved[rows * g : rows * g + rows]
        for r, dst in enumerate(outs[6:]):
            dst[...] = page[r, 0 : dst.shape[0]]


def finish(rows, sums, page, sizes):
    block = pl.BlockSpec((rows[0].shape[0] // 2, WIDTH), lambda i: (i, 0))
    whole = lambda shape: pl.BlockSpec(shape, lambda i: (0,) * len(shape))
    ins = [block, block] + [whole(a.shape) for a in (*sums, page)]
    qkv, out, up, down = [a.shape for a in sums]
    shapes = [qkv, out, (up[1], 4 * WIDTH), down] + [(n,) for n in sizes]
    outs = [block, block] + [whole(shape) for shape in shapes]
    shapes = [a.shape for a in rows] + shapes
    return pl.pallas_call(
        finish_kernel,
        grid=(2,),
        in_specs=ins,
        out_specs=outs,
        out_shape=[jax.ShapeDtypeStruct(shape, F32) for shape in shapes],
        name="finish",
    )(*rows, *sums, page)


def run_block(mesh_shape, exchanged, tokens, cotangent, documents, *weights):
    length, width = tokens.shape
    depth = mesh_shape["fsdp"] // 2
    vmem = pltpu.VMEM
    whole = pl.BlockSpec(memory_space=pltpu.VMEM)
    far = pl.BlockSpec(memory_space=pl.ANY)
    blocks = len(mask_blocks(length))
    rows = [jax.ShapeDtypeStruct((length, WIDTH), F32)] * 2
    if exchanged:
        shard = weights[0].shape[1]
        in_specs = [far, far, whole, far, far]
        out_shape = rows + [
            jax.ShapeDtypeStruct((shard, 3 * WIDTH), F32),
            jax.ShapeDtypeStruct((shard, WIDTH), F32),
            jax.ShapeDtypeStruct((4, shard, WIDTH), F32),
            jax.ShapeDtypeStruct((4 * shard, WIDTH), F32),
            jax.ShapeDtypeStruct((VEC_ROWS, 128), F32),
        ]
        out_specs = [far, far] + [whole] * 5
        places = (2, 2, depth, 2)
        held = [vmem((UNITS, *places, shard, WIDTH), BF)]
    else:
        in_specs = [far, far, whole, far, whole]
        out_shape = rows + [
            jax.ShapeDtypeStruct((UNITS, WIDTH, WIDTH), BF),
            jax.ShapeDtypeStruct((VEC_ROWS, 4 * WIDTH), F32),
        ]
        out_specs = [far, far, far, whole]
        held = [vmem((UNITS, WIDTH, WIDTH), BF)]
    low, full = vmem((length, WIDTH), BF), vmem((length, WIDTH), F32)
    scratch = held + [
        low,
        low,
        vmem((length, 3 * WIDTH), BF),
        low,
        vmem((6, 8, length), F32),
        vmem((blocks, QB, QB), F32),
        full,
        low,
        full,
        full,
        low,
        low,
        vmem((VEC_ROWS, 4 * WIDTH), F32),
        vmem((VEC_ROWS, 4 * WIDTH), F32),
        pltpu.SemaphoreType.DMA((8,)),
    ]
    if exchanged:
        dma = pltpu.SemaphoreType.DMA
        scratch += [
            vmem((2, 2, depth, 2, VEC_ROWS, 128), F32),
            vmem((8, depth, VEC_ROWS, 128), F32),
            vmem((UNITS, 2, depth, 2, shard, WIDTH), BF),
            vmem((UNITS, 2, depth, 2, shard, HALF), BF),
            vmem((UNITS, 2, depth, shard, HALF), BF),
            vmem((UNITS, depth - 1, shard, WIDTH), BF),
            dma((4 * UNITS,)),
            dma((4 * UNITS,)),
            dma((4 * UNITS,)),
            dma((4 * UNITS,)),
            dma((5,)),
            dma((5,)),
            dma((UNITS + 1,)),
        ]
    params = dict(vmem_limit_bytes=VMEM_BYTES)
    if exchanged:
        params.update(collective_id=0, has_side_effects=True)
    return pl.pallas_call(
        functools.partial(block_kernel, mesh_shape, exchanged),
        out_shape=out_shape,
        in_specs=in_specs,
        out_specs=out_specs,
        scratch_shapes=scratch,
        compiler_params=pltpu.CompilerParams(**params),
        name="block",
    )(tokens, cotangent, documents, *weights)


def local(mesh_shape, tokens, cotangent, document_ids, source_layer, *stacks):
    (attngain, attnshift, qkvmatrix, qvoffset, outmatrix, outoffset) = stacks[:6]
    (mlpgain, mlpshift, upmatrix, upoffset, downmatrix, downoffset) = stacks[6:]
    vectors = (attngain, attnshift, qvoffset, outoffset, mlpgain, mlpshift, upoffset, downoffset)
    matrices = (qkvmatrix, outmatrix, upmatrix, downmatrix)
    rows_seq, length, width = tokens.shape
    shard = qkvmatrix.shape[1]
    shards = WIDTH // shard
    x_rows, c_rows = tokens.reshape(length, width), cotangent.reshape(length, width)
    axes = ("dp", "fsdp")
    exchanged = mesh_shape["dp"] == 4 and mesh_shape["fsdp"] == 8 and shard % 8 == 0
    if exchanged:
        units, page = pack_layer(source_layer, vectors, matrices)
        result, input_grad, qkv, out, wide, tall, page = run_block(
            mesh_shape, True, x_rows, c_rows, document_ids, units, page
        )
        result, input_grad, qkv, out, wide, tall, *pieces = finish(
            (result, input_grad), (qkv, out, wide, tall), page, [shard * s for s in VEC_SIZES]
        )
    else:
        pick = lambda stack: lax.dynamic_index_in_dim(stack, source_layer, 0, keepdims=False)
        gather = lambda part: lax.all_gather(part, axes, axis=0, tiled=True)
        scatter = lambda part: lax.psum_scatter(part, axes, scatter_dimension=0, tiled=True)
        qkv, out, wide, tall = [gather(pick(m)) for m in matrices]
        thirds = qkv.reshape(WIDTH, 3, 3, 256).transpose(2, 0, 1, 3).reshape(3, WIDTH, WIDTH)
        ups, downs = wide.reshape(WIDTH, 4, WIDTH).transpose(1, 0, 2), tall.reshape(4, WIDTH, WIDTH)
        quarters = jnp.stack([ups, downs], 1).reshape(8, WIDTH, WIDTH)
        weights = jnp.concatenate([thirds, out[None], quarters], 0)
        rows = [gather(pick(v)).astype(F32) for v in vectors]
        table = jnp.stack([jnp.pad(r, (0, 4 * WIDTH - r.shape[0])) for r in rows])
        result, input_grad, weights, table = run_block(
            mesh_shape, False, x_rows, c_rows, document_ids, weights, table
        )
        weights = weights.astype(F32)
        qkv = weights[0:3].reshape(3, WIDTH, 3, 256).transpose(1, 2, 0, 3).reshape(WIDTH, -1)
        wide = weights[up(0) :: 2].transpose(1, 0, 2).reshape(WIDTH, -1)
        tall = weights[down(0) :: 2].reshape(4 * WIDTH, WIDTH)
        qkv, out, wide, tall = [scatter(m) for m in (qkv, weights[OUT], wide, tall)]
        pieces = [scatter(table[r, 0 : WIDTH * s]) for r, s in enumerate(VEC_SIZES)]
    gain, shift, qv, outb, mid_gain, mid_shift, upb, downb = pieces
    shape = tokens.shape
    return (
        result.reshape(shape),
        input_grad.reshape(shape),
        gain,
        shift,
        qkv,
        qv,
        out,
        outb,
        mid_gain,
        mid_shift,
        wide,
        upb,
        tall,
        downb,
    )


def solution(mesh):
    axes = ("dp", "fsdp")
    rows, vector, matrix = P(axes, None, None), P(None, axes), P(None, axes, None)
    return jax.shard_map(
        functools.partial(local, dict(mesh.shape)),
        mesh=mesh,
        in_specs=(
            rows,
            rows,
            P(axes, None),
            P(),
            vector,
            vector,
            matrix,
            vector,
            matrix,
            vector,
            vector,
            vector,
            matrix,
            vector,
            matrix,
            vector,
        ),
        out_specs=(
            rows,
            rows,
            P(axes),
            P(axes),
            P(axes, None),
            P(axes),
            P(axes, None),
            P(axes),
            P(axes),
            P(axes),
            P(axes, None),
            P(axes),
            P(axes, None),
            P(axes),
        ),
        check_vma=False,
    )
```

```python
import functools

import jax
import jax.numpy as jnp
from jax import lax
from jax.experimental import pallas as pl
from jax.experimental.pallas import tpu as pltpu
from jax.sharding import PartitionSpec as P

MESH = pl.DeviceIdType.MESH
F32 = jnp.float32
BF = jnp.bfloat16
EPSILON = 1e-05
NEG_LARGE = -1000000000.0
GELU_COEF = 0.7978845608028654
GELU_CUBIC = 0.044715
WIDTH = 768
HALF = 384
HEAD = 64
QB = 256
VEC_ROWS = 8
VMEM_BYTES = 63 * 2**20
VEC_SIZES = (1, 1, 2, 1, 1, 1, 4, 1)
OUT, UNITS = 3, 12
TURNED = (6, 10)
LAST, LAST_HALF = 2, 12


def up(quarter):
    return OUT + 1 + 2 * quarter


def down(quarter):
    return OUT + 2 + 2 * quarter


SCHEDULE = {
    "rows": {
        0: ((0, 0, 2),),
    },
    "att0": {
        0: ((0, 1, 2), (0, 0, 3), (0, 2, 2), (0, 1, 3), (0, 3, 2), (0, 0, 4), (0, 2, 3), (0, 6, 2),),
    },
    "att1": {
        0: ((0, 4, 2),),
    },
    "att2": {
        0: ((0, 1, 4),),
        1: ((0, 3, 3), (0, 5, 2),),
        2: ((0, 2, 4), (0, 6, 3), (0, 7, 2),),
        3: ((0, 4, 3), (0, 8, 2),),
        4: ((0, 3, 4),),
        5: ((0, 5, 3), (0, 7, 3), (0, 9, 2), (0, 10, 2),),
    },
    "attended": {
        0: ((0, 11, 2),),
    },
    "masksT": {
        0: ((0, 4, 4),),
    },
    "ff0": {
        0: ((0, 8, 3), (0, 5, 4),),
    },
    "ff1": {
        0: ((0, 7, 4),),
        1: ((0, 9, 3),),
        2: ((0, 8, 4), (1, 5, 2), (1, 4, 2),),
        3: ((0, 9, 4),),
        4: ((1, 5, 3), (1, 7, 2),),
        5: ((0, 10, 4), (1, 4, 3), (1, 6, 2),),
        6: ((1, 4, 4), (1, 9, 2), (1, 8, 2), (1, 5, 5),),
        7: ((1, 6, 3),),
    },
    "ff3": {
        0: ((0, 6, 4), (0, 10, 3),),
        2: ((1, 5, 4),),
        3: ((1, 7, 4),),
    },
    "ff4": {
        0: ((0, 11, 3),),
        1: ((0, 11, 4),),
        3: ((1, 4, 5),),
    },
    "ff5": {
        2: ((1, 7, 3),),
        3: ((1, 9, 3),),
    },
    "back_two": {
        0: ((1, 8, 3), (1, 11, 2), (1, 6, 4), (1, 10, 2), (1, 7, 5),),
    },
    "back_out": {
        0: ((1, 9, 4),),
    },
    "dWo": {
        0: ((1, 8, 4),),
    },
    "ab0": {
        0: ((1, 11, 3), (1, 3, 2), (1, 6, 5),),
        1: ((1, 10, 3), (1, 9, 5),),
        2: ((1, 10, 4), (1, 3, 3), (1, 0, 2),),
        3: ((1, 11, 5),),
        4: ((1, 0, 3), (1, 1, 2),),
        5: ((1, 0, 4), (1, 2, 2), (1, 3, 5),),
    },
    "ab2": {
        0: ((1, 11, 4), (1, 8, 5),),
        1: ((1, 3, 4), (1, 10, 5),),
    },
    "da1": {
        0: ((1, 1, 3), (1, 12, 2), (1, 2, 3),),
        1: ((1, 0, 5),),
    },
    "back_one": {
        0: ((1, 1, 4),),
    },
    "r2p": {
        0: ((1, 12, 3), (1, 2, 4),),
    },
    "y": {
        0: ((1, 12, 4),),
        1: ((1, 1, 5), (1, 2, 5),),
    },
    "drain": {
        0: ((1, 12, 5),),
    },
}


def dg(left, right, left_dim, right_dim):
    return lax.dot_general(
        left, right, (((left_dim,), (right_dim,)), ((), ())), preferred_element_type=F32
    )


def mm(left, right):
    return jnp.dot(left, right, preferred_element_type=F32)


def regroup(rows, back):
    to = lax.broadcasted_iota(jnp.int32, (HALF, HALF), 1).astype(F32)
    source = lax.broadcasted_iota(jnp.int32, (HALF, HALF), 0).astype(F32)
    if back:
        to, source = source, to
    high = jnp.floor((to + 0.5) * (1 / (4 * rows)))
    rest = to - 4 * rows * high
    middle = jnp.floor((rest + 0.5) * (1 / rows))
    return source == 4 * rows * middle + rows * high + (rest - rows * middle)


def pack_kernel(layer_ref, *refs):
    vec_in, (qkv, out, up_in, down_in), units, vec_out = refs[:8], refs[8:12], refs[12], refs[13]
    layer = layer_ref[0]
    for t in range(3):
        for part in range(3):
            for half in range(2):
                start = WIDTH * part + 256 * t + 128 * half
                lanes = slice(HALF * half + 128 * part, HALF * half + 128 * part + 128)
                units[t, :, lanes] = qkv[0, :, start : start + 128]
    units[OUT] = out[0]
    rows = units.shape[1]
    shards = WIDTH // rows
    wide = up_in[0].astype(F32)
    groups = [wide[:, HALF * g : HALF * g + HALF] for g in range(shards // 4)]
    moved = mm(jnp.concatenate(groups, 0).astype(BF), regroup(rows, False).astype(BF))
    for j in range(4):
        lanes = slice(4 * rows * j, 4 * rows * j + 4 * rows)
        pieces = [moved[rows * g : rows * g + rows, lanes] for g in range(shards // 4)]
        units[up(j)] = jnp.concatenate(pieces, 1).astype(BF)
    wide = down_in[0].astype(F32)
    for j in range(4):
        units[down(j)] = wide[rows * j : rows * j + rows].astype(BF)
    vec_out[...] = jnp.zeros_like(vec_out)
    for r, ref in enumerate(vec_in):
        stack = ref[...].astype(F32)
        index = lax.broadcasted_iota(jnp.int32, stack.shape, 0)
        row = jnp.sum(jnp.where(index == layer, stack, 0.0), axis=0, keepdims=True)
        vec_out[r : r + 1, 0 : stack.shape[1]] = row


def pack_layer(layer, vectors, matrices):
    rows = matrices[0].shape[1]
    whole = [pl.BlockSpec(v.shape, lambda i, s: (0, 0)) for v in vectors]
    picked = [
        pl.BlockSpec((1,) + m.shape[1:], lambda i, s: (s[0], 0, 0)) for m in matrices
    ]
    return pl.pallas_call(
        pack_kernel,
        grid_spec=pltpu.PrefetchScalarGridSpec(
            num_scalar_prefetch=1,
            grid=(1,),
            in_specs=whole + picked,
            out_specs=[
                pl.BlockSpec((UNITS, rows, WIDTH), lambda i, s: (0, 0, 0)),
                pl.BlockSpec((VEC_ROWS, 128), lambda i, s: (0, 0)),
            ],
        ),
        out_shape=[
            jax.ShapeDtypeStruct((UNITS, rows, WIDTH), BF),
            jax.ShapeDtypeStruct((VEC_ROWS, 128), F32),
        ],
        name="pick_layer",
    )(layer.reshape(1), *vectors, *matrices)


def vector_parts(shards):
    base = WIDTH // shards
    parts = {}
    for r, size in enumerate(VEC_SIZES):
        for j in range(4 if size == 4 else 1):
            width = base * (1 if size == 4 else size)
            parts.setdefault(width, []).append((r, base * j, WIDTH * j))
    return parts


def page_maps(shards, width):
    total = shards * width
    col = lax.broadcasted_iota(jnp.int32, (128, total), 1).astype(F32)
    place = lax.broadcasted_iota(jnp.int32, (128, total), 0).astype(F32)
    one_hot = (col - jnp.floor((col + 0.5) * (1 / width)) * width) == place
    col_s = lax.broadcasted_iota(jnp.int32, (shards, total), 1)
    first = lax.broadcasted_iota(jnp.int32, (shards, total), 0) * width
    return one_hot, (col_s >= first) & (col_s < first + width)


def pages_to_rows(pages, fvec, shards):
    for width, parts in vector_parts(shards).items():
        one_hot, mine = page_maps(shards, width)
        one_hot = one_hot.astype(BF)
        for r, lane, start in parts:
            page = pages[:, r, :]
            if lane:
                page = pltpu.roll(page, 128 - lane, 1)
            spread = mm(page.astype(BF), one_hot)
            fvec[r : r + 1, start : start + shards * width] = jnp.sum(
                jnp.where(mine, spread, 0.0), axis=0, keepdims=True
            )


def rows_to_pages(svec, pages, shards):
    for width, parts in vector_parts(shards).items():
        one_hot, mine = page_maps(shards, width)
        one_hot = one_hot.astype(BF)
        for r, lane, start in parts:
            spread = jnp.where(mine, svec[r : r + 1, start : start + shards * width], 0.0)
            high = spread.astype(BF)
            low = (spread - high.astype(F32)).astype(BF)
            page = dg(high, one_hot, 1, 1) + dg(low, one_hot, 1, 1)
            if lane:
                pages[:, r, :] = pages[:, r, :] + pltpu.roll(page, lane, 1)
            else:
                pages[:, r, :] = page


def norm_stats(values):
    mean = jnp.mean(values, axis=-1, keepdims=True)
    centred = values - mean
    spread = jnp.mean(centred * centred, axis=-1, keepdims=True)
    scale = lax.rsqrt(spread + EPSILON)
    return centred * scale, scale


def norm_back(grad, gain, normed, scale):
    scaled = grad * gain
    mean_one = jnp.mean(scaled, axis=-1, keepdims=True)
    mean_two = jnp.mean(scaled * normed, axis=-1, keepdims=True)
    return scale * (scaled - mean_one - normed * mean_two)


def key_ranges(length):
    reach = length // 2
    return [(max(0, i * QB - reach), (i + 1) * QB) for i in range(length // QB)]


def mask_blocks(length):
    blocks = {}
    for i, (lo, hi) in enumerate(key_ranges(length)):
        for key in range(lo, hi, QB):
            blocks[i, key // QB] = len(blocks)
    return blocks


def build_masks(doc_ref, masks, transposed):
    length = doc_ref.shape[1]
    row = doc_ref[...].astype(F32)
    for (i, b), at in mask_blocks(length).items():
        queries = row[:, i * QB : (i + 1) * QB]
        keys = row[:, b * QB : (b + 1) * QB]
        along, down = (queries, keys) if transposed else (keys, queries)
        down = jnp.transpose(jnp.broadcast_to(down, (128, QB)))
        down = jnp.concatenate([down, down], 1)
        q_dim = 1 if transposed else 0
        q_pos = lax.broadcasted_iota(jnp.int32, (QB, QB), q_dim) + i * QB
        k_pos = lax.broadcasted_iota(jnp.int32, (QB, QB), 1 - q_dim) + b * QB
        masks[at] = jnp.where((k_pos <= q_pos) & (down == along), 0.0, NEG_LARGE)


def head_lanes(values, head, other=0.0):
    lane = lax.broadcasted_iota(jnp.int32, values.shape, 1)
    keep = lane >= HEAD if head else lane < HEAD
    return jnp.where(keep, values, jnp.full(values.shape, other, values.dtype))


def pair_lanes(unit, half):
    start = [unit * WIDTH + HALF * half + 128 * part for part in range(3)]
    return [pl.ds(pl.multiple_of(s, 128), 128) for s in start]


def forward_pair(unit, half, qkv, mixed, lse, masks):
    length = qkv.shape[0]
    lanes_q, lanes_k, lanes_v = pair_lanes(unit, half)
    ranges, blocks = key_ranges(length), mask_blocks(length)
    pair = 2 * unit + half
    lanes_o = pl.ds(pl.multiple_of(pair * 128, 128), 128)
    steps = [(i, h) for i in range(len(ranges)) for h in range(2)]

    def scores(step):
        i, h = step
        lo, hi = ranges[i]
        rows = slice(i * QB, (i + 1) * QB)
        raw = dg(head_lanes(qkv[rows, lanes_q], h), qkv[lo:hi, lanes_k], 1, 1)
        mask = [masks[blocks[i, b]] for b in range(lo // QB, hi // QB)]
        return raw + jnp.concatenate(mask, 1)

    def finish(step, score):
        i, h = step
        lo, hi = ranges[i]
        top = jnp.max(score, axis=1, keepdims=True)
        soft = jnp.exp(score - top).astype(BF)
        return mm(soft, head_lanes(qkv[lo:hi, lanes_v], h, 1.0)), top

    current, done = scores(steps[0]), {}
    for n, step in enumerate(steps):
        following = scores(steps[n + 1]) if n + 1 < len(steps) else None
        done[step] = finish(step, current)
        current = following
        i, h = step
        if h == 1:
            (acc0, top0), (acc1, top1) = done.pop((i, 0)), done.pop((i, 1))
            rows = slice(i * QB, (i + 1) * QB)
            first = lax.broadcasted_iota(jnp.int32, acc0.shape, 1) < HEAD
            total = pltpu.roll(jnp.where(first, acc1, acc0), HEAD, 1)
            mixed[rows, lanes_o] = (jnp.where(first, acc0, acc1) / total).astype(BF)
            logs = jnp.transpose(jnp.where(first, top0, top1) + jnp.log(total))
            lse[pair, 0:1, rows] = logs[0:1]
            lse[pair, 1:2, rows] = logs[HEAD : HEAD + 1]


def backward_pair(unit, half, qkv, mixed, mixed_grad, lse, masks, key_acc, value_acc):
    length = qkv.shape[0]
    lanes_q, lanes_k, lanes_v = pair_lanes(unit, half)
    ranges, blocks = key_ranges(length), mask_blocks(length)
    pair = 2 * unit + half
    lanes_o = pl.ds(pl.multiple_of(pair * 128, 128), 128)
    keys_t = jnp.transpose(qkv[:, lanes_k])
    steps = [(i, h) for i in range(len(ranges)) for h in range(2)]
    products = {}

    def start(step):
        i, h = step
        lo, hi = ranges[i]
        rows = slice(i * QB, (i + 1) * QB)
        query = head_lanes(qkv[rows, lanes_q], h)
        grad = head_lanes(mixed_grad[rows, lanes_o], h)
        mask = [masks[blocks[i, b]] for b in range(lo // QB, hi // QB)]
        score = dg(qkv[lo:hi, lanes_k], query, 1, 1) + jnp.concatenate(mask, 0)
        return score, dg(qkv[lo:hi, lanes_v], grad, 1, 1), query, grad

    def finish(step, started):
        i, h = step
        lo, hi = ranges[i]
        rows = slice(i * QB, (i + 1) * QB)
        score, soft_grad, query, grad = started
        if h == 0:
            products[i] = jnp.transpose(
                mixed_grad[rows, lanes_o].astype(F32) * mixed[rows, lanes_o].astype(F32)
            )
        soft = jnp.exp(score - lse[pair, h : h + 1, rows])
        centre = jnp.sum(products[i][HEAD * h : HEAD * h + HEAD], axis=0, keepdims=True)
        score_grad = (soft * (soft_grad - centre)).astype(BF)
        soft = soft.astype(BF)
        return (
            mm(keys_t[HEAD * h : HEAD * h + HEAD, lo:hi], score_grad),
            mm(score_grad, query),
            mm(soft, grad),
        )

    current, done = start(steps[0]), {}
    for n, step in enumerate(steps):
        following = start(steps[n + 1]) if n + 1 < len(steps) else None
        done[step] = finish(step, current)
        current = following
        i, h = step
        if h == 1:
            (q0, k0, v0), (q1, k1, v1) = done.pop((i, 0)), done.pop((i, 1))
            rows = slice(i * QB, (i + 1) * QB)
            lo, hi = ranges[i]
            query_grad = jnp.transpose(jnp.concatenate([q0, q1], 0))
            qkv[rows, lanes_q] = (query_grad * HEAD**-0.5).astype(BF)
            keys, values, old = k0 + k1, v0 + v1, hi - QB - lo
            if old:
                key_acc[lo : lo + old] += keys[:old]
                value_acc[lo : lo + old] += values[:old]
            key_acc[hi - QB : hi] = keys[old:]
            value_acc[hi - QB : hi] = values[old:]
    qkv[:, lanes_k] = key_acc[...].astype(BF)
    qkv[:, lanes_v] = value_acc[...].astype(BF)


def turned(unit):
    return isinstance(unit, int) and unit in TURNED


class Exchange:
    def __init__(self, mesh_shape, weights, shards, refs):
        self.depth = mesh_shape["fsdp"] // 2
        self.weights, self.shards = weights, shards
        self.__dict__.update(refs)
        dp, fsdp = lax.axis_index("dp"), lax.axis_index("fsdp")
        self.y, self.c = dp // 2, dp % 2
        self.z, self.x = fsdp // 2, fsdp % 2
        self.flips = [(b // 4, b // 2 % 2, b % 2) for b in range(1, 8)]

    def device(self, y=None, c=None, z=None, x=None):
        y, c = self.y if y is None else y, self.c if c is None else c
        z, x = self.z if z is None else z, self.x if x is None else x
        return (y * 2 + c, z * 2 + x)

    def far(self, d):
        return lax.rem(self.z + d, self.depth)

    def flipped(self, flip):
        own = (self.y, self.c, self.x)
        return [1 - a if f else a for a, f in zip(own, flip, strict=True)]

    def barrier(self):
        barrier = pltpu.get_barrier_semaphore()
        peers = [self.device(z=self.far(d)) for d in range(1, self.depth)]
        for flip in self.flips:
            y, c, x = self.flipped(flip)
            peers.append(self.device(y=y, c=c, x=x))
        for peer in peers:
            pl.semaphore_signal(barrier, inc=1, device_id=peer, device_id_type=MESH)
        pl.semaphore_wait(barrier, len(peers))

    def at(self, unit, y, c, z, x, lanes=slice(None)):
        return self.weights.at[unit, y, c, z, x, :, lanes]

    def remote(self, src, dst, sems, slot, device):
        return pltpu.make_async_remote_copy(
            src_ref=src,
            dst_ref=dst,
            send_sem=sems[0].at[slot],
            recv_sem=sems[1].at[slot],
            device_id=device,
            device_id_type=MESH,
        )

    def gather_copies(self, unit, step):
        y, c, z, x = self.y, self.c, self.z, self.x
        low, high, every = slice(0, HALF), slice(HALF, WIDTH), slice(None)
        to_x, to_y, to_c = self.device(x=1 - x), self.device(y=1 - y), self.device(c=1 - c)
        if turned(unit) and step < 4:
            moves = self.turned_moves(unit, step)
        elif step == 1:
            place = self.at(unit, y, c, z, x)
            moves = [(self.shards.at[unit], place, self.device(z=self.far(d))) for d in range(1, self.depth)]
        elif step == 2:
            one, two = [self.at(unit, y, c, every, x, lanes) for lanes in (low, high)]
            moves = [(one, one, to_x), (two, two, to_y)]
        elif step == 3:
            one = self.at(unit, y, c, every, every, low)
            two = self.at(unit, every, c, every, x, high)
            moves = [(one, one, to_y), (two, two, to_x)]
        else:
            core = self.at(unit, every, c, every, every)
            moves = [(core, core, to_c)]
        return [self.remote(src, dst, self.gather_sems, 4 * unit + step - 1, to) for src, dst, to in moves]

    def turned_moves(self, unit, step):
        y, c, z, x = self.y, self.c, self.z, self.x
        low, high, every = slice(0, HALF), slice(HALF, WIDTH), slice(None)
        to_x, to_y = self.device(x=1 - x), self.device(y=1 - y)
        if step == 1:
            return [
                (self.shards.at[unit, :, lanes], self.at(unit, y, c, z, x, lanes), to)
                for lanes, to in ((low, to_x), (high, to_y))
            ]
        if step == 2:
            one, two = self.at(unit, y, c, z, every, low), self.at(unit, every, c, z, x, high)
            return [(one, one, to_y), (two, two, to_x)]
        plane = self.at(unit, every, c, z, every)
        return [(plane, plane, self.device(z=self.far(d))) for d in range(1, self.depth)]

    def gather_all(self, unit, step):
        y, c, z, x, every = self.y, self.c, self.z, self.x, slice(None)
        part = (
            self.at(unit, y, c, z, x),
            self.at(unit, y, c, z, every),
            self.at(unit, every, c, slice(0, self.depth - 1), every),
            self.at(unit, every, c, every, every),
        )[step - 1] if turned(unit) else (
            self.at(unit, y, c, slice(0, self.depth - 1), x),
            self.at(unit, y, c, every, x),
            self.at(unit, y, c, every, every),
            self.at(unit, every, c, every, every),
        )[step - 1]
        return self.remote(part, part, self.gather_sems, 4 * unit + step - 1, self.device(c=1 - c))

    def own_page(self, unit):
        place = self.at(unit, self.y, self.c, self.z, self.x)
        return pltpu.make_async_copy(self.shards.at[unit], place, self.local_sems.at[unit])

    def gather_step(self, unit, step):
        if step == 1:
            self.own_page(unit).start()
        if step == 2:
            self.own_page(unit).wait()
        if step > 1:
            self.gather_received(unit, step - 1)
        for copy in self.gather_copies(unit, step):
            copy.start()

    def gather_received(self, unit, step):
        self.gather_all(unit, step).wait_recv()

    def gather_sent(self, unit):
        if not isinstance(unit, int):
            normal = unit >= 0
            for other in TURNED:
                normal = normal & (unit != other)
                pl.when(unit == other)(functools.partial(self.all_sent, other))
            pl.when(normal)(functools.partial(self.all_sent, unit))
        else:
            self.all_sent(unit)

    def all_sent(self, unit):
        for step in range(1, 5):
            self.gather_all(unit, step).wait_send()

    def vector_copies(self, step):
        y, c, z, x = self.y, self.c, self.z, self.x
        pages, landing = self.vec_pages, self.vec_landing
        moves = []
        if step == 1:
            place = pages.at[y, c, z, x]
            moves = [(self.vec_shard, place, self.device(z=self.far(d))) for d in range(1, self.depth)]
        elif step in (2, 3):
            for k, flip in enumerate(self.flips):
                yy, cc, xx = self.flipped(flip)
                own = pages.at[y, c, :, x]
                pair = (own, own) if step == 2 else (pages.at[yy, cc, :, xx], landing.at[k])
                moves.append((*pair, self.device(y=yy, c=cc, x=xx)))
        else:
            for d in range(1, self.depth):
                zz = self.far(d)
                moves.append((pages.at[y, c, zz, x], landing.at[7, d], self.device(z=zz)))
        return [self.remote(src, dst, self.vec_sems, step, to) for src, dst, to in moves]

    def vector_all(self, step):
        if step in (1, 4):
            part = self.vec_landing.at[7, 0 : self.depth - 1]
        else:
            part = self.vec_landing.at[0:7]
        return self.remote(part, part, self.vec_sems, step, self.device(c=1 - self.c))

    def vector_step(self, step):
        y, c, z, x = self.y, self.c, self.z, self.x
        pages, landing = self.vec_pages, self.vec_landing
        own = pltpu.make_async_copy(self.vec_shard, pages.at[y, c, z, x], self.local_sems.at[UNITS])
        if step == 1:
            own.start()
        elif step == 2:
            own.wait()
        if step in (2, 4, 5):
            self.vector_all(step - 1).wait_recv()
        if step == 4:
            for k in range(self.depth):
                total = pages[y, c, k, x]
                for j in range(7):
                    total = total + landing[j, k]
                pages[y, c, k, x] = total
        if step == 5:
            total = pages[y, c, z, x]
            for d in range(1, self.depth):
                total = total + landing[7, d]
            self.vec_sum[...] = total
            return
        for copy in self.vector_copies(step):
            copy.start()

    def vectors_sent(self, *steps):
        for step in steps:
            self.vector_all(step).wait_send()

    def add(self, place, other):
        place[...] = (place[...].astype(F32) + other[...].astype(F32)).astype(BF)

    def sum_copies(self, unit, slot, step):
        y, c, z, x = self.y, self.c, self.z, self.x
        low, high, every = slice(0, HALF), slice(HALF, WIDTH), slice(None)
        to_x, to_y, to_c = self.device(x=1 - x), self.device(y=1 - y), self.device(c=1 - c)
        if step == 1:
            moves = [(self.at(slot, every, 1 - c, every, every), self.from_core.at[unit], to_c)]
        elif step == 2:
            two = self.from_two
            moves = [(self.at(slot, 1 - y, c, every, every, low), two.at[unit, 0], to_y)]
            for k in range(2):
                moves.append((self.at(slot, k, c, every, 1 - x, high), two.at[unit, 1, :, k], to_x))
        elif step == 3:
            three = self.from_three
            moves = [
                (self.at(slot, y, c, every, 1 - x, low), three.at[unit, 0], to_x),
                (self.at(slot, 1 - y, c, every, x, high), three.at[unit, 1], to_y),
            ]
        else:
            moves = []
            for d in range(1, self.depth):
                zz = self.far(d)
                moves.append((self.at(slot, y, c, zz, x), self.from_four.at[unit, d - 1], self.device(z=zz)))
        return [self.remote(src, dst, self.sum_sems, 4 * unit + step - 1, to) for src, dst, to in moves]

    def sum_all(self, unit, slot, step):
        y, c, z, x, every = self.y, self.c, self.z, self.x, slice(None)
        src, dst = (
            (self.at(slot, every, c, every, every), self.from_core.at[unit]),
            (self.at(slot, y, c, every, every), self.from_two.at[unit]),
            (self.at(slot, y, c, every, x), self.from_three.at[unit]),
            (self.at(slot, y, c, slice(0, self.depth - 1), x), self.from_four.at[unit]),
        )[step - 1]
        return self.remote(src, dst, self.sum_sems, 4 * unit + step - 1, self.device(c=1 - c))

    def sum_sent(self, unit, slot):
        for step in range(1, 5):
            self.sum_all(unit, slot, step).wait_send()

    def sum_step(self, unit, slot, step):
        y, c, z, x = self.y, self.c, self.z, self.x
        low, high = slice(0, HALF), slice(HALF, WIDTH)
        if step > 1:
            self.sum_all(unit, slot, step - 1).wait_recv()
        def add_one(k, carry):
            if step == 2:
                for j in range(2):
                    for i in range(2):
                        self.add(self.at(slot, j, c, k, i), self.from_core.at[unit, j, k, i])
            elif step == 3:
                for j in range(2):
                    self.add(self.at(slot, y, c, k, j, low), self.from_two.at[unit, 0, k, j])
                    self.add(self.at(slot, j, c, k, x, high), self.from_two.at[unit, 1, k, j])
            else:
                self.add(self.at(slot, y, c, k, x, low), self.from_three.at[unit, 0, k])
                self.add(self.at(slot, y, c, k, x, high), self.from_three.at[unit, 1, k])
            return carry

        if step > 1:
            lax.fori_loop(0, self.depth, add_one, 0)
        for copy in self.sum_copies(unit, slot, step):
            copy.start()

    def half_copies(self, half, slot, step):
        y, c, z, x, every = self.y, self.c, self.z, self.x, slice(None)
        to_x, to_y, to_c = self.device(x=1 - x), self.device(y=1 - y), self.device(c=1 - c)
        lanes = pl.ds(pl.multiple_of(HALF * half, 128), HALF) if not isinstance(half, int) else pl.ds(HALF * half, HALF)
        middle = self.depth // 2
        near, far = slice(0, middle), slice(middle, self.depth)
        own = pl.ds(middle * half, middle)
        two, three, four = [a.at[LAST] for a in (self.from_two, self.from_three, self.from_four)]
        if step == 1:
            core = self.from_core.at[LAST, :, :, :, :, lanes]
            moves = [(self.at(slot, every, 1 - c, every, every, lanes), core, to_c)]
        elif step == 2:
            moves = [
                (self.at(slot, 1 - y, c, near, every, lanes), two.at[0, own], to_y),
                (self.at(slot, every, c, far, 1 - x, lanes), two.at[1, own], to_x),
            ]
        elif step == 3:
            moves = [
                (self.at(slot, y, c, near, 1 - x, lanes), three.at[0, own], to_x),
                (self.at(slot, 1 - y, c, far, x, lanes), three.at[1, own], to_y),
            ]
        else:
            moves = []
            for d in range(1, self.depth):
                zz = self.far(d)
                moves.append((self.at(slot, y, c, zz, x, lanes), four.at[d - 1, :, lanes], self.device(z=zz)))
        index = 4 * (LAST + (LAST_HALF - LAST) * half) + step - 1
        copies = [self.remote(src, dst, self.sum_sems, index, to) for src, dst, to in moves]
        src, dst = (
            (self.at(slot, every, c, every, every, lanes), self.from_core.at[LAST, :, :, :, :, lanes]),
            (self.at(slot, y, c, every, every, lanes), two.at[:, own]),
            (self.at(slot, y, c, every, x, lanes), three.at[:, own]),
            (self.at(slot, y, c, slice(0, self.depth - 1), x, lanes), four.at[:, :, lanes]),
        )[step - 1]
        return copies, self.remote(src, dst, self.sum_sems, index, to_c)

    def half_sent(self, half, slot):
        for step in range(1, 5):
            self.half_copies(half, slot, step)[1].wait_send()

    def half_step(self, half, slot, step):
        y, c, x = self.y, self.c, self.x
        middle = self.depth // 2
        if step > 1:
            self.half_copies(half, slot, step - 1)[1].wait_recv()
            lanes = slice(HALF * half, HALF * half + HALF)
        if step == 2:

            def add_one(k, carry):
                for j in range(2):
                    for i in range(2):
                        self.add(self.at(slot, j, c, k, i, lanes), self.from_core.at[LAST, j, k, i, :, lanes])
                return carry

            lax.fori_loop(0, self.depth, add_one, 0)
        elif step == 3:
            for k in range(middle):
                for j in range(2):
                    low, high = self.at(slot, y, c, k, j, lanes), self.at(slot, j, c, middle + k, x, lanes)
                    self.add(low, self.from_two.at[LAST, 0, middle * half + k, j])
                    self.add(high, self.from_two.at[LAST, 1, middle * half + j, k])
        elif step == 4:
            for k in range(middle):
                low, high = self.at(slot, y, c, k, x, lanes), self.at(slot, y, c, middle + k, x, lanes)
                self.add(low, self.from_three.at[LAST, 0, middle * half + k])
                self.add(high, self.from_three.at[LAST, 1, middle * half + k])
        for copy in self.half_copies(half, slot, step)[0]:
            copy.start()

    def half_summed(self, half, slot):
        self.half_copies(half, slot, 4)[1].wait_recv()
        lanes = slice(HALF * half, HALF * half + HALF)
        total = self.at(slot, self.y, self.c, self.z, self.x, lanes)[...].astype(F32)
        for d in range(self.depth - 1):
            total += self.from_four[LAST, d, :, lanes].astype(F32)
        return total

    def summed(self, unit, slot):
        self.sum_all(unit, slot, 4).wait_recv()
        total = self.at(slot, self.y, self.c, self.z, self.x)[...].astype(F32)
        for d in range(self.depth - 1):
            total += self.from_four[unit, d].astype(F32)
        return total


def block_kernel(mesh_shape, exchanged, *refs):
    refs = list(refs)
    take = lambda n: [refs.pop(0) for _ in range(n)]
    tokens, cotangent, documents = take(3)
    if exchanged:
        shards, vec_shard = take(2)
    else:
        weights_in, vectors_in = take(2)
    result, input_grad, hidden_kept, down_kept = take(4)
    if exchanged:
        qkv_sum, out_sum, up_sum, down_sum, vec_sum = take(5)
    else:
        weights_out, vectors_out = take(2)
    (weights, cot, normed_one, qkv, mixed, lse, masks, residual, normed_two) = take(9)
    (acc_one, acc_two, low_one, low_two, fvec, svec, io_sems) = take(7)
    x_in = low_two
    key_acc, value_acc = residual.at[:, 0:128], residual.at[:, 128:256]
    length = x_in.shape[0]
    tiles = length // QB

    ex = None
    if exchanged:
        names = ("vec_pages", "vec_landing", "from_core", "from_two", "from_three", "from_four")
        extra = dict(zip(names, take(len(names))))
        gs, gr, ss, sr, vs, vr, local = take(7)
        extra.update(gather_sems=(gs, gr), sum_sems=(ss, sr), vec_sems=(vs, vr), local_sems=local)
        extra.update(vec_shard=vec_shard, vec_sum=vec_sum)
        ex = Exchange(mesh_shape, weights, shards, extra)

    def matrix(unit, start=0, width=WIDTH):
        lanes = pl.ds(start, width)
        if exchanged:
            return weights[unit, :, :, :, :, :, lanes].reshape(WIDTH, width)
        return weights[unit, :, lanes]

    def matrix_rows(unit, half):
        if exchanged:
            return weights[unit, half].reshape(HALF, WIDTH)
        return weights[unit, pl.ds(pl.multiple_of(HALF * half, HALF), HALF)]

    def gradient(unit, left, right, lanes=pl.ds(0, WIDTH)):
        def step(half, carry):
            rows = pl.ds(pl.multiple_of(HALF * half, 128), HALF)
            values = dg(left[:, rows], right(), 0, 0).astype(BF)
            if exchanged:
                shape = (*weights.shape[2:6], lanes.size)
                weights[unit, half, :, :, :, :, lanes] = values.reshape(shape)
            else:
                weights[unit, rows, lanes] = values
            return carry

        lax.fori_loop(0, 2, step, 0)

    def tile_loop(body, size=QB):
        def step(i, carry):
            body(pl.ds(pl.multiple_of(i * size, size), size))
            return carry

        lax.fori_loop(0, length // size, step, 0)

    def fv(row, size=1):
        return fvec[row : row + 1, 0 : WIDTH * size]

    def tokens_sum(values):
        return jnp.sum(values.astype(F32), axis=0, keepdims=True)

    def copy(slot):
        src, dst = ((tokens, x_in), (cotangent, cot), (low_one, result), (normed_one, input_grad))[slot]
        return pltpu.make_async_copy(src, dst, io_sems.at[slot])

    hidden_homes = (normed_two, cot, low_one, mixed)

    def keep_hidden(chunk):
        return pltpu.make_async_copy(low_one, hidden_kept.at[chunk], io_sems.at[5])

    def keep_down(chunk):
        return pltpu.make_async_copy(weights.at[down(chunk)], down_kept.at[chunk], io_sems.at[6])

    def fetch_hidden(chunk):
        return pltpu.make_async_copy(hidden_kept.at[chunk], hidden_homes[chunk], io_sems.at[8 + chunk])

    def fetch_down(chunk):
        return pltpu.make_async_copy(down_kept.at[chunk], weights.at[down(chunk)], io_sems.at[12 + chunk])

    def place(name, turn=0):
        for index, steps in SCHEDULE.get(name, {}).items() if exchanged else ():

            def run(steps=steps):
                for of_sum, unit, step in steps:
                    if of_sum:
                        add_up(unit, step)
                    else:
                        ex.gather_step(unit, step)

            if isinstance(turn, int):
                if turn == index:
                    run()
            else:
                pl.when(turn == index)(run)

    def begin(unit, slot=None):
        if exchanged:
            ex.sum_step(unit, unit if slot is None else slot, 1)

    def arrived(unit):
        if exchanged:
            ex.gather_received(unit, 4)

    def add_up(unit, step):
        if unit in (LAST, LAST_HALF):
            half = int(unit == LAST_HALF)
            if step < 5:
                ex.half_step(half, up(LAST), step)
                return
            total = ex.half_summed(half, up(LAST))
            for part in range(3):
                start = WIDTH * part + 256 * LAST + 128 * half
                qkv_sum[:, start : start + 128] = total[:, 128 * part : 128 * part + 128]
            return
        slot = up(unit) if unit < OUT else unit
        if step < 5:
            ex.sum_step(unit, slot, step)
            return
        total = ex.summed(unit, slot)
        rows = total.shape[0]
        chunk, kind = (unit - up(0)) // 2, (unit - up(0)) % 2
        if unit < OUT:
            for part in range(3):
                for half in range(2):
                    start, own = WIDTH * part + 256 * unit + 128 * half, HALF * half + 128 * part
                    qkv_sum[:, start : start + 128] = total[:, own : own + 128]
        elif unit == OUT:
            out_sum[...] = total
        elif kind == 0:
            up_sum[chunk] = total
        else:
            down_sum[rows * chunk : rows * chunk + rows] = total

    copy(0).start()
    copy(1).start()
    svec[...] = jnp.zeros(svec.shape, F32)
    if exchanged:
        ex.barrier()
        ex.vector_step(1)
        for unit in range(UNITS):
            ex.gather_step(unit, 1)
        build_masks(documents, masks, False)
        place("masks")
        ex.vector_step(2)
        place("vec")
        ex.vector_all(2).wait_recv()
        ex.vectors_sent(1, 2)
        pages_to_rows(ex.vec_pages.reshape(32, VEC_ROWS, 128), fvec, 32)
        place("rows")
    else:
        weights_copy = pltpu.make_async_copy(weights_in, weights, io_sems.at[4])
        weights_copy.start()
        build_masks(documents, masks, False)
        fvec[...] = vectors_in[...]
    copy(0).wait()

    def norm_one(rows):
        normed, _ = norm_stats(x_in[rows].astype(F32))
        normed_one[rows] = (normed * fv(0) + fv(1)).astype(BF)

    tile_loop(norm_one)
    place("norm")
    if not exchanged:
        weights_copy.wait()

    def attention(unit, carry):
        place("att0", unit)
        arrived(unit)

        def project(rows):
            full = mm(normed_one[rows], matrix(unit))
            for half in range(2):
                lanes_q, lanes_k, lanes_v = pair_lanes(unit, half)
                start, first = HALF * half, 256 * unit + 128 * half
                bias = [fvec[2:3, pl.ds(pl.multiple_of(b + first, 128), 128)] for b in (0, WIDTH)]
                query = (full[:, start : start + 128] + bias[0]).astype(BF).astype(F32)
                qkv[rows, lanes_q] = (query * HEAD**-0.5).astype(BF)
                qkv[rows, lanes_k] = full[:, start + 128 : start + 256].astype(BF)
                qkv[rows, lanes_v] = (full[:, start + 256 : start + HALF] + bias[1]).astype(BF)

        tile_loop(project, 2 * QB)
        place("att1", unit)

        def pair(half, carry):
            forward_pair(unit, half, qkv, mixed, lse, masks)
            place("att2", 2 * unit + half)
            return carry

        return lax.fori_loop(0, 2, pair, carry)

    lax.fori_loop(0, 3, attention, 0)

    place("attend")
    arrived(OUT)
    copy(1).wait()

    def attend(rows):
        total = x_in[rows].astype(F32) + (mm(mixed[rows], matrix(OUT)) + fv(3))
        residual[rows] = total
        normed, _ = norm_stats(total)
        normed_two[rows] = (normed * fv(4) + fv(5)).astype(BF)
        acc_one[rows] = total + fv(7)
        acc_two[rows] = jnp.zeros_like(total)

    tile_loop(attend)
    place("attended")
    build_masks(documents, masks, True)
    place("masksT")

    def feed_forward(chunk, carry):
        up_unit, down_unit = up(chunk), down(chunk)
        place("ff0", chunk)
        arrived(up_unit)
        arrived(down_unit)
        keep_down(chunk).start()

        def half_hidden(half, carry):
            lanes = pl.ds(pl.multiple_of(HALF * half, 128), HALF)
            wide = pl.ds(pl.multiple_of(WIDTH * chunk + HALF * half, 128), HALF)

            def hidden(start):
                rows = slice(start, start + QB)
                pre = mm(normed_two[rows], matrix(up_unit, lanes.start, HALF)) + fvec[6:7, wide]
                return pre, dg(cot[rows], matrix_rows(down_unit, half), 1, 1)

            def activate(start, pair):
                pre, grad = pair
                square = pre * pre
                bent = jnp.tanh(pre * (GELU_COEF + (GELU_COEF * GELU_CUBIC) * square))
                upper = 0.5 + 0.5 * bent
                slope = upper + (0.5 * pre) * (1.0 - bent * bent) * (
                    GELU_COEF + (3.0 * GELU_COEF * GELU_CUBIC) * square
                )
                rows = slice(start, start + QB)
                low_one[rows, lanes] = (pre * upper).astype(BF)
                back = (grad * slope).astype(BF)
                low_two[rows, lanes] = back
                svec[6:7, wide] += tokens_sum(back)

            current = hidden(0)
            for i in range(tiles):
                following = hidden((i + 1) * QB) if i + 1 < tiles else None
                activate(i * QB, current)
                current = following
            place("ff1", 2 * chunk + half)
            return carry

        lax.fori_loop(0, 2, half_hidden, 0)
        keep_hidden(chunk).start()

        def outward(rows):
            acc_two[rows] += dg(low_two[rows], matrix(up_unit), 1, 1)

        tile_loop(outward, 2 * QB)
        place("ff3", chunk)
        if exchanged:
            ex.gather_sent(down_unit)
        keep_down(chunk).wait()
        gradient(down_unit, low_one, lambda: cot[...])
        begin(down_unit)
        place("ff4", chunk)
        if exchanged:
            ex.gather_sent(up_unit)
        gradient(up_unit, normed_two, lambda: low_two[...])
        begin(up_unit)
        place("ff5", chunk)
        keep_hidden(chunk).wait()
        return carry

    lax.fori_loop(0, 4, feed_forward, 0)
    fetch_hidden(0).start()

    def back_two(rows):
        normed, scale = norm_stats(residual[rows])
        grad = acc_two[rows]
        grads = cot[rows].astype(F32)
        total = grads + norm_back(grad, fv(4), normed, scale)
        acc_two[rows] = total
        low = total.astype(BF)
        low_two[rows] = low
        for row, part in ((4, grad * normed), (5, grad), (7, grads), (3, low)):
            svec[row : row + 1, 0:WIDTH] += tokens_sum(part)

    def back_out(rows):
        low_one[rows] = dg(low_two[rows], matrix(OUT), 1, 1).astype(BF)

    tile_loop(back_two)
    place("back_two")
    tile_loop(back_out, 2 * QB)
    place("back_out")
    if exchanged:
        ex.gather_sent(OUT)
    gradient(OUT, mixed, lambda: low_two[...])
    begin(OUT)
    place("dWo")
    copy(0).start()
    fetch_hidden(1).start()

    def attention_back(unit, carry):
        def free(slot):
            if exchanged:
                ex.sum_sent(slot, slot)
            else:
                done = pltpu.make_async_copy(weights.at[slot], weights_out.at[slot], io_sems.at[4])
                done.start()
                done.wait()

        def pair(half, carry):
            backward_pair(unit, half, qkv, mixed, low_one, lse, masks, key_acc, value_acc)
            place("ab0", 2 * unit + half)

            @pl.when(unit == LAST)
            def _():
                pl.when(half == 0)(lambda: free(up(LAST)))
                own = pl.ds(pl.multiple_of(WIDTH * LAST + HALF * half, 128), HALF)
                lanes = pl.ds(pl.multiple_of(HALF * half, 128), HALF)
                gradient(up(LAST), normed_one, lambda: qkv[:, own], lanes)
                if exchanged:
                    ex.half_step(half, up(LAST), 1)

            return carry

        lax.fori_loop(0, 2, pair, 0)

        @pl.when(unit != LAST)
        def _():
            free(up(unit))
            all_three = pl.ds(pl.multiple_of(WIDTH * unit, WIDTH), WIDTH)
            gradient(up(unit), normed_one, lambda: qkv[:, all_three])
            begin(unit, up(unit))

        place("ab2", unit)
        for half in range(2):
            lanes_q, _, lanes_v = pair_lanes(unit, half)
            for row, lanes in ((0, lanes_q), (WIDTH, lanes_v)):
                bias = pl.ds(pl.multiple_of(row + 256 * unit + 128 * half, 128), 128)
                svec[2:3, bias] = tokens_sum(qkv[:, lanes])

        return carry

    def back_qkv(rows):
        total = dg(qkv[rows, 0:WIDTH], matrix(0), 1, 1)
        for unit in (1, 2):
            total += dg(qkv[rows, WIDTH * unit : WIDTH * unit + WIDTH], matrix(unit), 1, 1)
        residual[rows] = total
        place("da1", rows.start // (2 * QB))

    lax.fori_loop(0, 3, attention_back, 0)
    fetch_hidden(2).start()
    fetch_hidden(3).start()
    for chunk in range(4):
        if exchanged:
            ex.sum_sent(down(chunk), down(chunk))
        else:
            done = pltpu.make_async_copy(weights.at[down(chunk)], weights_out.at[down(chunk)], io_sems.at[4])
            done.start()
            done.wait()
        fetch_down(chunk).start()
    tile_loop(back_qkv, 2 * QB)
    copy(0).wait()

    def back_one(rows):
        normed, scale = norm_stats(x_in[rows].astype(F32))
        grad = residual[rows]
        normed_one[rows] = (acc_two[rows] + norm_back(grad, fv(0), normed, scale)).astype(BF)
        for row, part in ((0, grad * normed), (1, grad)):
            svec[row : row + 1, 0:WIDTH] += tokens_sum(part)

    tile_loop(back_one)
    copy(3).start()
    if exchanged:
        place("back_one")
        rows_to_pages(svec, ex.vec_pages.reshape(32, VEC_ROWS, 128), 32)
        ex.vector_step(3)
        place("r2p")
    for chunk in range(4):
        fetch_hidden(chunk).wait()
        fetch_down(chunk).wait()

    def output(rows):
        total = acc_one[rows]
        for chunk, home in enumerate(hidden_homes):
            total += mm(home[rows], matrix(down(chunk)))
        low_one[rows] = total.astype(BF)
        place("y", rows.start // (2 * QB))
        if exchanged:
            pl.when(rows.start == 0)(lambda: ex.vector_step(4))

    tile_loop(output, 2 * QB)
    copy(2).start()
    if exchanged:
        place("drain")
        ex.vector_step(5)
        ex.vectors_sent(3, 4)
        for unit in range(3):
            ex.gather_sent(unit)
            if unit != LAST:
                ex.sum_sent(unit, up(unit))
        for half in range(2):
            ex.half_sent(half, up(LAST))
        for unit in (OUT, up(3)):
            ex.sum_sent(unit, unit)
    else:
        vectors_out[...] = svec[...]
        for src, dst in [(up(k), k) for k in range(3)] + [(OUT, OUT), (up(3), up(3))]:
            done = pltpu.make_async_copy(weights.at[src], weights_out.at[dst], io_sems.at[4])
            done.start()
            done.wait()
    copy(2).wait()
    copy(3).wait()


def finish_kernel(*refs):
    page, outs = refs[6], refs[7:]
    outs[0][...] = refs[0][...].astype(F32)
    outs[1][...] = refs[1][...].astype(F32)

    @pl.when(pl.program_id(0) == 0)
    def _():
        for k in (2, 3, 5):
            outs[k][...] = refs[k][...]
        up, rows = refs[4], refs[4].shape[1]
        shards = WIDTH // rows
        groups = [
            jnp.concatenate([up[j, :, 4 * rows * g : 4 * rows * g + 4 * rows] for j in range(4)], 1)
            for g in range(shards // 4)
        ]
        stacked, one_hot = jnp.concatenate(groups, 0), regroup(rows, True).astype(BF)
        high = stacked.astype(BF)
        moved = mm(high, one_hot) + mm((stacked - high.astype(F32)).astype(BF), one_hot)
        for g in range(shards // 4):
            outs[4][:, HALF * g : HALF * g + HALF] = moved[rows * g : rows * g + rows]
        for r, dst in enumerate(outs[6:]):
            dst[...] = page[r, 0 : dst.shape[0]]


def finish(rows, sums, page, sizes):
    block = pl.BlockSpec((rows[0].shape[0] // 2, WIDTH), lambda i: (i, 0))
    whole = lambda shape: pl.BlockSpec(shape, lambda i: (0,) * len(shape))
    ins = [block, block] + [whole(a.shape) for a in (*sums, page)]
    qkv, out, up, down = [a.shape for a in sums]
    shapes = [qkv, out, (up[1], 4 * WIDTH), down] + [(n,) for n in sizes]
    outs = [block, block] + [whole(shape) for shape in shapes]
    shapes = [a.shape for a in rows] + shapes
    return pl.pallas_call(
        finish_kernel,
        grid=(2,),
        in_specs=ins,
        out_specs=outs,
        out_shape=[jax.ShapeDtypeStruct(shape, F32) for shape in shapes],
        name="finish",
    )(*rows, *sums, page)


def run_block(mesh_shape, exchanged, tokens, cotangent, documents, *weights):
    length, width = tokens.shape
    depth = mesh_shape["fsdp"] // 2
    vmem = pltpu.VMEM
    whole = pl.BlockSpec(memory_space=pltpu.VMEM)
    far = pl.BlockSpec(memory_space=pl.ANY)
    blocks = len(mask_blocks(length))
    page = (2, 2, depth, 2, weights[0].shape[1], WIDTH) if exchanged else (WIDTH, WIDTH)
    rows = [jax.ShapeDtypeStruct((length, WIDTH), BF)] * 2
    rows += [jax.ShapeDtypeStruct((4, length, WIDTH), BF), jax.ShapeDtypeStruct((4, *page), BF)]
    if exchanged:
        shard = weights[0].shape[1]
        in_specs = [far, far, whole, far, far]
        out_shape = rows + [
            jax.ShapeDtypeStruct((shard, 3 * WIDTH), F32),
            jax.ShapeDtypeStruct((shard, WIDTH), F32),
            jax.ShapeDtypeStruct((4, shard, WIDTH), F32),
            jax.ShapeDtypeStruct((4 * shard, WIDTH), F32),
            jax.ShapeDtypeStruct((VEC_ROWS, 128), F32),
        ]
        out_specs = [far] * 4 + [whole] * 5
        places = (2, 2, depth, 2)
        held = [vmem((UNITS, *places, shard, WIDTH), BF)]
    else:
        in_specs = [far, far, whole, far, whole]
        out_shape = rows + [
            jax.ShapeDtypeStruct((UNITS, WIDTH, WIDTH), BF),
            jax.ShapeDtypeStruct((VEC_ROWS, 4 * WIDTH), F32),
        ]
        out_specs = [far] * 5 + [whole]
        held = [vmem((UNITS, WIDTH, WIDTH), BF)]
    low, full = vmem((length, WIDTH), BF), vmem((length, WIDTH), F32)
    scratch = held + [
        low,
        low,
        vmem((length, 3 * WIDTH), BF),
        low,
        vmem((6, 8, length), F32),
        vmem((blocks, QB, QB), F32),
        full,
        low,
        full,
        full,
        low,
        low,
        vmem((VEC_ROWS, 4 * WIDTH), F32),
        vmem((VEC_ROWS, 4 * WIDTH), F32),
        pltpu.SemaphoreType.DMA((16,)),
    ]
    if exchanged:
        dma = pltpu.SemaphoreType.DMA
        scratch += [
            vmem((2, 2, depth, 2, VEC_ROWS, 128), F32),
            vmem((8, depth, VEC_ROWS, 128), F32),
            vmem((UNITS, 2, depth, 2, shard, WIDTH), BF),
            vmem((UNITS, 2, depth, 2, shard, HALF), BF),
            vmem((UNITS, 2, depth, shard, HALF), BF),
            vmem((UNITS, depth - 1, shard, WIDTH), BF),
            dma((4 * UNITS,)),
            dma((4 * UNITS,)),
            dma((4 * UNITS + 4,)),
            dma((4 * UNITS + 4,)),
            dma((5,)),
            dma((5,)),
            dma((UNITS + 1,)),
        ]
    params = dict(vmem_limit_bytes=VMEM_BYTES)
    if exchanged:
        params.update(collective_id=0, has_side_effects=True)
    return pl.pallas_call(
        functools.partial(block_kernel, mesh_shape, exchanged),
        out_shape=out_shape,
        in_specs=in_specs,
        out_specs=out_specs,
        scratch_shapes=scratch,
        compiler_params=pltpu.CompilerParams(**params),
        name="block",
    )(tokens, cotangent, documents, *weights)


def local(mesh_shape, tokens, cotangent, document_ids, source_layer, *stacks):
    (attngain, attnshift, qkvmatrix, qvoffset, outmatrix, outoffset) = stacks[:6]
    (mlpgain, mlpshift, upmatrix, upoffset, downmatrix, downoffset) = stacks[6:]
    vectors = (attngain, attnshift, qvoffset, outoffset, mlpgain, mlpshift, upoffset, downoffset)
    matrices = (qkvmatrix, outmatrix, upmatrix, downmatrix)
    rows_seq, length, width = tokens.shape
    shard = qkvmatrix.shape[1]
    shards = WIDTH // shard
    x_rows, c_rows = tokens.reshape(length, width), cotangent.reshape(length, width)
    axes = ("dp", "fsdp")
    exchanged = mesh_shape["dp"] == 4 and mesh_shape["fsdp"] == 8 and shard % 8 == 0
    if exchanged:
        units, page = pack_layer(source_layer, vectors, matrices)
        result, input_grad, _, _, qkv, out, wide, tall, page = run_block(
            mesh_shape, True, x_rows, c_rows, document_ids, units, page
        )
        result, input_grad, qkv, out, wide, tall, *pieces = finish(
            (result, input_grad), (qkv, out, wide, tall), page, [shard * s for s in VEC_SIZES]
        )
    else:
        pick = lambda stack: lax.dynamic_index_in_dim(stack, source_layer, 0, keepdims=False)
        gather = lambda part: lax.all_gather(part, axes, axis=0, tiled=True)
        scatter = lambda part: lax.psum_scatter(part, axes, scatter_dimension=0, tiled=True)
        qkv, out, wide, tall = [gather(pick(m)) for m in matrices]
        thirds = qkv.reshape(WIDTH, 3, 3, 2, 128).transpose(2, 0, 3, 1, 4).reshape(3, WIDTH, WIDTH)
        ups, downs = wide.reshape(WIDTH, 4, WIDTH).transpose(1, 0, 2), tall.reshape(4, WIDTH, WIDTH)
        quarters = jnp.stack([ups, downs], 1).reshape(8, WIDTH, WIDTH)
        weights = jnp.concatenate([thirds, out[None], quarters], 0)
        rows = [gather(pick(v)).astype(F32) for v in vectors]
        table = jnp.stack([jnp.pad(r, (0, 4 * WIDTH - r.shape[0])) for r in rows])
        result, input_grad, _, _, weights, table = run_block(
            mesh_shape, False, x_rows, c_rows, document_ids, weights, table
        )
        weights = weights.astype(F32)
        qkv = weights[0:3].reshape(3, WIDTH, 2, 3, 128).transpose(1, 3, 0, 2, 4).reshape(WIDTH, -1)
        wide = weights[up(0) :: 2].transpose(1, 0, 2).reshape(WIDTH, -1)
        tall = weights[down(0) :: 2].reshape(4 * WIDTH, WIDTH)
        qkv, out, wide, tall = [scatter(m) for m in (qkv, weights[OUT], wide, tall)]
        pieces = [scatter(table[r, 0 : WIDTH * s]) for r, s in enumerate(VEC_SIZES)]
    gain, shift, qv, outb, mid_gain, mid_shift, upb, downb = pieces
    shape = tokens.shape
    result, input_grad = result.astype(F32), input_grad.astype(F32)
    return (
        result.reshape(shape),
        input_grad.reshape(shape),
        gain,
        shift,
        qkv,
        qv,
        out,
        outb,
        mid_gain,
        mid_shift,
        wide,
        upb,
        tall,
        downb,
    )


def solution(mesh):
    axes = ("dp", "fsdp")
    rows, vector, matrix = P(axes, None, None), P(None, axes), P(None, axes, None)
    return jax.shard_map(
        functools.partial(local, dict(mesh.shape)),
        mesh=mesh,
        in_specs=(
            rows,
            rows,
            P(axes, None),
            P(),
            vector,
            vector,
            matrix,
            vector,
            matrix,
            vector,
            vector,
            vector,
            matrix,
            vector,
            matrix,
            vector,
        ),
        out_specs=(
            rows,
            rows,
            P(axes),
            P(axes),
            P(axes, None),
            P(axes),
            P(axes, None),
            P(axes),
            P(axes),
            P(axes),
            P(axes, None),
            P(axes),
            P(axes, None),
            P(axes),
        ),
        check_vma=False,
    )
```

```python
import functools

import jax
import jax.numpy as jnp
from jax import lax
from jax.experimental import pallas as pl
from jax.experimental.pallas import tpu as pltpu
from jax.sharding import PartitionSpec as P

MESH = pl.DeviceIdType.MESH
F32 = jnp.float32
BF = jnp.bfloat16
EPSILON = 1e-05
NEG_LARGE = -1000000000.0
GELU_COEF = 0.7978845608028654
GELU_CUBIC = 0.044715
WIDTH = 768
HALF = 384
HEAD = 64
QB = 256
DOCS = 4
VEC_ROWS = 8
VMEM_BYTES = 63 * 2**20
VEC_SIZES = (1, 1, 2, 1, 1, 1, 4, 1)
OUT, UNITS = 3, 12
TURNED = (6, 10)
LAST, LAST_HALF = 2, 12


def up(quarter):
    return OUT + 1 + 2 * quarter


def down(quarter):
    return OUT + 2 + 2 * quarter


SCHEDULE = {
    "vec": {
        0: ((0, 0, 2),),
    },
    "att0": {
        0: ((0, 1, 2), (0, 0, 3), (0, 2, 2), (0, 1, 3), (0, 3, 2), (0, 0, 4), (0, 2, 3),),
    },
    "att1": {
        0: ((0, 4, 2),),
        2: ((0, 3, 4),),
    },
    "att2": {
        0: ((0, 1, 4),),
        1: ((0, 3, 3), (0, 5, 2), (0, 6, 2),),
        2: ((0, 2, 4), (0, 4, 3), (0, 7, 2),),
        4: ((0, 5, 3), (0, 6, 3), (0, 8, 2), (0, 9, 2),),
    },
    "attended": {
        0: ((0, 4, 4),),
    },
    "ff0": {
        0: ((0, 7, 3), (0, 10, 2), (0, 5, 4), (0, 8, 3), (0, 11, 2),),
    },
    "ff1": {
        0: ((0, 9, 3),),
        2: ((0, 8, 4), (0, 11, 3), (1, 5, 2), (1, 4, 2),),
        4: ((1, 7, 2), (1, 5, 3), (1, 6, 2),),
        5: ((0, 10, 4),),
        6: ((1, 8, 2),),
        7: ((1, 6, 3),),
    },
    "ff3": {
        0: ((0, 7, 4), (0, 6, 4),),
        1: ((0, 9, 4),),
        2: ((1, 4, 3),),
        3: ((1, 4, 4), (1, 5, 5),),
    },
    "ff4": {
        0: ((0, 10, 3),),
        3: ((1, 7, 4),),
    },
    "ff5": {
        1: ((0, 11, 4),),
        2: ((1, 7, 3), (1, 9, 2), (1, 5, 4),),
        3: ((1, 9, 3), (1, 11, 2),),
    },
    "back_two": {
        0: ((1, 8, 3), (1, 10, 2), (1, 4, 5),),
    },
    "back_out": {
        0: ((1, 6, 4), (1, 7, 5),),
    },
    "dWo": {
        0: ((1, 9, 4),),
    },
    "ab0": {
        0: ((1, 11, 3), (1, 3, 2), (1, 8, 4), (1, 6, 5),),
        1: ((1, 10, 3), (1, 9, 5),),
        2: ((1, 3, 3), (1, 0, 2), (1, 8, 5),),
        3: ((1, 10, 4), (1, 3, 4), (1, 11, 5),),
        4: ((1, 0, 3), (1, 1, 2), (1, 10, 5),),
        5: ((1, 0, 4), (1, 2, 2), (1, 3, 5),),
    },
    "ab2": {
        0: ((1, 11, 4),),
    },
    "da1": {
        0: ((1, 1, 3), (1, 2, 3), (1, 12, 2),),
        1: ((1, 0, 5),),
    },
    "back_one": {
        0: ((1, 1, 4), (1, 2, 4),),
    },
    "r2p": {
        0: ((1, 12, 3),),
    },
    "y": {
        0: ((1, 12, 4),),
        1: ((1, 1, 5), (1, 2, 5),),
    },
    "drain": {
        0: ((1, 12, 5),),
    },
}


def dg(left, right, left_dim, right_dim):
    return lax.dot_general(
        left, right, (((left_dim,), (right_dim,)), ((), ())), preferred_element_type=F32
    )


def mm(left, right):
    return jnp.dot(left, right, preferred_element_type=F32)


def regroup(rows, back):
    to = lax.broadcasted_iota(jnp.int32, (HALF, HALF), 1).astype(F32)
    source = lax.broadcasted_iota(jnp.int32, (HALF, HALF), 0).astype(F32)
    if back:
        to, source = source, to
    high = jnp.floor((to + 0.5) * (1 / (4 * rows)))
    rest = to - 4 * rows * high
    middle = jnp.floor((rest + 0.5) * (1 / rows))
    return source == 4 * rows * middle + rows * high + (rest - rows * middle)


def pack_kernel(layer_ref, *refs):
    vec_in, (qkv, out, up_in, down_in), units, vec_out = refs[:8], refs[8:12], refs[12], refs[13]
    layer = layer_ref[0]
    for t in range(3):
        for part in range(3):
            for half in range(2):
                start = WIDTH * part + 256 * t + 128 * half
                lanes = slice(HALF * half + 128 * part, HALF * half + 128 * part + 128)
                units[t, :, lanes] = qkv[0, :, start : start + 128]
    units[OUT] = out[0]
    rows = units.shape[1]
    shards = WIDTH // rows
    wide = up_in[0].astype(F32)
    groups = [wide[:, HALF * g : HALF * g + HALF] for g in range(shards // 4)]
    moved = mm(jnp.concatenate(groups, 0).astype(BF), regroup(rows, False).astype(BF))
    for j in range(4):
        lanes = slice(4 * rows * j, 4 * rows * j + 4 * rows)
        pieces = [moved[rows * g : rows * g + rows, lanes] for g in range(shards // 4)]
        units[up(j)] = jnp.concatenate(pieces, 1).astype(BF)
    wide = down_in[0].astype(F32)
    for j in range(4):
        units[down(j)] = wide[rows * j : rows * j + rows].astype(BF)
    vec_out[...] = jnp.zeros_like(vec_out)
    for r, ref in enumerate(vec_in):
        stack = ref[...].astype(F32)
        index = lax.broadcasted_iota(jnp.int32, stack.shape, 0)
        row = jnp.sum(jnp.where(index == layer, stack, 0.0), axis=0, keepdims=True)
        vec_out[r : r + 1, 0 : stack.shape[1]] = row


def pack_layer(layer, vectors, matrices):
    rows = matrices[0].shape[1]
    whole = [pl.BlockSpec(v.shape, lambda i, s: (0, 0)) for v in vectors]
    picked = [
        pl.BlockSpec((1,) + m.shape[1:], lambda i, s: (s[0], 0, 0)) for m in matrices
    ]
    return pl.pallas_call(
        pack_kernel,
        grid_spec=pltpu.PrefetchScalarGridSpec(
            num_scalar_prefetch=1,
            grid=(1,),
            in_specs=whole + picked,
            out_specs=[
                pl.BlockSpec((UNITS, rows, WIDTH), lambda i, s: (0, 0, 0)),
                pl.BlockSpec((VEC_ROWS, 128), lambda i, s: (0, 0)),
            ],
        ),
        out_shape=[
            jax.ShapeDtypeStruct((UNITS, rows, WIDTH), BF),
            jax.ShapeDtypeStruct((VEC_ROWS, 128), F32),
        ],
        name="pick_layer",
    )(layer.reshape(1), *vectors, *matrices)


def vector_parts(shards):
    base = WIDTH // shards
    parts = {}
    for r, size in enumerate(VEC_SIZES):
        for j in range(4 if size == 4 else 1):
            width = base * (1 if size == 4 else size)
            parts.setdefault(width, []).append((r, base * j, WIDTH * j))
    return parts


def page_maps(shards, width):
    total = shards * width
    col = lax.broadcasted_iota(jnp.int32, (128, total), 1).astype(F32)
    place = lax.broadcasted_iota(jnp.int32, (128, total), 0).astype(F32)
    one_hot = (col - jnp.floor((col + 0.5) * (1 / width)) * width) == place
    col_s = lax.broadcasted_iota(jnp.int32, (shards, total), 1)
    first = lax.broadcasted_iota(jnp.int32, (shards, total), 0) * width
    return one_hot, (col_s >= first) & (col_s < first + width)


def pages_to_rows(pages, fvec, shards):
    for width, parts in vector_parts(shards).items():
        one_hot, mine = page_maps(shards, width)
        one_hot = one_hot.astype(BF)
        for r, lane, start in parts:
            page = pages[:, r, :]
            if lane:
                page = pltpu.roll(page, 128 - lane, 1)
            spread = mm(page.astype(BF), one_hot)
            fvec[r : r + 1, start : start + shards * width] = jnp.sum(
                jnp.where(mine, spread, 0.0), axis=0, keepdims=True
            )


def rows_to_pages(svec, pages, shards):
    for width, parts in vector_parts(shards).items():
        one_hot, mine = page_maps(shards, width)
        one_hot = one_hot.astype(BF)
        for r, lane, start in parts:
            spread = jnp.where(mine, svec[r : r + 1, start : start + shards * width], 0.0)
            high = spread.astype(BF)
            low = (spread - high.astype(F32)).astype(BF)
            page = dg(high, one_hot, 1, 1) + dg(low, one_hot, 1, 1)
            if lane:
                pages[:, r, :] = pages[:, r, :] + pltpu.roll(page, lane, 1)
            else:
                pages[:, r, :] = page


def norm_stats(values):
    mean = jnp.mean(values, axis=-1, keepdims=True)
    centred = values - mean
    spread = jnp.mean(centred * centred, axis=-1, keepdims=True)
    scale = lax.rsqrt(spread + EPSILON)
    return centred * scale, scale


def norm_back(grad, gain, normed, scale):
    scaled = grad * gain
    mean_one = jnp.mean(scaled, axis=-1, keepdims=True)
    mean_two = jnp.mean(scaled * normed, axis=-1, keepdims=True)
    return scale * (scaled - mean_one - normed * mean_two)


def key_ranges(length):
    reach = length // 2
    return [(max(0, i * QB - reach), (i + 1) * QB) for i in range(length // QB)]


def build_masks(doc_ref, causal, features):
    for by_key in range(2):
        q_pos = lax.broadcasted_iota(jnp.int32, (QB, QB), by_key)
        k_pos = lax.broadcasted_iota(jnp.int32, (QB, QB), 1 - by_key)
        causal[by_key] = jnp.where(k_pos <= q_pos, 0.0, NEG_LARGE)
    length = doc_ref.shape[1]
    own = jnp.transpose(jnp.broadcast_to(doc_ref[...].astype(F32), (128, length)))
    lane = lax.broadcasted_iota(jnp.int32, (length, 128), 1)
    lane = jnp.where(lane >= HEAD, lane - HEAD, lane).astype(F32)
    same = own == lane
    features[0] = jnp.where(same | (lane >= DOCS), 0.0, NEG_LARGE).astype(BF)
    features[1] = jnp.where(same, 1.0, 0.0).astype(BF)


def head_lanes(values, head, other):
    lane = lax.broadcasted_iota(jnp.int32, values.shape, 1)
    keep = lane >= HEAD if head else lane < HEAD
    return jnp.where(keep, values, other)


def alone(values, head, fill=0.0):
    return head_lanes(values, head, jnp.full(values.shape, fill, values.dtype))


def pair_lanes(unit, half):
    start = [unit * WIDTH + HALF * half + 128 * part for part in range(3)]
    return [pl.ds(pl.multiple_of(s, 128), 128) for s in start]


def forward_pair(unit, half, qkv, mixed, lse, causal, features):
    length = qkv.shape[0]
    lanes_q, lanes_k, lanes_v = pair_lanes(unit, half)
    ranges = key_ranges(length)
    keys = [head_lanes(qkv[:, lanes_k], h, features[1]) for h in range(2)]
    pair = 2 * unit + half
    lanes_o = pl.ds(pl.multiple_of(pair * 128, 128), 128)
    steps = [(i, h) for i in range(len(ranges)) for h in range(2)]

    def scores(step):
        i, h = step
        lo, hi = ranges[i]
        rows = slice(i * QB, (i + 1) * QB)
        raw = dg(head_lanes(qkv[rows, lanes_q], h, features[0, rows]), keys[h][lo:hi], 1, 1)
        last = raw[:, hi - lo - QB :] + causal[0]
        return jnp.concatenate([raw[:, : hi - lo - QB], last], 1) if hi - lo > QB else last

    def finish(step, score):
        i, h = step
        lo, hi = ranges[i]
        top = jnp.max(score, axis=1, keepdims=True)
        soft = jnp.exp(score - top).astype(BF)
        return mm(soft, alone(qkv[lo:hi, lanes_v], h, 1.0)), top

    current, done = scores(steps[0]), {}
    for n, step in enumerate(steps):
        following = scores(steps[n + 1]) if n + 1 < len(steps) else None
        done[step] = finish(step, current)
        current = following
        i, h = step
        if h == 1:
            (acc0, top0), (acc1, top1) = done.pop((i, 0)), done.pop((i, 1))
            rows = slice(i * QB, (i + 1) * QB)
            first = lax.broadcasted_iota(jnp.int32, acc0.shape, 1) < HEAD
            total = pltpu.roll(jnp.where(first, acc1, acc0), HEAD, 1)
            mixed[rows, lanes_o] = (jnp.where(first, acc0, acc1) / total).astype(BF)
            logs = jnp.transpose(jnp.where(first, top0, top1) + jnp.log(total))
            lse[pair, 0:1, rows] = logs[0:1]
            lse[pair, 1:2, rows] = logs[HEAD : HEAD + 1]


def backward_pair(unit, half, qkv, mixed, mixed_grad, lse, causal, features, key_acc, value_acc):
    length = qkv.shape[0]
    lanes_q, lanes_k, lanes_v = pair_lanes(unit, half)
    ranges = key_ranges(length)
    keys = [head_lanes(qkv[:, lanes_k], h, features[1]) for h in range(2)]
    pair = 2 * unit + half
    lanes_o = pl.ds(pl.multiple_of(pair * 128, 128), 128)
    keys_t = jnp.transpose(qkv[:, lanes_k])
    steps = [(i, h) for i in range(len(ranges)) for h in range(2)]
    products = {}

    def start(step):
        i, h = step
        lo, hi = ranges[i]
        rows = slice(i * QB, (i + 1) * QB)
        query = alone(qkv[rows, lanes_q], h)
        grad = alone(mixed_grad[rows, lanes_o], h)
        raw = dg(keys[h][lo:hi], head_lanes(qkv[rows, lanes_q], h, features[0, rows]), 1, 1)
        last = raw[hi - lo - QB :] + causal[1]
        score = jnp.concatenate([raw[: hi - lo - QB], last], 0) if hi - lo > QB else last
        return score, dg(qkv[lo:hi, lanes_v], grad, 1, 1), query, grad

    def finish(step, started):
        i, h = step
        lo, hi = ranges[i]
        rows = slice(i * QB, (i + 1) * QB)
        score, soft_grad, query, grad = started
        if h == 0:
            products[i] = jnp.transpose(
                mixed_grad[rows, lanes_o].astype(F32) * mixed[rows, lanes_o].astype(F32)
            )
        soft = jnp.exp(score - lse[pair, h : h + 1, rows])
        centre = jnp.sum(products[i][HEAD * h : HEAD * h + HEAD], axis=0, keepdims=True)
        score_grad = (soft * (soft_grad - centre)).astype(BF)
        soft = soft.astype(BF)
        return (
            mm(keys_t[HEAD * h : HEAD * h + HEAD, lo:hi], score_grad),
            mm(score_grad, query),
            mm(soft, grad),
        )

    current, done = start(steps[0]), {}
    for n, step in enumerate(steps):
        following = start(steps[n + 1]) if n + 1 < len(steps) else None
        done[step] = finish(step, current)
        current = following
        i, h = step
        if h == 1:
            (q0, k0, v0), (q1, k1, v1) = done.pop((i, 0)), done.pop((i, 1))
            rows = slice(i * QB, (i + 1) * QB)
            lo, hi = ranges[i]
            query_grad = jnp.transpose(jnp.concatenate([q0, q1], 0))
            qkv[rows, lanes_q] = (query_grad * HEAD**-0.5).astype(BF)
            key_part, value_part, old = k0 + k1, v0 + v1, hi - QB - lo
            if old:
                key_acc[lo : lo + old] += key_part[:old]
                value_acc[lo : lo + old] += value_part[:old]
            key_acc[hi - QB : hi] = key_part[old:]
            value_acc[hi - QB : hi] = value_part[old:]
    qkv[:, lanes_k] = key_acc[...].astype(BF)
    qkv[:, lanes_v] = value_acc[...].astype(BF)


def turned(unit):
    return isinstance(unit, int) and unit in TURNED


class Exchange:
    def __init__(self, mesh_shape, weights, shards, refs):
        self.depth = mesh_shape["fsdp"] // 2
        self.weights, self.shards = weights, shards
        self.__dict__.update(refs)
        dp, fsdp = lax.axis_index("dp"), lax.axis_index("fsdp")
        self.y, self.c = dp // 2, dp % 2
        self.z, self.x = fsdp // 2, fsdp % 2
        self.flips = [(b // 4, b // 2 % 2, b % 2) for b in range(1, 8)]

    def device(self, y=None, c=None, z=None, x=None):
        y, c = self.y if y is None else y, self.c if c is None else c
        z, x = self.z if z is None else z, self.x if x is None else x
        return (y * 2 + c, z * 2 + x)

    def far(self, d):
        return lax.rem(self.z + d, self.depth)

    def flipped(self, flip):
        own = (self.y, self.c, self.x)
        return [1 - a if f else a for a, f in zip(own, flip, strict=True)]

    def barrier(self):
        barrier = pltpu.get_barrier_semaphore()
        peers = [self.device(z=self.far(d)) for d in range(1, self.depth)]
        for flip in self.flips:
            y, c, x = self.flipped(flip)
            peers.append(self.device(y=y, c=c, x=x))
        for peer in peers:
            pl.semaphore_signal(barrier, inc=1, device_id=peer, device_id_type=MESH)
        pl.semaphore_wait(barrier, len(peers))

    def at(self, unit, y, c, z, x, lanes=slice(None)):
        return self.weights.at[unit, y, c, z, x, :, lanes]

    def remote(self, src, dst, sems, slot, device):
        return pltpu.make_async_remote_copy(
            src_ref=src,
            dst_ref=dst,
            send_sem=sems[0].at[slot],
            recv_sem=sems[1].at[slot],
            device_id=device,
            device_id_type=MESH,
        )

    def gather_copies(self, unit, step):
        y, c, z, x = self.y, self.c, self.z, self.x
        low, high, every = slice(0, HALF), slice(HALF, WIDTH), slice(None)
        to_x, to_y, to_c = self.device(x=1 - x), self.device(y=1 - y), self.device(c=1 - c)
        if turned(unit) and step < 4:
            moves = self.turned_moves(unit, step)
        elif step == 1:
            place = self.at(unit, y, c, z, x)
            moves = [(self.shards.at[unit], place, self.device(z=self.far(d))) for d in range(1, self.depth)]
        elif step == 2:
            one, two = [self.at(unit, y, c, every, x, lanes) for lanes in (low, high)]
            moves = [(one, one, to_x), (two, two, to_y)]
        elif step == 3:
            one = self.at(unit, y, c, every, every, low)
            two = self.at(unit, every, c, every, x, high)
            moves = [(one, one, to_y), (two, two, to_x)]
        else:
            core = self.at(unit, every, c, every, every)
            moves = [(core, core, to_c)]
        return [self.remote(src, dst, self.gather_sems, 4 * unit + step - 1, to) for src, dst, to in moves]

    def turned_moves(self, unit, step):
        y, c, z, x = self.y, self.c, self.z, self.x
        low, high, every = slice(0, HALF), slice(HALF, WIDTH), slice(None)
        to_x, to_y = self.device(x=1 - x), self.device(y=1 - y)
        if step == 1:
            return [
                (self.shards.at[unit, :, lanes], self.at(unit, y, c, z, x, lanes), to)
                for lanes, to in ((low, to_x), (high, to_y))
            ]
        if step == 2:
            one, two = self.at(unit, y, c, z, every, low), self.at(unit, every, c, z, x, high)
            return [(one, one, to_y), (two, two, to_x)]
        plane = self.at(unit, every, c, z, every)
        return [(plane, plane, self.device(z=self.far(d))) for d in range(1, self.depth)]

    def gather_all(self, unit, step):
        y, c, z, x, every = self.y, self.c, self.z, self.x, slice(None)
        part = (
            self.at(unit, y, c, z, x),
            self.at(unit, y, c, z, every),
            self.at(unit, every, c, slice(0, self.depth - 1), every),
            self.at(unit, every, c, every, every),
        )[step - 1] if turned(unit) else (
            self.at(unit, y, c, slice(0, self.depth - 1), x),
            self.at(unit, y, c, every, x),
            self.at(unit, y, c, every, every),
            self.at(unit, every, c, every, every),
        )[step - 1]
        return self.remote(part, part, self.gather_sems, 4 * unit + step - 1, self.device(c=1 - c))

    def own_page(self, unit):
        place = self.at(unit, self.y, self.c, self.z, self.x)
        return pltpu.make_async_copy(self.shards.at[unit], place, self.local_sems.at[unit])

    def gather_step(self, unit, step):
        if step == 1:
            self.own_page(unit).start()
        if step == 2:
            self.own_page(unit).wait()
        if step > 1:
            self.gather_received(unit, step - 1)
        for copy in self.gather_copies(unit, step):
            copy.start()

    def gather_received(self, unit, step):
        self.gather_all(unit, step).wait_recv()

    def gather_sent(self, unit):
        if not isinstance(unit, int):
            normal = unit >= 0
            for other in TURNED:
                normal = normal & (unit != other)
                pl.when(unit == other)(functools.partial(self.all_sent, other))
            pl.when(normal)(functools.partial(self.all_sent, unit))
        else:
            self.all_sent(unit)

    def all_sent(self, unit):
        for step in range(1, 5):
            self.gather_all(unit, step).wait_send()

    def vector_copies(self, step):
        y, c, z, x = self.y, self.c, self.z, self.x
        pages, landing = self.vec_pages, self.vec_landing
        moves = []
        if step == 1:
            place = pages.at[y, c, z, x]
            moves = [(self.vec_shard, place, self.device(z=self.far(d))) for d in range(1, self.depth)]
        elif step in (2, 3):
            for k, flip in enumerate(self.flips):
                yy, cc, xx = self.flipped(flip)
                own = pages.at[y, c, :, x]
                pair = (own, own) if step == 2 else (pages.at[yy, cc, :, xx], landing.at[k])
                moves.append((*pair, self.device(y=yy, c=cc, x=xx)))
        else:
            for d in range(1, self.depth):
                zz = self.far(d)
                moves.append((pages.at[y, c, zz, x], landing.at[7, d], self.device(z=zz)))
        return [self.remote(src, dst, self.vec_sems, step, to) for src, dst, to in moves]

    def vector_all(self, step):
        if step in (1, 4):
            part = self.vec_landing.at[7, 0 : self.depth - 1]
        else:
            part = self.vec_landing.at[0:7]
        return self.remote(part, part, self.vec_sems, step, self.device(c=1 - self.c))

    def vector_step(self, step):
        y, c, z, x = self.y, self.c, self.z, self.x
        pages, landing = self.vec_pages, self.vec_landing
        own = pltpu.make_async_copy(self.vec_shard, pages.at[y, c, z, x], self.local_sems.at[UNITS])
        if step == 1:
            own.start()
        elif step == 2:
            own.wait()
        if step in (2, 4, 5):
            self.vector_all(step - 1).wait_recv()
        if step == 4:
            for k in range(self.depth):
                total = pages[y, c, k, x]
                for j in range(7):
                    total = total + landing[j, k]
                pages[y, c, k, x] = total
        if step == 5:
            total = pages[y, c, z, x]
            for d in range(1, self.depth):
                total = total + landing[7, d]
            self.vec_sum[...] = total
            return
        for copy in self.vector_copies(step):
            copy.start()

    def vectors_sent(self, *steps):
        for step in steps:
            self.vector_all(step).wait_send()

    def add(self, place, other):
        place[...] = place[...] + other[...]

    def sum_copies(self, unit, slot, step):
        y, c, z, x = self.y, self.c, self.z, self.x
        low, high, every = slice(0, HALF), slice(HALF, WIDTH), slice(None)
        to_x, to_y, to_c = self.device(x=1 - x), self.device(y=1 - y), self.device(c=1 - c)
        if step == 1:
            moves = [(self.at(slot, every, 1 - c, every, every), self.from_core.at[unit], to_c)]
        elif step == 2:
            two = self.from_two
            moves = [(self.at(slot, 1 - y, c, every, every, low), two.at[unit, 0], to_y)]
            for k in range(2):
                moves.append((self.at(slot, k, c, every, 1 - x, high), two.at[unit, 1, :, k], to_x))
        elif step == 3:
            three = self.from_three
            moves = [
                (self.at(slot, y, c, every, 1 - x, low), three.at[unit, 0], to_x),
                (self.at(slot, 1 - y, c, every, x, high), three.at[unit, 1], to_y),
            ]
        else:
            moves = []
            for d in range(1, self.depth):
                zz = self.far(d)
                moves.append((self.at(slot, y, c, zz, x), self.from_four.at[unit, d - 1], self.device(z=zz)))
        return [self.remote(src, dst, self.sum_sems, 4 * unit + step - 1, to) for src, dst, to in moves]

    def sum_all(self, unit, slot, step):
        y, c, z, x, every = self.y, self.c, self.z, self.x, slice(None)
        src, dst = (
            (self.at(slot, every, c, every, every), self.from_core.at[unit]),
            (self.at(slot, y, c, every, every), self.from_two.at[unit]),
            (self.at(slot, y, c, every, x), self.from_three.at[unit]),
            (self.at(slot, y, c, slice(0, self.depth - 1), x), self.from_four.at[unit]),
        )[step - 1]
        return self.remote(src, dst, self.sum_sems, 4 * unit + step - 1, self.device(c=1 - c))

    def sum_sent(self, unit, slot):
        for step in range(1, 5):
            self.sum_all(unit, slot, step).wait_send()

    def sum_step(self, unit, slot, step):
        y, c, z, x = self.y, self.c, self.z, self.x
        low, high = slice(0, HALF), slice(HALF, WIDTH)
        if step > 1:
            self.sum_all(unit, slot, step - 1).wait_recv()
        def add_one(k, carry):
            if step == 2:
                for j in range(2):
                    for i in range(2):
                        self.add(self.at(slot, j, c, k, i), self.from_core.at[unit, j, k, i])
            elif step == 3:
                for j in range(2):
                    self.add(self.at(slot, y, c, k, j, low), self.from_two.at[unit, 0, k, j])
                    self.add(self.at(slot, j, c, k, x, high), self.from_two.at[unit, 1, k, j])
            else:
                self.add(self.at(slot, y, c, k, x, low), self.from_three.at[unit, 0, k])
                self.add(self.at(slot, y, c, k, x, high), self.from_three.at[unit, 1, k])
            return carry

        if step > 1:
            lax.fori_loop(0, self.depth, add_one, 0)
        for copy in self.sum_copies(unit, slot, step):
            copy.start()

    def half_copies(self, half, slot, step):
        y, c, z, x, every = self.y, self.c, self.z, self.x, slice(None)
        to_x, to_y, to_c = self.device(x=1 - x), self.device(y=1 - y), self.device(c=1 - c)
        lanes = pl.ds(pl.multiple_of(HALF * half, 128), HALF) if not isinstance(half, int) else pl.ds(HALF * half, HALF)
        middle = self.depth // 2
        near, far = slice(0, middle), slice(middle, self.depth)
        own = pl.ds(middle * half, middle)
        two, three, four = [a.at[LAST] for a in (self.from_two, self.from_three, self.from_four)]
        if step == 1:
            core = self.from_core.at[LAST, :, :, :, :, lanes]
            moves = [(self.at(slot, every, 1 - c, every, every, lanes), core, to_c)]
        elif step == 2:
            moves = [
                (self.at(slot, 1 - y, c, near, every, lanes), two.at[0, own], to_y),
                (self.at(slot, every, c, far, 1 - x, lanes), two.at[1, own], to_x),
            ]
        elif step == 3:
            moves = [
                (self.at(slot, y, c, near, 1 - x, lanes), three.at[0, own], to_x),
                (self.at(slot, 1 - y, c, far, x, lanes), three.at[1, own], to_y),
            ]
        else:
            moves = []
            for d in range(1, self.depth):
                zz = self.far(d)
                moves.append((self.at(slot, y, c, zz, x, lanes), four.at[d - 1, :, lanes], self.device(z=zz)))
        index = 4 * (LAST + (LAST_HALF - LAST) * half) + step - 1
        copies = [self.remote(src, dst, self.sum_sems, index, to) for src, dst, to in moves]
        src, dst = (
            (self.at(slot, every, c, every, every, lanes), self.from_core.at[LAST, :, :, :, :, lanes]),
            (self.at(slot, y, c, every, every, lanes), two.at[:, own]),
            (self.at(slot, y, c, every, x, lanes), three.at[:, own]),
            (self.at(slot, y, c, slice(0, self.depth - 1), x, lanes), four.at[:, :, lanes]),
        )[step - 1]
        return copies, self.remote(src, dst, self.sum_sems, index, to_c)

    def half_sent(self, half, slot):
        for step in range(1, 5):
            self.half_copies(half, slot, step)[1].wait_send()

    def half_step(self, half, slot, step):
        y, c, x = self.y, self.c, self.x
        middle = self.depth // 2
        if step > 1:
            self.half_copies(half, slot, step - 1)[1].wait_recv()
            lanes = slice(HALF * half, HALF * half + HALF)
        if step == 2:

            def add_one(k, carry):
                for j in range(2):
                    for i in range(2):
                        self.add(self.at(slot, j, c, k, i, lanes), self.from_core.at[LAST, j, k, i, :, lanes])
                return carry

            lax.fori_loop(0, self.depth, add_one, 0)
        elif step == 3:
            for k in range(middle):
                for j in range(2):
                    low, high = self.at(slot, y, c, k, j, lanes), self.at(slot, j, c, middle + k, x, lanes)
                    self.add(low, self.from_two.at[LAST, 0, middle * half + k, j])
                    self.add(high, self.from_two.at[LAST, 1, middle * half + j, k])
        elif step == 4:
            for k in range(middle):
                low, high = self.at(slot, y, c, k, x, lanes), self.at(slot, y, c, middle + k, x, lanes)
                self.add(low, self.from_three.at[LAST, 0, middle * half + k])
                self.add(high, self.from_three.at[LAST, 1, middle * half + k])
        for copy in self.half_copies(half, slot, step)[0]:
            copy.start()

    def half_summed(self, half, slot):
        self.half_copies(half, slot, 4)[1].wait_recv()
        lanes = slice(HALF * half, HALF * half + HALF)
        total = self.at(slot, self.y, self.c, self.z, self.x, lanes)[...].astype(F32)
        for d in range(self.depth - 1):
            total += self.from_four[LAST, d, :, lanes].astype(F32)
        return total

    def summed(self, unit, slot):
        self.sum_all(unit, slot, 4).wait_recv()
        total = self.at(slot, self.y, self.c, self.z, self.x)[...].astype(F32)
        for d in range(self.depth - 1):
            total += self.from_four[unit, d].astype(F32)
        return total


def block_kernel(mesh_shape, exchanged, *refs):
    refs = list(refs)
    take = lambda n: [refs.pop(0) for _ in range(n)]
    tokens, cotangent, documents = take(3)
    if exchanged:
        shards, vec_shard = take(2)
    else:
        weights_in, vectors_in = take(2)
    result, input_grad, hidden_kept, down_kept = take(4)
    if exchanged:
        qkv_sum, out_sum, up_sum, down_sum, vec_sum = take(5)
    else:
        weights_out, vectors_out = take(2)
    (weights, cot, normed_one, qkv, mixed, lse, causal, features, residual, normed_two) = take(10)
    (acc_one, acc_two, low_one, low_two, fvec, svec, io_sems) = take(7)
    x_in = low_two
    key_acc, value_acc = residual.at[:, 0:128], residual.at[:, 128:256]
    length = x_in.shape[0]
    tiles = length // QB

    ex = None
    if exchanged:
        names = ("vec_pages", "vec_landing", "from_core", "from_two", "from_three", "from_four")
        extra = dict(zip(names, take(len(names))))
        gs, gr, ss, sr, vs, vr, local = take(7)
        extra.update(gather_sems=(gs, gr), sum_sems=(ss, sr), vec_sems=(vs, vr), local_sems=local)
        extra.update(vec_shard=vec_shard, vec_sum=vec_sum)
        ex = Exchange(mesh_shape, weights, shards, extra)

    def matrix(unit, start=0, width=WIDTH):
        lanes = pl.ds(start, width)
        if exchanged:
            return weights[unit, :, :, :, :, :, lanes].reshape(WIDTH, width)
        return weights[unit, :, lanes]

    def matrix_rows(unit, half):
        if exchanged:
            return weights[unit, half].reshape(HALF, WIDTH)
        return weights[unit, pl.ds(pl.multiple_of(HALF * half, HALF), HALF)]

    def gradient(unit, left, right, lanes=pl.ds(0, WIDTH)):
        def step(half, carry):
            rows = pl.ds(pl.multiple_of(HALF * half, 128), HALF)
            values = dg(left[:, rows], right(), 0, 0).astype(BF)
            if exchanged:
                shape = (*weights.shape[2:6], lanes.size)
                weights[unit, half, :, :, :, :, lanes] = values.reshape(shape)
            else:
                weights[unit, rows, lanes] = values
            return carry

        lax.fori_loop(0, 2, step, 0)

    def tile_loop(body, size=QB):
        def step(i, carry):
            body(pl.ds(pl.multiple_of(i * size, size), size))
            return carry

        lax.fori_loop(0, length // size, step, 0)

    def fv(row, size=1):
        return fvec[row : row + 1, 0 : WIDTH * size]

    def tokens_sum(values):
        return jnp.sum(values.astype(F32), axis=0, keepdims=True)

    def copy(slot):
        src, dst = ((tokens, x_in), (cotangent, cot), (low_one, result), (normed_one, input_grad))[slot]
        return pltpu.make_async_copy(src, dst, io_sems.at[slot])

    hidden_homes = (normed_two, cot, low_one, mixed)

    def keep_hidden(chunk):
        return pltpu.make_async_copy(low_one, hidden_kept.at[chunk], io_sems.at[5])

    def keep_down(chunk):
        return pltpu.make_async_copy(weights.at[down(chunk)], down_kept.at[chunk], io_sems.at[6])

    def fetch_hidden(chunk):
        return pltpu.make_async_copy(hidden_kept.at[chunk], hidden_homes[chunk], io_sems.at[8 + chunk])

    def fetch_down(chunk):
        return pltpu.make_async_copy(down_kept.at[chunk], weights.at[down(chunk)], io_sems.at[12 + chunk])

    def place(name, turn=0):
        for index, steps in SCHEDULE.get(name, {}).items() if exchanged else ():

            def run(steps=steps):
                for of_sum, unit, step in steps:
                    if of_sum:
                        add_up(unit, step)
                    else:
                        ex.gather_step(unit, step)

            if isinstance(turn, int):
                if turn == index:
                    run()
            else:
                pl.when(turn == index)(run)

    def begin(unit, slot=None):
        if exchanged:
            ex.sum_step(unit, unit if slot is None else slot, 1)

    def arrived(unit):
        if exchanged:
            ex.gather_received(unit, 4)

    def add_up(unit, step):
        if unit in (LAST, LAST_HALF):
            half = int(unit == LAST_HALF)
            if step < 5:
                ex.half_step(half, up(LAST), step)
                return
            total = ex.half_summed(half, up(LAST))
            for part in range(3):
                start = WIDTH * part + 256 * LAST + 128 * half
                qkv_sum[:, start : start + 128] = total[:, 128 * part : 128 * part + 128]
            return
        slot = up(unit) if unit < OUT else unit
        if step < 5:
            ex.sum_step(unit, slot, step)
            return
        total = ex.summed(unit, slot)
        rows = total.shape[0]
        chunk, kind = (unit - up(0)) // 2, (unit - up(0)) % 2
        if unit < OUT:
            for part in range(3):
                for half in range(2):
                    start, own = WIDTH * part + 256 * unit + 128 * half, HALF * half + 128 * part
                    qkv_sum[:, start : start + 128] = total[:, own : own + 128]
        elif unit == OUT:
            out_sum[...] = total
        elif kind == 0:
            up_sum[chunk] = total
        else:
            down_sum[rows * chunk : rows * chunk + rows] = total

    copy(0).start()
    copy(1).start()
    svec[...] = jnp.zeros(svec.shape, F32)
    if exchanged:
        ex.barrier()
        ex.vector_step(1)
        for unit in range(UNITS):
            ex.gather_step(unit, 1)
        build_masks(documents, causal, features)
        place("masks")
        ex.vector_step(2)
        place("vec")
        ex.vector_all(2).wait_recv()
        ex.vectors_sent(1, 2)
        pages_to_rows(ex.vec_pages.reshape(32, VEC_ROWS, 128), fvec, 32)
        place("rows")
    else:
        weights_copy = pltpu.make_async_copy(weights_in, weights, io_sems.at[4])
        weights_copy.start()
        build_masks(documents, causal, features)
        fvec[...] = vectors_in[...]
    copy(0).wait()

    def norm_one(rows):
        normed, _ = norm_stats(x_in[rows].astype(F32))
        normed_one[rows] = (normed * fv(0) + fv(1)).astype(BF)

    tile_loop(norm_one)
    place("norm")
    if not exchanged:
        weights_copy.wait()

    def attention(unit, carry):
        place("att0", unit)
        arrived(unit)

        def project(rows):
            full = mm(normed_one[rows], matrix(unit))
            for half in range(2):
                lanes_q, lanes_k, lanes_v = pair_lanes(unit, half)
                start, first = HALF * half, 256 * unit + 128 * half
                bias = [fvec[2:3, pl.ds(pl.multiple_of(b + first, 128), 128)] for b in (0, WIDTH)]
                query = (full[:, start : start + 128] + bias[0]).astype(BF).astype(F32)
                qkv[rows, lanes_q] = (query * HEAD**-0.5).astype(BF)
                qkv[rows, lanes_k] = full[:, start + 128 : start + 256].astype(BF)
                qkv[rows, lanes_v] = (full[:, start + 256 : start + HALF] + bias[1]).astype(BF)

        tile_loop(project, 2 * QB)
        place("att1", unit)

        def pair(half, carry):
            forward_pair(unit, half, qkv, mixed, lse, causal, features)
            place("att2", 2 * unit + half)
            return carry

        return lax.fori_loop(0, 2, pair, carry)

    lax.fori_loop(0, 3, attention, 0)

    place("attend")
    arrived(OUT)
    copy(1).wait()

    def attend(rows):
        total = x_in[rows].astype(F32) + (mm(mixed[rows], matrix(OUT)) + fv(3))
        residual[rows] = total
        normed, _ = norm_stats(total)
        normed_two[rows] = (normed * fv(4) + fv(5)).astype(BF)
        acc_one[rows] = total + fv(7)
        acc_two[rows] = jnp.zeros_like(total)

    tile_loop(attend, 2 * QB)
    place("attended")

    def feed_forward(chunk, carry):
        up_unit, down_unit = up(chunk), down(chunk)
        place("ff0", chunk)
        arrived(up_unit)
        arrived(down_unit)
        keep_down(chunk).start()

        def half_hidden(half, carry):
            lanes = pl.ds(pl.multiple_of(HALF * half, 128), HALF)
            wide = pl.ds(pl.multiple_of(WIDTH * chunk + HALF * half, 128), HALF)

            def hidden(start):
                rows = slice(start, start + QB)
                pre = mm(normed_two[rows], matrix(up_unit, lanes.start, HALF)) + fvec[6:7, wide]
                return pre, dg(cot[rows], matrix_rows(down_unit, half), 1, 1)

            def activate(start, pair):
                pre, grad = pair
                square = pre * pre
                bent = jnp.tanh(pre * (GELU_COEF + (GELU_COEF * GELU_CUBIC) * square))
                upper = 0.5 + 0.5 * bent
                value = pre * upper
                slope = upper + (value - value * upper) * (
                    2.0 * GELU_COEF + (6.0 * GELU_COEF * GELU_CUBIC) * square
                )
                rows = slice(start, start + QB)
                low_one[rows, lanes] = value.astype(BF)
                back = (grad * slope).astype(BF)
                low_two[rows, lanes] = back
                svec[6:7, wide] += tokens_sum(back)

            current = hidden(0)
            for i in range(tiles):
                following = hidden((i + 1) * QB) if i + 1 < tiles else None
                activate(i * QB, current)
                current = following
            place("ff1", 2 * chunk + half)
            return carry

        lax.fori_loop(0, 2, half_hidden, 0)
        keep_hidden(chunk).start()

        def outward(rows):
            acc_two[rows] += dg(low_two[rows], matrix(up_unit), 1, 1)

        tile_loop(outward, 2 * QB)
        place("ff3", chunk)
        if exchanged:
            ex.gather_sent(down_unit)
        keep_down(chunk).wait()
        gradient(down_unit, low_one, lambda: cot[...])
        begin(down_unit)
        place("ff4", chunk)
        if exchanged:
            ex.gather_sent(up_unit)
        gradient(up_unit, normed_two, lambda: low_two[...])
        begin(up_unit)
        place("ff5", chunk)
        keep_hidden(chunk).wait()
        return carry

    lax.fori_loop(0, 4, feed_forward, 0)
    fetch_hidden(0).start()

    def back_two(rows):
        normed, scale = norm_stats(residual[rows])
        grad = acc_two[rows]
        grads = cot[rows].astype(F32)
        total = grads + norm_back(grad, fv(4), normed, scale)
        acc_two[rows] = total
        low = total.astype(BF)
        low_two[rows] = low
        for row, part in ((4, grad * normed), (5, grad), (7, grads), (3, low)):
            svec[row : row + 1, 0:WIDTH] += tokens_sum(part)

    def back_out(rows):
        low_one[rows] = dg(low_two[rows], matrix(OUT), 1, 1).astype(BF)

    tile_loop(back_two)
    place("back_two")
    tile_loop(back_out, 2 * QB)
    place("back_out")
    if exchanged:
        ex.gather_sent(OUT)
    gradient(OUT, mixed, lambda: low_two[...])
    begin(OUT)
    place("dWo")
    copy(0).start()
    fetch_hidden(1).start()

    def attention_back(unit, carry):
        def free(slot):
            if exchanged:
                ex.sum_sent(slot, slot)
            else:
                done = pltpu.make_async_copy(weights.at[slot], weights_out.at[slot], io_sems.at[4])
                done.start()
                done.wait()

        def pair(half, carry):
            backward_pair(unit, half, qkv, mixed, low_one, lse, causal, features, key_acc, value_acc)
            place("ab0", 2 * unit + half)

            @pl.when(unit == LAST)
            def _():
                pl.when(half == 0)(lambda: free(up(LAST)))
                own = pl.ds(pl.multiple_of(WIDTH * LAST + HALF * half, 128), HALF)
                lanes = pl.ds(pl.multiple_of(HALF * half, 128), HALF)
                gradient(up(LAST), normed_one, lambda: qkv[:, own], lanes)
                if exchanged:
                    ex.half_step(half, up(LAST), 1)

            return carry

        lax.fori_loop(0, 2, pair, 0)

        @pl.when(unit != LAST)
        def _():
            free(up(unit))
            all_three = pl.ds(pl.multiple_of(WIDTH * unit, WIDTH), WIDTH)
            gradient(up(unit), normed_one, lambda: qkv[:, all_three])
            begin(unit, up(unit))

        place("ab2", unit)
        for half in range(2):
            lanes_q, _, lanes_v = pair_lanes(unit, half)
            for row, lanes in ((0, lanes_q), (WIDTH, lanes_v)):
                bias = pl.ds(pl.multiple_of(row + 256 * unit + 128 * half, 128), 128)
                svec[2:3, bias] = tokens_sum(qkv[:, lanes])

        return carry

    def back_qkv(rows):
        total = dg(qkv[rows, 0:WIDTH], matrix(0), 1, 1)
        for unit in (1, 2):
            total += dg(qkv[rows, WIDTH * unit : WIDTH * unit + WIDTH], matrix(unit), 1, 1)
        residual[rows] = total
        place("da1", rows.start // (2 * QB))

    lax.fori_loop(0, 3, attention_back, 0)
    fetch_hidden(2).start()
    fetch_hidden(3).start()
    for chunk in range(4):
        if exchanged:
            ex.sum_sent(down(chunk), down(chunk))
        else:
            done = pltpu.make_async_copy(weights.at[down(chunk)], weights_out.at[down(chunk)], io_sems.at[4])
            done.start()
            done.wait()
        fetch_down(chunk).start()
    tile_loop(back_qkv, 2 * QB)
    copy(0).wait()

    def back_one(rows):
        normed, scale = norm_stats(x_in[rows].astype(F32))
        grad = residual[rows]
        normed_one[rows] = (acc_two[rows] + norm_back(grad, fv(0), normed, scale)).astype(BF)
        for row, part in ((0, grad * normed), (1, grad)):
            svec[row : row + 1, 0:WIDTH] += tokens_sum(part)

    tile_loop(back_one)
    copy(3).start()
    if exchanged:
        place("back_one")
        rows_to_pages(svec, ex.vec_pages.reshape(32, VEC_ROWS, 128), 32)
        ex.vector_step(3)
        place("r2p")
    for chunk in range(4):
        fetch_hidden(chunk).wait()
        fetch_down(chunk).wait()

    def sent_rows(rows):
        sem = io_sems.at[2 + 5 * (rows.start // (2 * QB))]
        return pltpu.make_async_copy(low_one.at[rows], result.at[rows], sem)

    def output(rows):
        total = acc_one[rows]
        for chunk, home in enumerate(hidden_homes):
            total += mm(home[rows], matrix(down(chunk)))
        low_one[rows] = total.astype(BF)
        place("y", rows.start // (2 * QB))
        if exchanged:
            pl.when(rows.start == 0)(lambda: ex.vector_step(4))
        sent_rows(rows).start()

    tile_loop(output, 2 * QB)
    if exchanged:
        place("drain")
        ex.vector_step(5)
        ex.vectors_sent(3, 4)
        for unit in range(3):
            ex.gather_sent(unit)
            if unit != LAST:
                ex.sum_sent(unit, up(unit))
        for half in range(2):
            ex.half_sent(half, up(LAST))
        for unit in (OUT, up(3)):
            ex.sum_sent(unit, unit)
    else:
        vectors_out[...] = svec[...]
        for src, dst in [(up(k), k) for k in range(3)] + [(OUT, OUT), (up(3), up(3))]:
            done = pltpu.make_async_copy(weights.at[src], weights_out.at[dst], io_sems.at[4])
            done.start()
            done.wait()
    for start in range(0, length, 2 * QB):
        sent_rows(pl.ds(start, 2 * QB)).wait()
    copy(3).wait()


def finish_kernel(*refs):
    page, outs = refs[6], refs[7:]
    outs[0][...] = refs[0][...].astype(F32)
    outs[1][...] = refs[1][...].astype(F32)

    @pl.when(pl.program_id(0) == 0)
    def _():
        for k in (2, 3, 5):
            outs[k][...] = refs[k][...]
        up, rows = refs[4], refs[4].shape[1]
        shards = WIDTH // rows
        groups = [
            jnp.concatenate([up[j, :, 4 * rows * g : 4 * rows * g + 4 * rows] for j in range(4)], 1)
            for g in range(shards // 4)
        ]
        stacked, one_hot = jnp.concatenate(groups, 0), regroup(rows, True).astype(BF)
        high = stacked.astype(BF)
        moved = mm(high, one_hot) + mm((stacked - high.astype(F32)).astype(BF), one_hot)
        for g in range(shards // 4):
            outs[4][:, HALF * g : HALF * g + HALF] = moved[rows * g : rows * g + rows]
        for r, dst in enumerate(outs[6:]):
            dst[...] = page[r, 0 : dst.shape[0]]


def finish(rows, sums, page, sizes):
    block = pl.BlockSpec((rows[0].shape[0] // 2, WIDTH), lambda i: (i, 0))
    whole = lambda shape: pl.BlockSpec(shape, lambda i: (0,) * len(shape))
    ins = [block, block] + [whole(a.shape) for a in (*sums, page)]
    qkv, out, up, down = [a.shape for a in sums]
    shapes = [qkv, out, (up[1], 4 * WIDTH), down] + [(n,) for n in sizes]
    outs = [block, block] + [whole(shape) for shape in shapes]
    shapes = [a.shape for a in rows] + shapes
    return pl.pallas_call(
        finish_kernel,
        grid=(2,),
        in_specs=ins,
        out_specs=outs,
        out_shape=[jax.ShapeDtypeStruct(shape, F32) for shape in shapes],
        name="finish",
    )(*rows, *sums, page)


def run_block(mesh_shape, exchanged, tokens, cotangent, documents, *weights):
    length, width = tokens.shape
    depth = mesh_shape["fsdp"] // 2
    vmem = pltpu.VMEM
    whole = pl.BlockSpec(memory_space=pltpu.VMEM)
    far = pl.BlockSpec(memory_space=pl.ANY)
    page = (2, 2, depth, 2, weights[0].shape[1], WIDTH) if exchanged else (WIDTH, WIDTH)
    rows = [jax.ShapeDtypeStruct((length, WIDTH), BF)] * 2
    rows += [jax.ShapeDtypeStruct((4, length, WIDTH), BF), jax.ShapeDtypeStruct((4, *page), BF)]
    if exchanged:
        shard = weights[0].shape[1]
        in_specs = [far, far, whole, far, far]
        out_shape = rows + [
            jax.ShapeDtypeStruct((shard, 3 * WIDTH), F32),
            jax.ShapeDtypeStruct((shard, WIDTH), F32),
            jax.ShapeDtypeStruct((4, shard, WIDTH), F32),
            jax.ShapeDtypeStruct((4 * shard, WIDTH), F32),
            jax.ShapeDtypeStruct((VEC_ROWS, 128), F32),
        ]
        out_specs = [far] * 4 + [whole] * 5
        places = (2, 2, depth, 2)
        held = [vmem((UNITS, *places, shard, WIDTH), BF)]
    else:
        in_specs = [far, far, whole, far, whole]
        out_shape = rows + [
            jax.ShapeDtypeStruct((UNITS, WIDTH, WIDTH), BF),
            jax.ShapeDtypeStruct((VEC_ROWS, 4 * WIDTH), F32),
        ]
        out_specs = [far] * 5 + [whole]
        held = [vmem((UNITS, WIDTH, WIDTH), BF)]
    low, full = vmem((length, WIDTH), BF), vmem((length, WIDTH), F32)
    scratch = held + [
        low,
        low,
        vmem((length, 3 * WIDTH), BF),
        low,
        vmem((6, 8, length), F32),
        vmem((2, QB, QB), F32),
        vmem((2, length, 128), BF),
        full,
        low,
        full,
        full,
        low,
        low,
        vmem((VEC_ROWS, 4 * WIDTH), F32),
        vmem((VEC_ROWS, 4 * WIDTH), F32),
        pltpu.SemaphoreType.DMA((16,)),
    ]
    if exchanged:
        dma = pltpu.SemaphoreType.DMA
        scratch += [
            vmem((2, 2, depth, 2, VEC_ROWS, 128), F32),
            vmem((8, depth, VEC_ROWS, 128), F32),
            vmem((UNITS, 2, depth, 2, shard, WIDTH), BF),
            vmem((UNITS, 2, depth, 2, shard, HALF), BF),
            vmem((UNITS, 2, depth, shard, HALF), BF),
            vmem((UNITS, depth - 1, shard, WIDTH), BF),
            dma((4 * UNITS,)),
            dma((4 * UNITS,)),
            dma((4 * UNITS + 4,)),
            dma((4 * UNITS + 4,)),
            dma((5,)),
            dma((5,)),
            dma((UNITS + 1,)),
        ]
    params = dict(vmem_limit_bytes=VMEM_BYTES)
    if exchanged:
        params.update(collective_id=0, has_side_effects=True)
    return pl.pallas_call(
        functools.partial(block_kernel, mesh_shape, exchanged),
        out_shape=out_shape,
        in_specs=in_specs,
        out_specs=out_specs,
        scratch_shapes=scratch,
        compiler_params=pltpu.CompilerParams(**params),
        name="block",
    )(tokens, cotangent, documents, *weights)


def local(mesh_shape, tokens, cotangent, document_ids, source_layer, *stacks):
    (attngain, attnshift, qkvmatrix, qvoffset, outmatrix, outoffset) = stacks[:6]
    (mlpgain, mlpshift, upmatrix, upoffset, downmatrix, downoffset) = stacks[6:]
    vectors = (attngain, attnshift, qvoffset, outoffset, mlpgain, mlpshift, upoffset, downoffset)
    matrices = (qkvmatrix, outmatrix, upmatrix, downmatrix)
    rows_seq, length, width = tokens.shape
    shard = qkvmatrix.shape[1]
    shards = WIDTH // shard
    x_rows, c_rows = tokens.reshape(length, width), cotangent.reshape(length, width)
    axes = ("dp", "fsdp")
    exchanged = mesh_shape["dp"] == 4 and mesh_shape["fsdp"] == 8 and shard % 8 == 0
    if exchanged:
        units, page = pack_layer(source_layer, vectors, matrices)
        result, input_grad, _, _, qkv, out, wide, tall, page = run_block(
            mesh_shape, True, x_rows, c_rows, document_ids, units, page
        )
        result, input_grad, qkv, out, wide, tall, *pieces = finish(
            (result, input_grad), (qkv, out, wide, tall), page, [shard * s for s in VEC_SIZES]
        )
    else:
        pick = lambda stack: lax.dynamic_index_in_dim(stack, source_layer, 0, keepdims=False)
        gather = lambda part: lax.all_gather(part, axes, axis=0, tiled=True)
        scatter = lambda part: lax.psum_scatter(part, axes, scatter_dimension=0, tiled=True)
        qkv, out, wide, tall = [gather(pick(m)) for m in matrices]
        thirds = qkv.reshape(WIDTH, 3, 3, 2, 128).transpose(2, 0, 3, 1, 4).reshape(3, WIDTH, WIDTH)
        ups, downs = wide.reshape(WIDTH, 4, WIDTH).transpose(1, 0, 2), tall.reshape(4, WIDTH, WIDTH)
        quarters = jnp.stack([ups, downs], 1).reshape(8, WIDTH, WIDTH)
        weights = jnp.concatenate([thirds, out[None], quarters], 0)
        rows = [gather(pick(v)).astype(F32) for v in vectors]
        table = jnp.stack([jnp.pad(r, (0, 4 * WIDTH - r.shape[0])) for r in rows])
        result, input_grad, _, _, weights, table = run_block(
            mesh_shape, False, x_rows, c_rows, document_ids, weights, table
        )
        weights = weights.astype(F32)
        qkv = weights[0:3].reshape(3, WIDTH, 2, 3, 128).transpose(1, 3, 0, 2, 4).reshape(WIDTH, -1)
        wide = weights[up(0) :: 2].transpose(1, 0, 2).reshape(WIDTH, -1)
        tall = weights[down(0) :: 2].reshape(4 * WIDTH, WIDTH)
        qkv, out, wide, tall = [scatter(m) for m in (qkv, weights[OUT], wide, tall)]
        pieces = [scatter(table[r, 0 : WIDTH * s]) for r, s in enumerate(VEC_SIZES)]
    gain, shift, qv, outb, mid_gain, mid_shift, upb, downb = pieces
    shape = tokens.shape
    result, input_grad = result.astype(F32), input_grad.astype(F32)
    return (
        result.reshape(shape),
        input_grad.reshape(shape),
        gain,
        shift,
        qkv,
        qv,
        out,
        outb,
        mid_gain,
        mid_shift,
        wide,
        upb,
        tall,
        downb,
    )


def solution(mesh):
    axes = ("dp", "fsdp")
    rows, vector, matrix = P(axes, None, None), P(None, axes), P(None, axes, None)
    return jax.shard_map(
        functools.partial(local, dict(mesh.shape)),
        mesh=mesh,
        in_specs=(
            rows,
            rows,
            P(axes, None),
            P(),
            vector,
            vector,
            matrix,
            vector,
            matrix,
            vector,
            vector,
            vector,
            matrix,
            vector,
            matrix,
            vector,
        ),
        out_specs=(
            rows,
            rows,
            P(axes),
            P(axes),
            P(axes, None),
            P(axes),
            P(axes, None),
            P(axes),
            P(axes),
            P(axes),
            P(axes, None),
            P(axes),
            P(axes, None),
            P(axes),
        ),
        check_vma=False,
    )
```

```python
import functools

import jax
import jax.numpy as jnp
from jax import lax
from jax.experimental import pallas as pl
from jax.experimental.pallas import tpu as pltpu
from jax.sharding import PartitionSpec as P

MESH = pl.DeviceIdType.MESH
F32 = jnp.float32
BF = jnp.bfloat16
EPSILON = 1e-05
NEG_LARGE = -1000000000.0
GELU_COEF = 0.7978845608028654
GELU_CUBIC = 0.044715
WIDTH = 768
HALF = 384
HEAD = 64
QB = 256
DOCS = 4
VEC_ROWS = 8
VMEM_BYTES = 63 * 2**20
VEC_SIZES = (1, 1, 2, 1, 1, 1, 4, 1)
OUT, UNITS = 3, 12
TURNED = (6, 10)
LAST, LAST_HALF = 2, 12


def up(quarter):
    return OUT + 1 + 2 * quarter


def down(quarter):
    return OUT + 2 + 2 * quarter


SCHEDULE = {
    "vec": {
        0: ((0, 0, 2),),
    },
    "att0": {
        0: ((0, 1, 2), (0, 0, 3), (0, 2, 2), (0, 1, 3), (0, 3, 2), (0, 0, 4), (0, 2, 3),),
    },
    "att1": {
        0: ((0, 4, 2),),
        2: ((0, 3, 4),),
    },
    "att2": {
        0: ((0, 1, 4),),
        1: ((0, 3, 3), (0, 5, 2), (0, 6, 2),),
        2: ((0, 2, 4), (0, 4, 3), (0, 7, 2),),
        4: ((0, 5, 3), (0, 6, 3), (0, 8, 2), (0, 9, 2),),
    },
    "attended": {
        0: ((0, 4, 4),),
    },
    "ff0": {
        0: ((0, 7, 3), (0, 10, 2), (0, 5, 4), (0, 8, 3), (0, 11, 2),),
    },
    "ff1": {
        0: ((0, 9, 3),),
        2: ((0, 8, 4), (0, 11, 3), (1, 5, 2), (1, 4, 2),),
        4: ((1, 7, 2), (1, 5, 3), (1, 6, 2),),
        5: ((0, 10, 4),),
        6: ((1, 8, 2),),
        7: ((1, 6, 3),),
    },
    "ff3": {
        0: ((0, 7, 4), (0, 6, 4),),
        1: ((0, 9, 4),),
        2: ((1, 4, 3),),
        3: ((1, 4, 4), (1, 5, 5),),
    },
    "ff4": {
        0: ((0, 10, 3),),
        3: ((1, 7, 4),),
    },
    "ff5": {
        1: ((0, 11, 4),),
        2: ((1, 7, 3), (1, 9, 2), (1, 5, 4),),
        3: ((1, 9, 3), (1, 11, 2),),
    },
    "back_two": {
        0: ((1, 8, 3), (1, 10, 2), (1, 4, 5),),
    },
    "back_out": {
        0: ((1, 6, 4), (1, 7, 5),),
    },
    "dWo": {
        0: ((1, 9, 4),),
    },
    "ab0": {
        0: ((1, 11, 3), (1, 3, 2), (1, 8, 4), (1, 6, 5),),
        1: ((1, 10, 3), (1, 9, 5),),
        2: ((1, 3, 3), (1, 0, 2), (1, 8, 5),),
        3: ((1, 10, 4), (1, 3, 4), (1, 11, 5),),
        4: ((1, 0, 3), (1, 1, 2), (1, 10, 5),),
        5: ((1, 0, 4), (1, 2, 2), (1, 3, 5),),
    },
    "ab2": {
        0: ((1, 11, 4),),
    },
    "da1": {
        0: ((1, 1, 3), (1, 2, 3), (1, 12, 2),),
        1: ((1, 0, 5),),
    },
    "back_one": {
        0: ((1, 1, 4), (1, 2, 4),),
    },
    "r2p": {
        0: ((1, 12, 3),),
    },
    "y": {
        0: ((1, 12, 4),),
        1: ((1, 1, 5), (1, 2, 5),),
    },
    "drain": {
        0: ((1, 12, 5),),
    },
}


def dg(left, right, left_dim, right_dim):
    return lax.dot_general(
        left, right, (((left_dim,), (right_dim,)), ((), ())), preferred_element_type=F32
    )


def mm(left, right):
    return jnp.dot(left, right, preferred_element_type=F32)


def regroup(rows, back):
    to = lax.broadcasted_iota(jnp.int32, (HALF, HALF), 1).astype(F32)
    source = lax.broadcasted_iota(jnp.int32, (HALF, HALF), 0).astype(F32)
    if back:
        to, source = source, to
    high = jnp.floor((to + 0.5) * (1 / (4 * rows)))
    rest = to - 4 * rows * high
    middle = jnp.floor((rest + 0.5) * (1 / rows))
    return source == 4 * rows * middle + rows * high + (rest - rows * middle)


def pack_kernel(layer_ref, *refs):
    vec_in, (qkv, out, up_in, down_in), units, vec_out = refs[:8], refs[8:12], refs[12], refs[13]
    layer = layer_ref[0]
    for t in range(3):
        for part in range(3):
            for half in range(2):
                start = WIDTH * part + 256 * t + 128 * half
                lanes = slice(HALF * half + 128 * part, HALF * half + 128 * part + 128)
                units[t, :, lanes] = qkv[0, :, start : start + 128]
    units[OUT] = out[0]
    rows = units.shape[1]
    shards = WIDTH // rows
    wide = up_in[0].astype(F32)
    groups = [wide[:, HALF * g : HALF * g + HALF] for g in range(shards // 4)]
    moved = mm(jnp.concatenate(groups, 0).astype(BF), regroup(rows, False).astype(BF))
    for j in range(4):
        lanes = slice(4 * rows * j, 4 * rows * j + 4 * rows)
        pieces = [moved[rows * g : rows * g + rows, lanes] for g in range(shards // 4)]
        units[up(j)] = jnp.concatenate(pieces, 1).astype(BF)
    wide = down_in[0].astype(F32)
    for j in range(4):
        units[down(j)] = wide[rows * j : rows * j + rows].astype(BF)
    vec_out[...] = jnp.zeros_like(vec_out)
    for r, ref in enumerate(vec_in):
        stack = ref[...].astype(F32)
        index = lax.broadcasted_iota(jnp.int32, stack.shape, 0)
        row = jnp.sum(jnp.where(index == layer, stack, 0.0), axis=0, keepdims=True)
        vec_out[r : r + 1, 0 : stack.shape[1]] = row


def pack_layer(layer, vectors, matrices):
    rows = matrices[0].shape[1]
    whole = [pl.BlockSpec(v.shape, lambda i, s: (0, 0)) for v in vectors]
    picked = [
        pl.BlockSpec((1,) + m.shape[1:], lambda i, s: (s[0], 0, 0)) for m in matrices
    ]
    return pl.pallas_call(
        pack_kernel,
        grid_spec=pltpu.PrefetchScalarGridSpec(
            num_scalar_prefetch=1,
            grid=(1,),
            in_specs=whole + picked,
            out_specs=[
                pl.BlockSpec((UNITS, rows, WIDTH), lambda i, s: (0, 0, 0)),
                pl.BlockSpec((VEC_ROWS, 128), lambda i, s: (0, 0)),
            ],
        ),
        out_shape=[
            jax.ShapeDtypeStruct((UNITS, rows, WIDTH), BF),
            jax.ShapeDtypeStruct((VEC_ROWS, 128), F32),
        ],
        name="pick_layer",
    )(layer.reshape(1), *vectors, *matrices)


def vector_parts(shards):
    base = WIDTH // shards
    parts = {}
    for r, size in enumerate(VEC_SIZES):
        for j in range(4 if size == 4 else 1):
            width = base * (1 if size == 4 else size)
            parts.setdefault(width, []).append((r, base * j, WIDTH * j))
    return parts


def page_maps(shards, width):
    total = shards * width
    col = lax.broadcasted_iota(jnp.int32, (128, total), 1).astype(F32)
    place = lax.broadcasted_iota(jnp.int32, (128, total), 0).astype(F32)
    one_hot = (col - jnp.floor((col + 0.5) * (1 / width)) * width) == place
    col_s = lax.broadcasted_iota(jnp.int32, (shards, total), 1)
    first = lax.broadcasted_iota(jnp.int32, (shards, total), 0) * width
    return one_hot, (col_s >= first) & (col_s < first + width)


def pages_to_rows(pages, fvec, shards):
    for width, parts in vector_parts(shards).items():
        one_hot, mine = page_maps(shards, width)
        one_hot = one_hot.astype(BF)
        for r, lane, start in parts:
            page = pages[:, r, :]
            if lane:
                page = pltpu.roll(page, 128 - lane, 1)
            spread = mm(page.astype(BF), one_hot)
            fvec[r : r + 1, start : start + shards * width] = jnp.sum(
                jnp.where(mine, spread, 0.0), axis=0, keepdims=True
            )


def rows_to_pages(svec, pages, shards):
    for width, parts in vector_parts(shards).items():
        one_hot, mine = page_maps(shards, width)
        one_hot = one_hot.astype(BF)
        for r, lane, start in parts:
            spread = jnp.where(mine, svec[r : r + 1, start : start + shards * width], 0.0)
            high = spread.astype(BF)
            low = (spread - high.astype(F32)).astype(BF)
            page = dg(high, one_hot, 1, 1) + dg(low, one_hot, 1, 1)
            if lane:
                pages[:, r, :] = pages[:, r, :] + pltpu.roll(page, lane, 1)
            else:
                pages[:, r, :] = page


def norm_stats(values):
    mean = jnp.mean(values, axis=-1, keepdims=True)
    centred = values - mean
    spread = jnp.mean(centred * centred, axis=-1, keepdims=True)
    scale = lax.rsqrt(spread + EPSILON)
    return centred * scale, scale


def norm_back(grad, gain, normed, scale):
    scaled = grad * gain
    mean_one = jnp.mean(scaled, axis=-1, keepdims=True)
    mean_two = jnp.mean(scaled * normed, axis=-1, keepdims=True)
    return scale * (scaled - mean_one - normed * mean_two)


def key_ranges(length):
    reach = length // 2
    return [(max(0, i * QB - reach), (i + 1) * QB) for i in range(length // QB)]


def build_masks(doc_ref, causal, features):
    for by_key in range(2):
        q_pos = lax.broadcasted_iota(jnp.int32, (QB, QB), by_key)
        k_pos = lax.broadcasted_iota(jnp.int32, (QB, QB), 1 - by_key)
        causal[by_key] = jnp.where(k_pos <= q_pos, 0.0, NEG_LARGE)
    length = doc_ref.shape[1]
    own = jnp.transpose(jnp.broadcast_to(doc_ref[...].astype(F32), (128, length)))
    lane = lax.broadcasted_iota(jnp.int32, (length, 128), 1)
    lane = jnp.where(lane >= HEAD, lane - HEAD, lane).astype(F32)
    same = own == lane
    features[0] = jnp.where(same | (lane >= DOCS), 0.0, NEG_LARGE).astype(BF)
    features[1] = jnp.where(same, 1.0, 0.0).astype(BF)


def head_lanes(values, head, other):
    lane = lax.broadcasted_iota(jnp.int32, values.shape, 1)
    keep = lane >= HEAD if head else lane < HEAD
    return jnp.where(keep, values, other)


def alone(values, head, fill=0.0):
    return head_lanes(values, head, jnp.full(values.shape, fill, values.dtype))


def pair_lanes(unit, half):
    start = [unit * WIDTH + HALF * half + 128 * part for part in range(3)]
    return [pl.ds(pl.multiple_of(s, 128), 128) for s in start]


def forward_pair(unit, half, qkv, mixed, lse, causal, features):
    length = qkv.shape[0]
    lanes_q, lanes_k, lanes_v = pair_lanes(unit, half)
    ranges = key_ranges(length)
    keys = [head_lanes(qkv[:, lanes_k], h, features[1]) for h in range(2)]
    pair = 2 * unit + half
    lanes_o = pl.ds(pl.multiple_of(pair * 128, 128), 128)
    steps = [(i, h) for i in range(len(ranges)) for h in range(2)]

    def scores(step):
        i, h = step
        lo, hi = ranges[i]
        rows = slice(i * QB, (i + 1) * QB)
        raw = dg(head_lanes(qkv[rows, lanes_q], h, features[0, rows]), keys[h][lo:hi], 1, 1)
        last = raw[:, hi - lo - QB :] + causal[0]
        return jnp.concatenate([raw[:, : hi - lo - QB], last], 1) if hi - lo > QB else last

    def finish(step, score):
        i, h = step
        lo, hi = ranges[i]
        top = jnp.max(score, axis=1, keepdims=True)
        soft = jnp.exp(score - top).astype(BF)
        return mm(soft, alone(qkv[lo:hi, lanes_v], h, 1.0)), top

    current, done = scores(steps[0]), {}
    for n, step in enumerate(steps):
        following = scores(steps[n + 1]) if n + 1 < len(steps) else None
        done[step] = finish(step, current)
        current = following
        i, h = step
        if h == 1:
            (acc0, top0), (acc1, top1) = done.pop((i, 0)), done.pop((i, 1))
            rows = slice(i * QB, (i + 1) * QB)
            first = lax.broadcasted_iota(jnp.int32, acc0.shape, 1) < HEAD
            total = pltpu.roll(jnp.where(first, acc1, acc0), HEAD, 1)
            mixed[rows, lanes_o] = (jnp.where(first, acc0, acc1) / total).astype(BF)
            logs = jnp.transpose(jnp.where(first, top0, top1) + jnp.log(total))
            lse[pair, 0:1, rows] = logs[0:1]
            lse[pair, 1:2, rows] = logs[HEAD : HEAD + 1]


def backward_pair(unit, half, qkv, mixed, mixed_grad, lse, causal, features, key_acc, value_acc):
    length = qkv.shape[0]
    lanes_q, lanes_k, lanes_v = pair_lanes(unit, half)
    ranges = key_ranges(length)
    keys = [head_lanes(qkv[:, lanes_k], h, features[1]) for h in range(2)]
    pair = 2 * unit + half
    lanes_o = pl.ds(pl.multiple_of(pair * 128, 128), 128)
    keys_t = jnp.transpose(qkv[:, lanes_k])
    steps = [(i, h) for i in range(len(ranges)) for h in range(2)]
    products = {}

    def start(step):
        i, h = step
        lo, hi = ranges[i]
        rows = slice(i * QB, (i + 1) * QB)
        query = alone(qkv[rows, lanes_q], h)
        grad = alone(mixed_grad[rows, lanes_o], h)
        raw = dg(keys[h][lo:hi], head_lanes(qkv[rows, lanes_q], h, features[0, rows]), 1, 1)
        last = raw[hi - lo - QB :] + causal[1]
        score = jnp.concatenate([raw[: hi - lo - QB], last], 0) if hi - lo > QB else last
        return score, dg(qkv[lo:hi, lanes_v], grad, 1, 1), query, grad

    def finish(step, started):
        i, h = step
        lo, hi = ranges[i]
        rows = slice(i * QB, (i + 1) * QB)
        score, soft_grad, query, grad = started
        if h == 0:
            products[i] = jnp.transpose(
                mixed_grad[rows, lanes_o].astype(F32) * mixed[rows, lanes_o].astype(F32)
            )
        soft = jnp.exp(score - lse[pair, h : h + 1, rows])
        centre = jnp.sum(products[i][HEAD * h : HEAD * h + HEAD], axis=0, keepdims=True)
        score_grad = (soft * (soft_grad - centre)).astype(BF)
        soft = soft.astype(BF)
        return (
            mm(keys_t[HEAD * h : HEAD * h + HEAD, lo:hi], score_grad),
            mm(score_grad, query),
            mm(soft, grad),
        )

    current, done = start(steps[0]), {}
    for n, step in enumerate(steps):
        following = start(steps[n + 1]) if n + 1 < len(steps) else None
        done[step] = finish(step, current)
        current = following
        i, h = step
        if h == 1:
            (q0, k0, v0), (q1, k1, v1) = done.pop((i, 0)), done.pop((i, 1))
            rows = slice(i * QB, (i + 1) * QB)
            lo, hi = ranges[i]
            query_grad = jnp.transpose(jnp.concatenate([q0, q1], 0))
            qkv[rows, lanes_q] = (query_grad * HEAD**-0.5).astype(BF)
            key_part, value_part, old = k0 + k1, v0 + v1, hi - QB - lo
            if old:
                key_acc[lo : lo + old] += key_part[:old]
                value_acc[lo : lo + old] += value_part[:old]
            key_acc[hi - QB : hi] = key_part[old:]
            value_acc[hi - QB : hi] = value_part[old:]
    qkv[:, lanes_k] = key_acc[...].astype(BF)
    qkv[:, lanes_v] = value_acc[...].astype(BF)


def turned(unit):
    return isinstance(unit, int) and unit in TURNED


class Exchange:
    def __init__(self, mesh_shape, weights, shards, refs):
        self.depth = mesh_shape["fsdp"] // 2
        self.weights, self.shards = weights, shards
        self.__dict__.update(refs)
        dp, fsdp = lax.axis_index("dp"), lax.axis_index("fsdp")
        self.y, self.c = dp // 2, dp % 2
        self.z, self.x = fsdp // 2, fsdp % 2
        self.flips = [(b // 4, b // 2 % 2, b % 2) for b in range(1, 8)]

    def device(self, y=None, c=None, z=None, x=None):
        y, c = self.y if y is None else y, self.c if c is None else c
        z, x = self.z if z is None else z, self.x if x is None else x
        return (y * 2 + c, z * 2 + x)

    def far(self, d):
        return lax.rem(self.z + d, self.depth)

    def flipped(self, flip):
        own = (self.y, self.c, self.x)
        return [1 - a if f else a for a, f in zip(own, flip, strict=True)]

    def barrier(self):
        barrier = pltpu.get_barrier_semaphore()
        peers = [self.device(z=self.far(d)) for d in range(1, self.depth)]
        for flip in self.flips:
            y, c, x = self.flipped(flip)
            peers.append(self.device(y=y, c=c, x=x))
        for peer in peers:
            pl.semaphore_signal(barrier, inc=1, device_id=peer, device_id_type=MESH)
        pl.semaphore_wait(barrier, len(peers))

    def at(self, unit, y, c, z, x, lanes=slice(None)):
        return self.weights.at[unit, y, c, z, x, :, lanes]

    def remote(self, src, dst, sems, slot, device):
        return pltpu.make_async_remote_copy(
            src_ref=src,
            dst_ref=dst,
            send_sem=sems[0].at[slot],
            recv_sem=sems[1].at[slot],
            device_id=device,
            device_id_type=MESH,
        )

    def gather_copies(self, unit, step):
        y, c, z, x = self.y, self.c, self.z, self.x
        low, high, every = slice(0, HALF), slice(HALF, WIDTH), slice(None)
        to_x, to_y, to_c = self.device(x=1 - x), self.device(y=1 - y), self.device(c=1 - c)
        if turned(unit) and step < 4:
            moves = self.turned_moves(unit, step)
        elif step == 1:
            place = self.at(unit, y, c, z, x)
            moves = [(self.shards.at[unit], place, self.device(z=self.far(d))) for d in range(1, self.depth)]
        elif step == 2:
            one, two = [self.at(unit, y, c, every, x, lanes) for lanes in (low, high)]
            moves = [(one, one, to_x), (two, two, to_y)]
        elif step == 3:
            one = self.at(unit, y, c, every, every, low)
            two = self.at(unit, every, c, every, x, high)
            moves = [(one, one, to_y), (two, two, to_x)]
        else:
            core = self.at(unit, every, c, every, every)
            moves = [(core, core, to_c)]
        return [self.remote(src, dst, self.gather_sems, 4 * unit + step - 1, to) for src, dst, to in moves]

    def turned_moves(self, unit, step):
        y, c, z, x = self.y, self.c, self.z, self.x
        low, high, every = slice(0, HALF), slice(HALF, WIDTH), slice(None)
        to_x, to_y = self.device(x=1 - x), self.device(y=1 - y)
        if step == 1:
            return [
                (self.shards.at[unit, :, lanes], self.at(unit, y, c, z, x, lanes), to)
                for lanes, to in ((low, to_x), (high, to_y))
            ]
        if step == 2:
            one, two = self.at(unit, y, c, z, every, low), self.at(unit, every, c, z, x, high)
            return [(one, one, to_y), (two, two, to_x)]
        plane = self.at(unit, every, c, z, every)
        return [(plane, plane, self.device(z=self.far(d))) for d in range(1, self.depth)]

    def gather_all(self, unit, step):
        y, c, z, x, every = self.y, self.c, self.z, self.x, slice(None)
        part = (
            self.at(unit, y, c, z, x),
            self.at(unit, y, c, z, every),
            self.at(unit, every, c, slice(0, self.depth - 1), every),
            self.at(unit, every, c, every, every),
        )[step - 1] if turned(unit) else (
            self.at(unit, y, c, slice(0, self.depth - 1), x),
            self.at(unit, y, c, every, x),
            self.at(unit, y, c, every, every),
            self.at(unit, every, c, every, every),
        )[step - 1]
        return self.remote(part, part, self.gather_sems, 4 * unit + step - 1, self.device(c=1 - c))

    def own_page(self, unit):
        place = self.at(unit, self.y, self.c, self.z, self.x)
        return pltpu.make_async_copy(self.shards.at[unit], place, self.local_sems.at[unit])

    def gather_step(self, unit, step):
        if step == 1:
            self.own_page(unit).start()
        if step == 2:
            self.own_page(unit).wait()
        if step > 1:
            self.gather_received(unit, step - 1)
        for copy in self.gather_copies(unit, step):
            copy.start()

    def gather_received(self, unit, step):
        self.gather_all(unit, step).wait_recv()

    def gather_sent(self, unit):
        if not isinstance(unit, int):
            normal = unit >= 0
            for other in TURNED:
                normal = normal & (unit != other)
                pl.when(unit == other)(functools.partial(self.all_sent, other))
            pl.when(normal)(functools.partial(self.all_sent, unit))
        else:
            self.all_sent(unit)

    def all_sent(self, unit):
        for step in range(1, 5):
            self.gather_all(unit, step).wait_send()

    def vector_copies(self, step):
        y, c, z, x = self.y, self.c, self.z, self.x
        pages, landing = self.vec_pages, self.vec_landing
        moves = []
        if step == 1:
            place = pages.at[y, c, z, x]
            moves = [(self.vec_shard, place, self.device(z=self.far(d))) for d in range(1, self.depth)]
        elif step in (2, 3):
            for k, flip in enumerate(self.flips):
                yy, cc, xx = self.flipped(flip)
                own = pages.at[y, c, :, x]
                pair = (own, own) if step == 2 else (pages.at[yy, cc, :, xx], landing.at[k])
                moves.append((*pair, self.device(y=yy, c=cc, x=xx)))
        else:
            for d in range(1, self.depth):
                zz = self.far(d)
                moves.append((pages.at[y, c, zz, x], landing.at[7, d], self.device(z=zz)))
        return [self.remote(src, dst, self.vec_sems, step, to) for src, dst, to in moves]

    def vector_all(self, step):
        if step in (1, 4):
            part = self.vec_landing.at[7, 0 : self.depth - 1]
        else:
            part = self.vec_landing.at[0:7]
        return self.remote(part, part, self.vec_sems, step, self.device(c=1 - self.c))

    def vector_step(self, step):
        y, c, z, x = self.y, self.c, self.z, self.x
        pages, landing = self.vec_pages, self.vec_landing
        own = pltpu.make_async_copy(self.vec_shard, pages.at[y, c, z, x], self.local_sems.at[UNITS])
        if step == 1:
            own.start()
        elif step == 2:
            own.wait()
        if step in (2, 4, 5):
            self.vector_all(step - 1).wait_recv()
        if step == 4:
            for k in range(self.depth):
                total = pages[y, c, k, x]
                for j in range(7):
                    total = total + landing[j, k]
                pages[y, c, k, x] = total
        if step == 5:
            total = pages[y, c, z, x]
            for d in range(1, self.depth):
                total = total + landing[7, d]
            self.vec_sum[...] = total
            return
        for copy in self.vector_copies(step):
            copy.start()

    def vectors_sent(self, *steps):
        for step in steps:
            self.vector_all(step).wait_send()

    def add(self, place, other):
        place[...] = place[...] + other[...]

    def sum_copies(self, unit, slot, step):
        y, c, z, x = self.y, self.c, self.z, self.x
        low, high, every = slice(0, HALF), slice(HALF, WIDTH), slice(None)
        to_x, to_y, to_c = self.device(x=1 - x), self.device(y=1 - y), self.device(c=1 - c)
        if step == 1:
            moves = [(self.at(slot, every, 1 - c, every, every), self.from_core.at[unit], to_c)]
        elif step == 2:
            two = self.from_two
            moves = [(self.at(slot, 1 - y, c, every, every, low), two.at[unit, 0], to_y)]
            for k in range(2):
                moves.append((self.at(slot, k, c, every, 1 - x, high), two.at[unit, 1, :, k], to_x))
        elif step == 3:
            three = self.from_three
            moves = [
                (self.at(slot, y, c, every, 1 - x, low), three.at[unit, 0], to_x),
                (self.at(slot, 1 - y, c, every, x, high), three.at[unit, 1], to_y),
            ]
        else:
            moves = []
            for d in range(1, self.depth):
                zz = self.far(d)
                moves.append((self.at(slot, y, c, zz, x), self.from_four.at[unit, d - 1], self.device(z=zz)))
        return [self.remote(src, dst, self.sum_sems, 4 * unit + step - 1, to) for src, dst, to in moves]

    def sum_all(self, unit, slot, step):
        y, c, z, x, every = self.y, self.c, self.z, self.x, slice(None)
        src, dst = (
            (self.at(slot, every, c, every, every), self.from_core.at[unit]),
            (self.at(slot, y, c, every, every), self.from_two.at[unit]),
            (self.at(slot, y, c, every, x), self.from_three.at[unit]),
            (self.at(slot, y, c, slice(0, self.depth - 1), x), self.from_four.at[unit]),
        )[step - 1]
        return self.remote(src, dst, self.sum_sems, 4 * unit + step - 1, self.device(c=1 - c))

    def sum_sent(self, unit, slot):
        for step in range(1, 5):
            self.sum_all(unit, slot, step).wait_send()

    def sum_step(self, unit, slot, step):
        y, c, z, x = self.y, self.c, self.z, self.x
        low, high = slice(0, HALF), slice(HALF, WIDTH)
        if step > 1:
            self.sum_all(unit, slot, step - 1).wait_recv()
        def add_one(k, carry):
            if step == 2:
                for j in range(2):
                    for i in range(2):
                        self.add(self.at(slot, j, c, k, i), self.from_core.at[unit, j, k, i])
            elif step == 3:
                for j in range(2):
                    self.add(self.at(slot, y, c, k, j, low), self.from_two.at[unit, 0, k, j])
                    self.add(self.at(slot, j, c, k, x, high), self.from_two.at[unit, 1, k, j])
            else:
                self.add(self.at(slot, y, c, k, x, low), self.from_three.at[unit, 0, k])
                self.add(self.at(slot, y, c, k, x, high), self.from_three.at[unit, 1, k])
            return carry

        if step > 1:
            lax.fori_loop(0, self.depth, add_one, 0)
        for copy in self.sum_copies(unit, slot, step):
            copy.start()

    def half_copies(self, half, slot, step):
        y, c, z, x, every = self.y, self.c, self.z, self.x, slice(None)
        to_x, to_y, to_c = self.device(x=1 - x), self.device(y=1 - y), self.device(c=1 - c)
        lanes = pl.ds(pl.multiple_of(HALF * half, 128), HALF) if not isinstance(half, int) else pl.ds(HALF * half, HALF)
        middle = self.depth // 2
        near, far = slice(0, middle), slice(middle, self.depth)
        own = pl.ds(middle * half, middle)
        two, three, four = [a.at[LAST] for a in (self.from_two, self.from_three, self.from_four)]
        if step == 1:
            core = self.from_core.at[LAST, :, :, :, :, lanes]
            moves = [(self.at(slot, every, 1 - c, every, every, lanes), core, to_c)]
        elif step == 2:
            moves = [
                (self.at(slot, 1 - y, c, near, every, lanes), two.at[0, own], to_y),
                (self.at(slot, every, c, far, 1 - x, lanes), two.at[1, own], to_x),
            ]
        elif step == 3:
            moves = [
                (self.at(slot, y, c, near, 1 - x, lanes), three.at[0, own], to_x),
                (self.at(slot, 1 - y, c, far, x, lanes), three.at[1, own], to_y),
            ]
        else:
            moves = []
            for d in range(1, self.depth):
                zz = self.far(d)
                moves.append((self.at(slot, y, c, zz, x, lanes), four.at[d - 1, :, lanes], self.device(z=zz)))
        index = 4 * (LAST + (LAST_HALF - LAST) * half) + step - 1
        copies = [self.remote(src, dst, self.sum_sems, index, to) for src, dst, to in moves]
        src, dst = (
            (self.at(slot, every, c, every, every, lanes), self.from_core.at[LAST, :, :, :, :, lanes]),
            (self.at(slot, y, c, every, every, lanes), two.at[:, own]),
            (self.at(slot, y, c, every, x, lanes), three.at[:, own]),
            (self.at(slot, y, c, slice(0, self.depth - 1), x, lanes), four.at[:, :, lanes]),
        )[step - 1]
        return copies, self.remote(src, dst, self.sum_sems, index, to_c)

    def half_sent(self, half, slot):
        for step in range(1, 5):
            self.half_copies(half, slot, step)[1].wait_send()

    def half_step(self, half, slot, step):
        y, c, x = self.y, self.c, self.x
        middle = self.depth // 2
        if step > 1:
            self.half_copies(half, slot, step - 1)[1].wait_recv()
            lanes = slice(HALF * half, HALF * half + HALF)
        if step == 2:

            def add_one(k, carry):
                for j in range(2):
                    for i in range(2):
                        self.add(self.at(slot, j, c, k, i, lanes), self.from_core.at[LAST, j, k, i, :, lanes])
                return carry

            lax.fori_loop(0, self.depth, add_one, 0)
        elif step == 3:
            for k in range(middle):
                for j in range(2):
                    low, high = self.at(slot, y, c, k, j, lanes), self.at(slot, j, c, middle + k, x, lanes)
                    self.add(low, self.from_two.at[LAST, 0, middle * half + k, j])
                    self.add(high, self.from_two.at[LAST, 1, middle * half + j, k])
        elif step == 4:
            for k in range(middle):
                low, high = self.at(slot, y, c, k, x, lanes), self.at(slot, y, c, middle + k, x, lanes)
                self.add(low, self.from_three.at[LAST, 0, middle * half + k])
                self.add(high, self.from_three.at[LAST, 1, middle * half + k])
        for copy in self.half_copies(half, slot, step)[0]:
            copy.start()

    def half_summed(self, half, slot):
        self.half_copies(half, slot, 4)[1].wait_recv()
        lanes = slice(HALF * half, HALF * half + HALF)
        total = self.at(slot, self.y, self.c, self.z, self.x, lanes)[...].astype(F32)
        for d in range(self.depth - 1):
            total += self.from_four[LAST, d, :, lanes].astype(F32)
        return total

    def summed(self, unit, slot):
        self.sum_all(unit, slot, 4).wait_recv()
        total = self.at(slot, self.y, self.c, self.z, self.x)[...].astype(F32)
        for d in range(self.depth - 1):
            total += self.from_four[unit, d].astype(F32)
        return total


def block_kernel(mesh_shape, exchanged, *refs):
    refs = list(refs)
    take = lambda n: [refs.pop(0) for _ in range(n)]
    tokens, cotangent, documents = take(3)
    if exchanged:
        shards, vec_shard = take(2)
    else:
        weights_in, vectors_in = take(2)
    result, input_grad, hidden_kept, down_kept = take(4)
    if exchanged:
        qkv_sum, out_sum, up_sum, down_sum, vec_sum = take(5)
    else:
        weights_out, vectors_out = take(2)
    (weights, cot, normed_one, qkv, mixed, lse, causal, features, residual, normed_two) = take(10)
    (acc_one, acc_two, low_one, low_two, fvec, svec, io_sems) = take(7)
    x_in = low_two
    key_acc, value_acc = residual.at[:, 0:128], residual.at[:, 128:256]
    length = x_in.shape[0]
    tiles = length // QB

    ex = None
    if exchanged:
        names = ("vec_pages", "vec_landing", "from_core", "from_two", "from_three", "from_four")
        extra = dict(zip(names, take(len(names))))
        gs, gr, ss, sr, vs, vr, local = take(7)
        extra.update(gather_sems=(gs, gr), sum_sems=(ss, sr), vec_sems=(vs, vr), local_sems=local)
        extra.update(vec_shard=vec_shard, vec_sum=vec_sum)
        ex = Exchange(mesh_shape, weights, shards, extra)

    def matrix(unit, start=0, width=WIDTH):
        lanes = pl.ds(start, width)
        if exchanged:
            return weights[unit, :, :, :, :, :, lanes].reshape(WIDTH, width)
        return weights[unit, :, lanes]

    def matrix_rows(unit, half):
        if exchanged:
            return weights[unit, half].reshape(HALF, WIDTH)
        return weights[unit, pl.ds(pl.multiple_of(HALF * half, HALF), HALF)]

    def gradient(unit, left, right, lanes=pl.ds(0, WIDTH)):
        def step(half, carry):
            rows = pl.ds(pl.multiple_of(HALF * half, 128), HALF)
            values = dg(left[:, rows], right(), 0, 0).astype(BF)
            if exchanged:
                shape = (*weights.shape[2:6], lanes.size)
                weights[unit, half, :, :, :, :, lanes] = values.reshape(shape)
            else:
                weights[unit, rows, lanes] = values
            return carry

        lax.fori_loop(0, 2, step, 0)

    def tile_loop(body, size=QB):
        def step(i, carry):
            body(pl.ds(pl.multiple_of(i * size, size), size))
            return carry

        lax.fori_loop(0, length // size, step, 0)

    def fv(row, size=1):
        return fvec[row : row + 1, 0 : WIDTH * size]

    def tokens_sum(values):
        return jnp.sum(values.astype(F32), axis=0, keepdims=True)

    def copy(slot):
        src, dst = ((tokens, x_in), (cotangent, cot), (low_one, result), (normed_one, input_grad))[slot]
        return pltpu.make_async_copy(src, dst, io_sems.at[slot])

    hidden_homes = (normed_two, cot, low_one, mixed)

    def keep_hidden(chunk):
        return pltpu.make_async_copy(low_one, hidden_kept.at[chunk], io_sems.at[5])

    def keep_down(chunk):
        return pltpu.make_async_copy(weights.at[down(chunk)], down_kept.at[chunk], io_sems.at[6])

    def fetch_hidden(chunk):
        return pltpu.make_async_copy(hidden_kept.at[chunk], hidden_homes[chunk], io_sems.at[8 + chunk])

    def fetch_down(chunk):
        return pltpu.make_async_copy(down_kept.at[chunk], weights.at[down(chunk)], io_sems.at[12 + chunk])

    def place(name, turn=0):
        for index, steps in SCHEDULE.get(name, {}).items() if exchanged else ():

            def run(steps=steps):
                for of_sum, unit, step in steps:
                    if of_sum:
                        add_up(unit, step)
                    else:
                        ex.gather_step(unit, step)

            if isinstance(turn, int):
                if turn == index:
                    run()
            else:
                pl.when(turn == index)(run)

    def begin(unit, slot=None):
        if exchanged:
            ex.sum_step(unit, unit if slot is None else slot, 1)

    def arrived(unit):
        if exchanged:
            ex.gather_received(unit, 4)

    def add_up(unit, step):
        if unit in (LAST, LAST_HALF):
            half = int(unit == LAST_HALF)
            if step < 5:
                ex.half_step(half, up(LAST), step)
                return
            total = ex.half_summed(half, up(LAST))
            for part in range(3):
                start = WIDTH * part + 256 * LAST + 128 * half
                qkv_sum[:, start : start + 128] = total[:, 128 * part : 128 * part + 128]
            return
        slot = up(unit) if unit < OUT else unit
        if step < 5:
            ex.sum_step(unit, slot, step)
            return
        total = ex.summed(unit, slot)
        rows = total.shape[0]
        chunk, kind = (unit - up(0)) // 2, (unit - up(0)) % 2
        if unit < OUT:
            for part in range(3):
                for half in range(2):
                    start, own = WIDTH * part + 256 * unit + 128 * half, HALF * half + 128 * part
                    qkv_sum[:, start : start + 128] = total[:, own : own + 128]
        elif unit == OUT:
            out_sum[...] = total
        elif kind == 0:
            up_sum[chunk] = total
        else:
            down_sum[rows * chunk : rows * chunk + rows] = total

    copy(0).start()
    copy(1).start()
    svec[...] = jnp.zeros(svec.shape, F32)
    if exchanged:
        ex.barrier()
        ex.gather_step(0, 1)
        ex.vector_step(1)
        early = (1, 2, 3, *TURNED)
        for unit in early:
            ex.gather_step(unit, 1)
        build_masks(documents, causal, features)
        place("masks")
        ex.vector_step(2)
        place("vec")
        for unit in range(1, UNITS):
            if unit not in early:
                ex.gather_step(unit, 1)
        ex.vector_all(2).wait_recv()
        ex.vectors_sent(1, 2)
        pages_to_rows(ex.vec_pages.reshape(32, VEC_ROWS, 128), fvec, 32)
        place("rows")
    else:
        weights_copy = pltpu.make_async_copy(weights_in, weights, io_sems.at[4])
        weights_copy.start()
        build_masks(documents, causal, features)
        fvec[...] = vectors_in[...]
    copy(0).wait()

    def norm_one(rows):
        normed, _ = norm_stats(x_in[rows].astype(F32))
        normed_one[rows] = (normed * fv(0) + fv(1)).astype(BF)

    tile_loop(norm_one)
    place("norm")
    if not exchanged:
        weights_copy.wait()

    def attention(unit, carry):
        place("att0", unit)
        arrived(unit)

        def project(rows):
            full = mm(normed_one[rows], matrix(unit))
            for half in range(2):
                lanes_q, lanes_k, lanes_v = pair_lanes(unit, half)
                start, first = HALF * half, 256 * unit + 128 * half
                bias = [fvec[2:3, pl.ds(pl.multiple_of(b + first, 128), 128)] for b in (0, WIDTH)]
                query = (full[:, start : start + 128] + bias[0]).astype(BF).astype(F32)
                qkv[rows, lanes_q] = (query * HEAD**-0.5).astype(BF)
                qkv[rows, lanes_k] = full[:, start + 128 : start + 256].astype(BF)
                qkv[rows, lanes_v] = (full[:, start + 256 : start + HALF] + bias[1]).astype(BF)

        tile_loop(project, length)
        place("att1", unit)

        def pair(half, carry):
            forward_pair(unit, half, qkv, mixed, lse, causal, features)
            place("att2", 2 * unit + half)
            return carry

        return lax.fori_loop(0, 2, pair, carry)

    lax.fori_loop(0, 3, attention, 0)

    place("attend")
    arrived(OUT)
    copy(1).wait()

    def attend(rows):
        total = x_in[rows].astype(F32) + (mm(mixed[rows], matrix(OUT)) + fv(3))
        residual[rows] = total
        normed, _ = norm_stats(total)
        normed_two[rows] = (normed * fv(4) + fv(5)).astype(BF)
        acc_one[rows] = total + fv(7)
        acc_two[rows] = jnp.zeros_like(total)

    tile_loop(attend, 2 * QB)
    place("attended")

    def feed_forward(chunk, carry):
        up_unit, down_unit = up(chunk), down(chunk)
        place("ff0", chunk)
        arrived(up_unit)
        arrived(down_unit)
        keep_down(chunk).start()

        def half_hidden(half, carry):
            lanes = pl.ds(pl.multiple_of(HALF * half, 128), HALF)
            wide = pl.ds(pl.multiple_of(WIDTH * chunk + HALF * half, 128), HALF)

            def hidden(start):
                rows = slice(start, start + QB)
                pre = mm(normed_two[rows], matrix(up_unit, lanes.start, HALF)) + fvec[6:7, wide]
                return pre, dg(cot[rows], matrix_rows(down_unit, half), 1, 1)

            def activate(start, pair):
                pre, grad = pair
                square = pre * pre
                bent = jnp.tanh(pre * (GELU_COEF + (GELU_COEF * GELU_CUBIC) * square))
                upper = 0.5 + 0.5 * bent
                value = pre * upper
                slope = upper + (value - value * upper) * (
                    2.0 * GELU_COEF + (6.0 * GELU_COEF * GELU_CUBIC) * square
                )
                rows = slice(start, start + QB)
                low_one[rows, lanes] = value.astype(BF)
                back = (grad * slope).astype(BF)
                low_two[rows, lanes] = back
                svec[6:7, wide] += tokens_sum(back)

            current = hidden(0)
            for i in range(tiles):
                following = hidden((i + 1) * QB) if i + 1 < tiles else None
                activate(i * QB, current)
                current = following
            place("ff1", 2 * chunk + half)
            return carry

        lax.fori_loop(0, 2, half_hidden, 0)
        keep_hidden(chunk).start()

        def outward(rows):
            acc_two[rows] += dg(low_two[rows], matrix(up_unit), 1, 1)

        tile_loop(outward, length)
        place("ff3", chunk)
        if exchanged:
            ex.gather_sent(down_unit)
        keep_down(chunk).wait()
        gradient(down_unit, low_one, lambda: cot[...])
        begin(down_unit)
        place("ff4", chunk)
        if exchanged:
            ex.gather_sent(up_unit)
        gradient(up_unit, normed_two, lambda: low_two[...])
        begin(up_unit)
        place("ff5", chunk)
        keep_hidden(chunk).wait()
        return carry

    lax.fori_loop(0, 4, feed_forward, 0)
    fetch_hidden(0).start()

    def back_two(rows):
        normed, scale = norm_stats(residual[rows])
        grad = acc_two[rows]
        grads = cot[rows].astype(F32)
        total = grads + norm_back(grad, fv(4), normed, scale)
        acc_two[rows] = total
        low = total.astype(BF)
        low_two[rows] = low
        for row, part in ((4, grad * normed), (5, grad), (7, grads), (3, low)):
            svec[row : row + 1, 0:WIDTH] += tokens_sum(part)

    def back_out(rows):
        low_one[rows] = dg(low_two[rows], matrix(OUT), 1, 1).astype(BF)

    tile_loop(back_two)
    place("back_two")
    tile_loop(back_out, 2 * QB)
    place("back_out")
    if exchanged:
        ex.gather_sent(OUT)
    gradient(OUT, mixed, lambda: low_two[...])
    begin(OUT)
    place("dWo")
    copy(0).start()
    fetch_hidden(1).start()

    def attention_back(unit, carry):
        def free(slot):
            if exchanged:
                ex.sum_sent(slot, slot)
            else:
                done = pltpu.make_async_copy(weights.at[slot], weights_out.at[slot], io_sems.at[4])
                done.start()
                done.wait()

        def pair(half, carry):
            backward_pair(unit, half, qkv, mixed, low_one, lse, causal, features, key_acc, value_acc)
            place("ab0", 2 * unit + half)

            @pl.when(unit == LAST)
            def _():
                pl.when(half == 0)(lambda: free(up(LAST)))
                own = pl.ds(pl.multiple_of(WIDTH * LAST + HALF * half, 128), HALF)
                lanes = pl.ds(pl.multiple_of(HALF * half, 128), HALF)
                gradient(up(LAST), normed_one, lambda: qkv[:, own], lanes)
                if exchanged:
                    ex.half_step(half, up(LAST), 1)

            return carry

        lax.fori_loop(0, 2, pair, 0)

        @pl.when(unit != LAST)
        def _():
            free(up(unit))
            all_three = pl.ds(pl.multiple_of(WIDTH * unit, WIDTH), WIDTH)
            gradient(up(unit), normed_one, lambda: qkv[:, all_three])
            begin(unit, up(unit))

        place("ab2", unit)
        for half in range(2):
            lanes_q, _, lanes_v = pair_lanes(unit, half)
            for row, lanes in ((0, lanes_q), (WIDTH, lanes_v)):
                bias = pl.ds(pl.multiple_of(row + 256 * unit + 128 * half, 128), 128)
                svec[2:3, bias] = tokens_sum(qkv[:, lanes])

        return carry

    def back_qkv(rows):
        total = dg(qkv[rows, 0:WIDTH], matrix(0), 1, 1)
        for unit in (1, 2):
            total += dg(qkv[rows, WIDTH * unit : WIDTH * unit + WIDTH], matrix(unit), 1, 1)
        residual[rows] = total
        place("da1", rows.start // (2 * QB))

    lax.fori_loop(0, 3, attention_back, 0)
    fetch_hidden(2).start()
    fetch_hidden(3).start()
    for chunk in range(4):
        if exchanged:
            ex.sum_sent(down(chunk), down(chunk))
        else:
            done = pltpu.make_async_copy(weights.at[down(chunk)], weights_out.at[down(chunk)], io_sems.at[4])
            done.start()
            done.wait()
        fetch_down(chunk).start()
    tile_loop(back_qkv, 2 * QB)
    copy(0).wait()

    def back_one(rows):
        normed, scale = norm_stats(x_in[rows].astype(F32))
        grad = residual[rows]
        normed_one[rows] = (acc_two[rows] + norm_back(grad, fv(0), normed, scale)).astype(BF)
        for row, part in ((0, grad * normed), (1, grad)):
            svec[row : row + 1, 0:WIDTH] += tokens_sum(part)

    tile_loop(back_one)
    copy(3).start()
    if exchanged:
        place("back_one")
        rows_to_pages(svec, ex.vec_pages.reshape(32, VEC_ROWS, 128), 32)
        ex.vector_step(3)
        place("r2p")
    for chunk in range(4):
        fetch_hidden(chunk).wait()
        fetch_down(chunk).wait()

    def sent_rows(rows):
        sem = io_sems.at[2 + 5 * (rows.start // (2 * QB))]
        return pltpu.make_async_copy(low_one.at[rows], result.at[rows], sem)

    def output(rows):
        total = acc_one[rows]
        for chunk, home in enumerate(hidden_homes):
            total += mm(home[rows], matrix(down(chunk)))
        low_one[rows] = total.astype(BF)
        place("y", rows.start // (2 * QB))
        if exchanged:
            pl.when(rows.start == 0)(lambda: ex.vector_step(4))
        sent_rows(rows).start()

    tile_loop(output, 2 * QB)
    if exchanged:
        place("drain")
        ex.vector_step(5)
        ex.vectors_sent(3, 4)
        for unit in range(3):
            ex.gather_sent(unit)
            if unit != LAST:
                ex.sum_sent(unit, up(unit))
        for half in range(2):
            ex.half_sent(half, up(LAST))
        for unit in (OUT, up(3)):
            ex.sum_sent(unit, unit)
    else:
        vectors_out[...] = svec[...]
        for src, dst in [(up(k), k) for k in range(3)] + [(OUT, OUT), (up(3), up(3))]:
            done = pltpu.make_async_copy(weights.at[src], weights_out.at[dst], io_sems.at[4])
            done.start()
            done.wait()
    for start in range(0, length, 2 * QB):
        sent_rows(pl.ds(start, 2 * QB)).wait()
    copy(3).wait()


def finish_kernel(*refs):
    page, outs = refs[6], refs[7:]
    outs[0][...] = refs[0][...].astype(F32)
    outs[1][...] = refs[1][...].astype(F32)

    @pl.when(pl.program_id(0) == 0)
    def _():
        for k in (2, 3, 5):
            outs[k][...] = refs[k][...]
        up, rows = refs[4], refs[4].shape[1]
        shards = WIDTH // rows
        groups = [
            jnp.concatenate([up[j, :, 4 * rows * g : 4 * rows * g + 4 * rows] for j in range(4)], 1)
            for g in range(shards // 4)
        ]
        stacked, one_hot = jnp.concatenate(groups, 0), regroup(rows, True).astype(BF)
        high = stacked.astype(BF)
        moved = mm(high, one_hot) + mm((stacked - high.astype(F32)).astype(BF), one_hot)
        for g in range(shards // 4):
            outs[4][:, HALF * g : HALF * g + HALF] = moved[rows * g : rows * g + rows]
        for r, dst in enumerate(outs[6:]):
            dst[...] = page[r, 0 : dst.shape[0]]


def finish(rows, sums, page, sizes):
    block = pl.BlockSpec((rows[0].shape[0] // 2, WIDTH), lambda i: (i, 0))
    whole = lambda shape: pl.BlockSpec(shape, lambda i: (0,) * len(shape))
    ins = [block, block] + [whole(a.shape) for a in (*sums, page)]
    qkv, out, up, down = [a.shape for a in sums]
    shapes = [qkv, out, (up[1], 4 * WIDTH), down] + [(n,) for n in sizes]
    outs = [block, block] + [whole(shape) for shape in shapes]
    shapes = [a.shape for a in rows] + shapes
    return pl.pallas_call(
        finish_kernel,
        grid=(2,),
        in_specs=ins,
        out_specs=outs,
        out_shape=[jax.ShapeDtypeStruct(shape, F32) for shape in shapes],
        name="finish",
    )(*rows, *sums, page)


def run_block(mesh_shape, exchanged, tokens, cotangent, documents, *weights):
    length, width = tokens.shape
    depth = mesh_shape["fsdp"] // 2
    vmem = pltpu.VMEM
    whole = pl.BlockSpec(memory_space=pltpu.VMEM)
    far = pl.BlockSpec(memory_space=pl.ANY)
    page = (2, 2, depth, 2, weights[0].shape[1], WIDTH) if exchanged else (WIDTH, WIDTH)
    rows = [jax.ShapeDtypeStruct((length, WIDTH), BF)] * 2
    rows += [jax.ShapeDtypeStruct((4, length, WIDTH), BF), jax.ShapeDtypeStruct((4, *page), BF)]
    if exchanged:
        shard = weights[0].shape[1]
        in_specs = [far, far, whole, far, far]
        out_shape = rows + [
            jax.ShapeDtypeStruct((shard, 3 * WIDTH), F32),
            jax.ShapeDtypeStruct((shard, WIDTH), F32),
            jax.ShapeDtypeStruct((4, shard, WIDTH), F32),
            jax.ShapeDtypeStruct((4 * shard, WIDTH), F32),
            jax.ShapeDtypeStruct((VEC_ROWS, 128), F32),
        ]
        out_specs = [far] * 4 + [whole] * 5
        places = (2, 2, depth, 2)
        held = [vmem((UNITS, *places, shard, WIDTH), BF)]
    else:
        in_specs = [far, far, whole, far, whole]
        out_shape = rows + [
            jax.ShapeDtypeStruct((UNITS, WIDTH, WIDTH), BF),
            jax.ShapeDtypeStruct((VEC_ROWS, 4 * WIDTH), F32),
        ]
        out_specs = [far] * 5 + [whole]
        held = [vmem((UNITS, WIDTH, WIDTH), BF)]
    low, full = vmem((length, WIDTH), BF), vmem((length, WIDTH), F32)
    scratch = held + [
        low,
        low,
        vmem((length, 3 * WIDTH), BF),
        low,
        vmem((6, 8, length), F32),
        vmem((2, QB, QB), F32),
        vmem((2, length, 128), BF),
        full,
        low,
        full,
        full,
        low,
        low,
        vmem((VEC_ROWS, 4 * WIDTH), F32),
        vmem((VEC_ROWS, 4 * WIDTH), F32),
        pltpu.SemaphoreType.DMA((16,)),
    ]
    if exchanged:
        dma = pltpu.SemaphoreType.DMA
        scratch += [
            vmem((2, 2, depth, 2, VEC_ROWS, 128), F32),
            vmem((8, depth, VEC_ROWS, 128), F32),
            vmem((UNITS, 2, depth, 2, shard, WIDTH), BF),
            vmem((UNITS, 2, depth, 2, shard, HALF), BF),
            vmem((UNITS, 2, depth, shard, HALF), BF),
            vmem((UNITS, depth - 1, shard, WIDTH), BF),
            dma((4 * UNITS,)),
            dma((4 * UNITS,)),
            dma((4 * UNITS + 4,)),
            dma((4 * UNITS + 4,)),
            dma((5,)),
            dma((5,)),
            dma((UNITS + 1,)),
        ]
    params = dict(vmem_limit_bytes=VMEM_BYTES)
    if exchanged:
        params.update(collective_id=0, has_side_effects=True)
    return pl.pallas_call(
        functools.partial(block_kernel, mesh_shape, exchanged),
        out_shape=out_shape,
        in_specs=in_specs,
        out_specs=out_specs,
        scratch_shapes=scratch,
        compiler_params=pltpu.CompilerParams(**params),
        name="block",
    )(tokens, cotangent, documents, *weights)


def local(mesh_shape, tokens, cotangent, document_ids, source_layer, *stacks):
    (attngain, attnshift, qkvmatrix, qvoffset, outmatrix, outoffset) = stacks[:6]
    (mlpgain, mlpshift, upmatrix, upoffset, downmatrix, downoffset) = stacks[6:]
    vectors = (attngain, attnshift, qvoffset, outoffset, mlpgain, mlpshift, upoffset, downoffset)
    matrices = (qkvmatrix, outmatrix, upmatrix, downmatrix)
    rows_seq, length, width = tokens.shape
    shard = qkvmatrix.shape[1]
    shards = WIDTH // shard
    x_rows, c_rows = tokens.reshape(length, width), cotangent.reshape(length, width)
    axes = ("dp", "fsdp")
    exchanged = mesh_shape["dp"] == 4 and mesh_shape["fsdp"] == 8 and shard % 8 == 0
    if exchanged:
        units, page = pack_layer(source_layer, vectors, matrices)
        result, input_grad, _, _, qkv, out, wide, tall, page = run_block(
            mesh_shape, True, x_rows, c_rows, document_ids, units, page
        )
        result, input_grad, qkv, out, wide, tall, *pieces = finish(
            (result, input_grad), (qkv, out, wide, tall), page, [shard * s for s in VEC_SIZES]
        )
    else:
        pick = lambda stack: lax.dynamic_index_in_dim(stack, source_layer, 0, keepdims=False)
        gather = lambda part: lax.all_gather(part, axes, axis=0, tiled=True)
        scatter = lambda part: lax.psum_scatter(part, axes, scatter_dimension=0, tiled=True)
        qkv, out, wide, tall = [gather(pick(m)) for m in matrices]
        thirds = qkv.reshape(WIDTH, 3, 3, 2, 128).transpose(2, 0, 3, 1, 4).reshape(3, WIDTH, WIDTH)
        ups, downs = wide.reshape(WIDTH, 4, WIDTH).transpose(1, 0, 2), tall.reshape(4, WIDTH, WIDTH)
        quarters = jnp.stack([ups, downs], 1).reshape(8, WIDTH, WIDTH)
        weights = jnp.concatenate([thirds, out[None], quarters], 0)
        rows = [gather(pick(v)).astype(F32) for v in vectors]
        table = jnp.stack([jnp.pad(r, (0, 4 * WIDTH - r.shape[0])) for r in rows])
        result, input_grad, _, _, weights, table = run_block(
            mesh_shape, False, x_rows, c_rows, document_ids, weights, table
        )
        weights = weights.astype(F32)
        qkv = weights[0:3].reshape(3, WIDTH, 2, 3, 128).transpose(1, 3, 0, 2, 4).reshape(WIDTH, -1)
        wide = weights[up(0) :: 2].transpose(1, 0, 2).reshape(WIDTH, -1)
        tall = weights[down(0) :: 2].reshape(4 * WIDTH, WIDTH)
        qkv, out, wide, tall = [scatter(m) for m in (qkv, weights[OUT], wide, tall)]
        pieces = [scatter(table[r, 0 : WIDTH * s]) for r, s in enumerate(VEC_SIZES)]
    gain, shift, qv, outb, mid_gain, mid_shift, upb, downb = pieces
    shape = tokens.shape
    result, input_grad = result.astype(F32), input_grad.astype(F32)
    return (
        result.reshape(shape),
        input_grad.reshape(shape),
        gain,
        shift,
        qkv,
        qv,
        out,
        outb,
        mid_gain,
        mid_shift,
        wide,
        upb,
        tall,
        downb,
    )


def solution(mesh):
    axes = ("dp", "fsdp")
    rows, vector, matrix = P(axes, None, None), P(None, axes), P(None, axes, None)
    return jax.shard_map(
        functools.partial(local, dict(mesh.shape)),
        mesh=mesh,
        in_specs=(
            rows,
            rows,
            P(axes, None),
            P(),
            vector,
            vector,
            matrix,
            vector,
            matrix,
            vector,
            vector,
            vector,
            matrix,
            vector,
            matrix,
            vector,
        ),
        out_specs=(
            rows,
            rows,
            P(axes),
            P(axes),
            P(axes, None),
            P(axes),
            P(axes, None),
            P(axes),
            P(axes),
            P(axes),
            P(axes, None),
            P(axes),
            P(axes, None),
            P(axes),
        ),
        check_vma=False,
    )
```
